32 devices in a mesh: wide: 8 (over y, x, core), narrow: 4 (over z).
Axes of the slice: x: 2, y: 2, z: 4, core: 2. Of those that a mesh axis runs over, the one named last changes fastest.
Arguments:
- images: bfloat16 [64, 7, 7, 2048], P(('wide', 'narrow')), may hold values from 0 to 4
- tile_maps: bfloat16 [576, 2, 2, 2048], P(('wide', 'narrow')), may hold values from 0 to 4
- map_sizes: int32 [64], P(('wide', 'narrow')), may hold values from 0 to 7, as said below
- w_reduce: bfloat16 [2, 2048, 512], replicated, may hold values from -0.125 to 0.125
- w_spatial: bfloat16 [2, 3, 3, 512, 512], replicated, may hold values from -0.09375 to 0.09375
- w_expand: bfloat16 [2, 512, 2048], replicated, may hold values from -0.25 to 0.25
- gain_mid: float32 [2, 2, 512], replicated, may hold values from 0.5 to 1.5
- bias_mid: float32 [2, 2, 512], replicated, may hold values from -4 to 4
- gain_out: float32 [2, 2048], replicated, may hold values from 0.5 to 1.5
- bias_out: float32 [2, 2048], replicated, may hold values from -4 to 4
- grad_images: bfloat16 [64, 7, 7, 2048], P(('wide', 'narrow')), may hold values from -6 to 6
- grad_tiles: bfloat16 [576, 2, 2, 2048], P(('wide', 'narrow')), may hold values from -6 to 6
Outputs:
- out_images: float32 [64, 7, 7, 2048], P(('wide', 'narrow'))
- out_tiles: float32 [576, 2, 2, 2048], P(('wide', 'narrow'))
- grad_in_images: float32 [64, 7, 7, 2048], P(('wide', 'narrow'))
- grad_in_tiles: float32 [576, 2, 2, 2048], P(('wide', 'narrow'))
- grad_w_reduce: float32 [2, 2048, 512], P(None, 'narrow')
- grad_w_spatial: float32 [2, 3, 3, 512, 512], P(None, None, None, 'narrow')
- grad_w_expand: float32 [2, 512, 2048], P(None, 'narrow')
- grad_gain_mid: float32 [2, 2, 512], replicated
- grad_bias_mid: float32 [2, 2, 512], replicated
- grad_gain_out: float32 [2, 2048], replicated
- grad_bias_out: float32 [2, 2048], replicated
The draws below stay inside these ranges and needn't reach their ends.
Inputs may be any that keep to these rules, and one draw needn't show every extreme that they name: 0 marks an empty image slot, whose 9 tiles are empty too; a live image's map is the top-left map_sizes[i] x map_sizes[i] cells of its slot, with map_sizes[i] one of 5, 6, 7. On each device (aligned blocks of 2 slots) the live images fill the first slots, at least half of them, and one device has every slot live.
All inputs are finite; a program needn't handle non-finite values.
Results may differ from the reference program's by a relative error of at most 0.019.
Values sent between devices are 32-bit elements; how exact they have to be, the bound alone decides.
No kernel may reach another device: no remote copies, remote signals or barrier semaphores. Data moves between devices by JAX's collectives and lax.ppermute only.
A program may use at most 192 MiB of HBM per device.

```python
import jax
import jax.numpy as jnp
from jax import lax

D_IN = 2048
D_MID = 512
IMG_DEV = 2
BLOCKS = 2
MAP = 7
TILE = 2
PIECES = 9
IMAGES = 64
TILES = 576


def draw_map_sizes(key, part):
    device_total = IMAGES // IMG_DEV
    key_count, key_full, key_kind = jax.random.split(key, 3)
    live_count = jax.random.randint(key_count, (device_total,), (IMG_DEV + 1) // 2, IMG_DEV + 1)
    full_device = jax.random.randint(key_full, (), 0, device_total)
    live_count = jnp.where(jnp.arange(device_total) == full_device, IMG_DEV, live_count)
    kind_code = jax.random.randint(key_kind, (device_total, IMG_DEV), 0, 4)
    side_length = 5 + (kind_code == 2).astype(jnp.int32) + 2 * (kind_code == 3).astype(jnp.int32)
    slot_live = jnp.arange(IMG_DEV)[None, :] < live_count[:, None]
    return jnp.where(slot_live, side_length, 0).reshape(IMAGES).astype(jnp.int32)


def rising_maps(key, rows, side):
    place = jnp.arange(rows).astype(jnp.float32) / max(rows - 1, 1)
    values = jax.random.uniform(key, (rows, side, side, D_IN), jnp.float32, 0.0, 1.0)
    factor = 1.0 + 2.0 * place
    return values * factor[:, None, None, None]


def draw_images(key, part):
    return rising_maps(jax.random.fold_in(key, 11), IMAGES, MAP).astype(jnp.bfloat16)


def draw_tile_maps(key, part):
    return rising_maps(jax.random.fold_in(key, 13), TILES, TILE).astype(jnp.bfloat16)


def levels(rng, dims, cuts, least, top_value):
    def one(dim, blocks):
        heights = jax.random.uniform(jax.random.fold_in(jax.random.fold_in(rng, 6), dim), (blocks,), jnp.float32, least / len(cuts), top_value / len(cuts))
        return jnp.repeat(jnp.exp(heights), dims[dim] // blocks).reshape((-1,) + (1,) * (len(dims) - dim - 1))

    factor_of = one(*cuts[0])
    for cut in cuts[1:]:
        factor_of = factor_of * one(*cut)
    return factor_of


def noise(rng, extent, scale, reach, pieces=(), dtype=jnp.bfloat16):
    factor_of = levels(rng, extent, pieces, -0.22, 0.18) if pieces else 1.0
    result = jax.random.normal(rng, extent, jnp.float32) * scale * factor_of
    return jnp.minimum(jnp.maximum(result, -reach), reach).astype(dtype)


def setup_inputs(seed: int = 0) -> dict:
    keys = jax.random.split(jax.random.key(seed), 13)
    return {
        "images": draw_images(jax.random.fold_in(keys[12], 71), 0),
        "tile_maps": draw_tile_maps(jax.random.fold_in(keys[12], 71), 0),
        "map_sizes": draw_map_sizes(jax.random.fold_in(keys[12], 71), 0),
        "w_reduce": noise(keys[3], (BLOCKS, D_IN, D_MID), D_IN ** -0.5, 0.125),
        "w_spatial": noise(keys[4], (BLOCKS, 3, 3, D_MID, D_MID), (9 * D_MID) ** -0.5, 0.09375),
        "w_expand": noise(keys[5], (BLOCKS, D_MID, D_IN), D_MID ** -0.5, 0.25),
        "gain_mid": jnp.clip(1.0 + 0.1 * jax.random.normal(keys[6], (BLOCKS, 2, D_MID), jnp.float32), 0.5, 1.5),
        "bias_mid": noise(keys[7], (BLOCKS, 2, D_MID), 0.3, 4.0, (), jnp.float32),
        "gain_out": jnp.clip(1.0 + 0.1 * jax.random.normal(keys[8], (BLOCKS, D_IN), jnp.float32), 0.5, 1.5),
        "bias_out": noise(keys[9], (BLOCKS, D_IN), 0.3, 4.0, (), jnp.float32),
        "grad_images": noise(keys[10], (IMAGES, MAP, MAP, D_IN), 1.0, 6.0, ((0, 32),)),
        "grad_tiles": noise(keys[11], (TILES, TILE, TILE, D_IN), 1.0, 6.0, ((0, 32),)),
    }


@jax.custom_vjp
def low(v):
    return lax.optimization_barrier(v.astype(jnp.bfloat16)).astype(jnp.float32)

@jax.custom_vjp
def low_back(v):
    return v

def low_keep(v):
    return (low(v), None)

def low_pass(kept, grad):
    return (grad,)

def back_keep(v):
    return (v, None)

def back_low(kept, grad):
    return (low(grad),)
low.defvjp(low_keep, low_pass)
low_back.defvjp(back_keep, back_low)
epsilon = 1e-05
highest = lax.Precision.HIGHEST

def make_masks(map_sizes):
    position = jnp.arange(MAP).astype(jnp.int32)
    sides = map_sizes.astype(jnp.int32)
    inside = (position[None, :, None] < sides[:, None, None]) & (position[None, None, :] < sides[:, None, None])
    image_mask = inside.astype(jnp.float32)[..., None]
    occupied = jnp.repeat((sides > 0).astype(jnp.float32), PIECES)
    tile_mask = jnp.broadcast_to(occupied[:, None, None, None], (occupied.shape[0], TILE, TILE, 1))
    return (image_mask, tile_mask)

def project(values, weight):
    return jnp.einsum('nhwc,cd->nhwd', values, weight, precision=highest)

def spatial(values, weight):
    return lax.conv_general_dilated(values, weight, (1, 1), 'SAME', dimension_numbers=('NHWC', 'HWIO', 'NHWC'), precision=highest)

def normalize(values, pixel_mask, total_count, scale_gain, shift_bias):
    average = lax.optimization_barrier(jnp.sum(values * pixel_mask, axis=(0, 1, 2))) / total_count
    centered = (values - average) * pixel_mask
    spread = lax.optimization_barrier(jnp.sum(centered * centered, axis=(0, 1, 2))) / total_count
    return (values - average) * lax.rsqrt(spread + epsilon) * scale_gain + shift_bias

def bottleneck(inputs, pixel_mask, total_count, weight_one, weight_two, weight_three, gains, biases, gain_last, bias_last):
    reduced = low_back(project(low(inputs), weight_one))
    hidden = jax.nn.silu(normalize(reduced, pixel_mask, total_count, gains[0], biases[0])) * pixel_mask
    spatial_out = low_back(spatial(low(hidden), weight_two))
    hidden = jax.nn.silu(normalize(spatial_out, pixel_mask, total_count, gains[1], biases[1])) * pixel_mask
    expanded = low_back(project(low(hidden), weight_three))
    return jax.nn.silu(normalize(expanded, pixel_mask, total_count, gain_last, bias_last) + inputs) * pixel_mask

def reference(images, tile_maps, map_sizes, w_reduce, w_spatial, w_expand, gain_mid, bias_mid, gain_out, bias_out, grad_images, grad_tiles):
    image_mask, tile_mask = make_masks(map_sizes)
    image_count = jnp.sum(image_mask)
    tile_count = jnp.sum(tile_mask)

    def forward(image_in, tile_in, weight_one, weight_two, weight_three, gains, biases, gains_last, biases_last):
        image_act, tile_act = (image_in, tile_in)
        for number in range(BLOCKS):
            image_act = bottleneck(image_act, image_mask, image_count, weight_one[number], weight_two[number], weight_three[number], gains[number], biases[number], gains_last[number], biases_last[number])
            tile_act = bottleneck(tile_act, tile_mask, tile_count, weight_one[number], weight_two[number], weight_three[number], gains[number], biases[number], gains_last[number], biases_last[number])
        return (image_act, tile_act)
    outputs, pullback = jax.vjp(forward, images.astype(jnp.float32), tile_maps.astype(jnp.float32), w_reduce.astype(jnp.float32), w_spatial.astype(jnp.float32), w_expand.astype(jnp.float32), gain_mid, bias_mid, gain_out, bias_out)
    gradients = pullback((grad_images.astype(jnp.float32), grad_tiles.astype(jnp.float32)))
    return (outputs[0], outputs[1], gradients[0], gradients[1], gradients[2], gradients[3], gradients[4], gradients[5], gradients[6], gradients[7], gradients[8])
```

```python
import functools

import jax
import jax.numpy as jnp
from jax import lax
from jax.experimental import pallas as pl
from jax.experimental.pallas import tpu as pltpu
from jax.sharding import PartitionSpec as P

BLOCKS = 2
MAP = 7
MAPW = 8
TILE = 2
PIECES = 9
SLOTS = 2
IMG_ROWS = MAP * MAPW * SLOTS
EPS = 1e-05
CH = 512
BF = jnp.bfloat16
F32 = jnp.float32
VMEM_LIMIT = 48 * 1024 * 1024
AXES = ("wide", "narrow")


class Grid:
    def __init__(self, wide, narrow):
        chips = wide // 2
        side = 1
        while side * side < chips:
            side *= 2
        self.y, self.x, self.c, self.z = chips // side, side, 2, narrow

    def index(self):
        wide = lax.axis_index("wide")
        core = wide % 2
        chip = wide // 2
        return chip // self.x, chip % self.x, core, lax.axis_index("narrow")

    def swap(self, value, dy=0, dx=0, dc=0, dz=0):
        pairs = []
        for y in range(self.y):
            for x in range(self.x):
                for c in range(self.c):
                    for z in range(self.z):
                        src = ((y * self.x + x) * 2 + c) * self.z + z
                        dst = (((y ^ dy) * self.x + (x ^ dx)) * 2 + (c ^ dc)) * self.z + (z ^ dz)
                        pairs.append((src, dst))
        return lax.ppermute(value, AXES, pairs)

    def phases(self):
        found = [[dict(dc=1)]]
        step = 1
        while step < max(self.x, self.y):
            group = []
            for dy in (0, step):
                for dx in (0, step):
                    if (dy or dx) and dy < self.y and dx < self.x:
                        group.append(dict(dy=dy, dx=dx))
            found.append(group)
            step *= 2
        found.append([dict(dz=k) for k in range(1, min(self.z, 4))])
        step = 4
        while step < self.z:
            found.append([dict(dz=step)])
            step *= 2
        return found


def merge_moments(members, counts):
    total = sum(counts)
    out = []
    for stream in range(2):
        whole = total[stream]
        plain = sum(m[2 * stream] for m in members)
        mean = plain / whole
        square = sum(m[2 * stream + 1] for m in members)
        for m, n in zip(members, counts):
            gap = m[2 * stream] / jnp.maximum(n[stream], 1.0) - mean
            square = square + n[stream] * gap * gap
        out += [plain, square]
    return jnp.stack(out), total


class Sync:
    def __init__(self, grid, local_counts):
        self.grid = grid
        self.local = local_counts
        self.levels = None

    def moments(self, stats):
        grid = self.grid
        first = self.levels is None
        value = stats
        count = self.local
        levels = [] if first else self.levels
        for number, group in enumerate(grid.phases()):
            if first:
                width = value.shape[1]
                packed = jnp.concatenate(
                    [value, jnp.broadcast_to(count[:, None], (2, width)), jnp.zeros((2, width), F32)]
                )
                got = [grid.swap(packed, **step) for step in group]
                counts = [count] + [g[4:6, 0] for g in got]
                got = [g[0:4] for g in got]
                levels.append(counts)
            else:
                got = [grid.swap(value, **step) for step in group]
                counts = levels[number]
            value, count = merge_moments([value] + got, counts)
        if first:
            self.levels = levels
            self.total = count
        out = []
        for stream in range(2):
            out.append(value[2 * stream] / self.total[stream])
            out.append(lax.rsqrt(value[2 * stream + 1] / self.total[stream] + EPS))
        return jnp.stack(out)

    def sums(self, value):
        for group in self.grid.phases():
            value = value + sum(self.grid.swap(value, **step) for step in group)
        return value

    def shares(self, sums):
        return sums / jnp.stack([self.total[0], self.total[0], self.total[1], self.total[1]])[:, None]


def parts(rows):
    return ((0, 0, IMG_ROWS), (1, IMG_ROWS, rows))


def sigmoid(v):
    return 0.5 * jnp.tanh(0.5 * v) + 0.5


def slope(v):
    s = sigmoid(v)
    return s * (1.0 + v * (1.0 - s))


def local_moments(value, mask, inv_ref, stats_ref):
    for stream, lo, hi in parts(value.shape[0]):
        v = value[lo:hi]
        m = mask[lo:hi]
        plain = jnp.sum(v * m, axis=0, keepdims=True)
        gap = (v - plain * inv_ref[stream]) * m
        stats_ref[2 * stream : 2 * stream + 1, :] = plain
        stats_ref[2 * stream + 1 : 2 * stream + 2, :] = jnp.sum(gap * gap, axis=0, keepdims=True)


def normed_of(value, mr_ref, stream):
    return (value - mr_ref[2 * stream : 2 * stream + 1, :]) * mr_ref[2 * stream + 1 : 2 * stream + 2, :]


def shifted(image_ref, tile_ref, dy, dx, tile_rows):
    start = 24 + 2 * MAPW * dy + 2 * dx
    image = image_ref[start : start + IMG_ROWS, :]
    start = 8 + TILE * dy + dx
    tile = tile_ref[start : start + tile_rows, :]
    if dy or dx:
        place = lax.broadcasted_iota(jnp.int32, (tile_rows, 1), 0)
        ty = (place // TILE) % TILE + dy
        tx = place % TILE + dx
        valid = (ty >= 0) & (ty < TILE) & (tx >= 0) & (tx < TILE)
        tile = jnp.where(valid, tile, 0.0)
    return image, tile


def fill_patches(value, image_ref, tile_ref, patch_ref, sign):
    rows = value.shape[0]
    tile_rows = rows - IMG_ROWS
    width = value.shape[1]
    image_ref[0:24, :] = jnp.zeros((24, width), F32)
    image_ref[24 + IMG_ROWS : 48 + IMG_ROWS, :] = jnp.zeros((24, width), F32)
    image_ref[24 : 24 + IMG_ROWS, :] = value[0:IMG_ROWS]
    tile_ref[0:8, :] = jnp.zeros((8, width), F32)
    tile_ref[8 + tile_rows : 16 + tile_rows, :] = jnp.zeros((8, width), F32)
    tile_ref[8 : 8 + tile_rows, :] = value[IMG_ROWS:]
    for tap in range(9):
        dy, dx = tap // 3 - 1, tap % 3 - 1
        image, tile = shifted(image_ref, tile_ref, sign * dy, sign * dx, tile_rows)
        patch_ref[tap, 0:IMG_ROWS, :] = image.astype(BF)
        patch_ref[tap, IMG_ROWS:rows, :] = tile.astype(BF)


def dot(a, b):
    return jnp.dot(a, b, preferred_element_type=F32)


def dot_nt(a, b):
    return lax.dot_general(a, b, (((1,), (1,)), ((), ())), preferred_element_type=F32)


def full(shape):
    zeros = (0,) * len(shape)
    return pl.BlockSpec(shape, lambda k: zeros)


def cols(rows):
    return pl.BlockSpec((rows, CH), lambda k: (0, k))


def smem():
    return pl.BlockSpec(memory_space=pltpu.SMEM)


def call(body, steps, in_specs, out_specs, out_shape, scratch=(), name=None, flops=0, transcendentals=0):
    return pl.pallas_call(
        body,
        grid=(steps,),
        in_specs=in_specs,
        out_specs=out_specs,
        out_shape=out_shape,
        scratch_shapes=list(scratch),
        compiler_params=pltpu.CompilerParams(
            vmem_limit_bytes=VMEM_LIMIT, dimension_semantics=("arbitrary",)
        ),
        cost_estimate=pl.CostEstimate(flops=flops, bytes_accessed=4_000_000, transcendentals=transcendentals),
        name=name,
    )


def sds(shape, dtype=F32):
    return jax.ShapeDtypeStruct(shape, dtype)


def reduce_first(x, w_reduce, mask, inv):
    rows, d_in = x.shape
    mid = w_reduce.shape[2]

    def body(inv_ref, x_ref, w_ref, mask_ref, red_ref, stats_ref):
        k = pl.program_id(0)
        part = dot(x_ref[...], w_ref[0])

        @pl.when(k == 0)
        def _():
            red_ref[...] = part

        @pl.when(k > 0)
        def _():
            red_ref[...] += part

        @pl.when(k == pl.num_programs(0) - 1)
        def _():
            local_moments(red_ref[...], mask_ref[...], inv_ref, stats_ref)

    return call(
        body,
        d_in // CH,
        [smem(), cols(rows), pl.BlockSpec((1, CH, mid), lambda k: (0, k, 0)), full((rows, 1))],
        [full((rows, mid)), full((4, mid))],
        [sds((rows, mid)), sds((4, mid))],
        name="reduce_first",
        flops=2 * rows * d_in * mid,
    )(inv, x, w_reduce, mask)


def spatial_stage(number, red, mr, gain, bias, mask, w9, inv):
    rows, mid = red.shape

    def body(inv_ref, red_ref, mr_ref, gain_ref, bias_ref, mask_ref, w_ref, hid_ref, out_ref, stats_ref, image, tile, patch):
        k = pl.program_id(0)

        @pl.when(k == 0)
        def _():
            pieces = []
            for stream, lo, hi in parts(rows):
                z = normed_of(red_ref[lo:hi, :], mr_ref, stream) * gain_ref[...] + bias_ref[...]
                pieces.append(z * sigmoid(z) * mask_ref[lo:hi, :])
            hidden = jnp.concatenate(pieces, axis=0)
            hid_ref[...] = hidden.astype(BF)
            fill_patches(hidden, image, tile, patch, 1)
            out_ref[...] = jnp.zeros((rows, mid), F32)

        total = out_ref[...]
        for j in range(3):
            total += dot(patch[3 * k + j], w_ref[0, j])
        out_ref[...] = total

        @pl.when(k == 2)
        def _():
            local_moments(out_ref[...], mask_ref[...], inv_ref, stats_ref)

    return call(
        body,
        3,
        [
            smem(),
            full((rows, mid)),
            full((4, mid)),
            full((1, mid)),
            full((1, mid)),
            full((rows, 1)),
            pl.BlockSpec((1, 3, mid, mid), lambda k: (number, k, 0, 0)),
        ],
        [full((rows, mid)), full((rows, mid)), full((4, mid))],
        [sds((rows, mid), BF), sds((rows, mid)), sds((4, mid))],
        [
            pltpu.VMEM((IMG_ROWS + 48, mid), F32),
            pltpu.VMEM((rows - IMG_ROWS + 16, mid), F32),
            pltpu.VMEM((9, rows, mid), BF),
        ],
        name="spatial_stage",
        flops=2 * rows * 9 * mid * mid,
    )(inv, red, mr, gain, bias, mask, w9)


def expand_stage(number, spa, mr, gain, bias, mask, w_expand, inv):
    rows, mid = spa.shape
    d_in = w_expand.shape[2]

    def body(inv_ref, spa_ref, mr_ref, gain_ref, bias_ref, mask_ref, w_ref, hid_ref, out_ref, stats_ref):
        @pl.when(pl.program_id(0) == 0)
        def _():
            for stream, lo, hi in parts(rows):
                z = normed_of(spa_ref[lo:hi, :], mr_ref, stream) * gain_ref[...] + bias_ref[...]
                hid_ref[lo:hi, :] = (z * sigmoid(z) * mask_ref[lo:hi, :]).astype(BF)

        value = dot(hid_ref[...], w_ref[0])
        out_ref[...] = value
        local_moments(value, mask_ref[...], inv_ref, stats_ref)

    return call(
        body,
        d_in // CH,
        [
            smem(),
            full((rows, mid)),
            full((4, mid)),
            full((1, mid)),
            full((1, mid)),
            full((rows, 1)),
            pl.BlockSpec((1, mid, CH), lambda k: (number, 0, k)),
        ],
        [full((rows, mid)), cols(rows), cols(4)],
        [sds((rows, mid), BF), sds((rows, d_in)), sds((4, d_in))],
        name="expand_stage",
        flops=2 * rows * d_in * mid,
    )(inv, spa, mr, gain, bias, mask, w_expand)


def join_stage(number, exp, mr, gain, bias, act, mask, w_reduce, inv):
    rows, d_in = exp.shape
    mid = w_reduce.shape[2]

    def body(inv_ref, exp_ref, mr_ref, gain_ref, bias_ref, act_ref, mask_ref, w_ref, out_ref, low_ref, red_ref, stats_ref):
        k = pl.program_id(0)
        for stream, lo, hi in parts(rows):
            z = (
                normed_of(exp_ref[lo:hi, :], mr_ref, stream) * gain_ref[...]
                + bias_ref[...]
                + act_ref[lo:hi, :].astype(F32)
            )
            out = z * sigmoid(z) * mask_ref[lo:hi, :]
            out_ref[lo:hi, :] = out
            low_ref[lo:hi, :] = out.astype(BF)
        part = dot(low_ref[...], w_ref[0])

        @pl.when(k == 0)
        def _():
            red_ref[...] = part

        @pl.when(k > 0)
        def _():
            red_ref[...] += part

        @pl.when(k == pl.num_programs(0) - 1)
        def _():
            local_moments(red_ref[...], mask_ref[...], inv_ref, stats_ref)

    return call(
        body,
        d_in // CH,
        [
            smem(),
            cols(rows),
            cols(4),
            cols(1),
            cols(1),
            cols(rows),
            full((rows, 1)),
            pl.BlockSpec((1, CH, mid), lambda k: (number, k, 0)),
        ],
        [cols(rows), cols(rows), full((rows, mid)), full((4, mid))],
        [sds((rows, d_in)), sds((rows, d_in), BF), sds((rows, mid)), sds((4, mid))],
        name="join_stage",
        flops=2 * rows * d_in * mid,
        transcendentals=rows * d_in,
    )(inv, exp, mr, gain, bias, act, mask, w_reduce)


def put_sums(stream, pre, normed, sums_ref):
    sums_ref[2 * stream : 2 * stream + 1, :] = jnp.sum(pre, axis=0, keepdims=True)
    sums_ref[2 * stream + 1 : 2 * stream + 2, :] = jnp.sum(pre * normed, axis=0, keepdims=True)


def turn_stage(exp, mr, gain, bias, act, mask, grad):
    rows, d_in = exp.shape

    def body(exp_ref, mr_ref, gain_ref, bias_ref, act_ref, mask_ref, grad_ref, out_ref, pre_ref, sums_ref):
        for stream, lo, hi in parts(rows):
            n = normed_of(exp_ref[lo:hi, :], mr_ref, stream)
            z = n * gain_ref[...] + bias_ref[...] + act_ref[lo:hi, :].astype(F32)
            s = sigmoid(z)
            m = mask_ref[lo:hi, :]
            out_ref[lo:hi, :] = z * s * m
            pre = grad_ref[lo:hi, :].astype(F32) * m * (s * (1.0 + z * (1.0 - s)))
            pre_ref[lo:hi, :] = pre
            put_sums(stream, pre, n, sums_ref)

    return call(
        body,
        d_in // CH,
        [cols(rows), cols(4), cols(1), cols(1), cols(rows), full((rows, 1)), cols(rows)],
        [cols(rows), cols(rows), cols(4)],
        [sds((rows, d_in)), sds((rows, d_in)), sds((4, d_in))],
        name="turn_stage",
        flops=20 * rows * d_in,
        transcendentals=rows * d_in,
    )(exp, mr, gain, bias, act, mask, grad)


def norm_back(pre, normed, share_ref, mr_ref, gain_ref, mask, stream):
    return (
        mask
        * (gain_ref[...] * mr_ref[2 * stream + 1 : 2 * stream + 2, :])
        * (
            pre
            - share_ref[2 * stream : 2 * stream + 1, :]
            - normed * share_ref[2 * stream + 1 : 2 * stream + 2, :]
        )
    )


def back_expand(number, pre3, exp, mr3, share3, gain3, mask, w_expand, spa, mr2, gain2, bias2):
    rows, d_in = exp.shape
    mid = spa.shape[1]

    def body(pre3_ref, exp_ref, mr3_ref, share_ref, gain3_ref, mask_ref, w_ref, spa_ref, mr2_ref, gain2_ref, bias2_ref, ge_ref, pre2_ref, sums_ref):
        k = pl.program_id(0)
        for stream, lo, hi in parts(rows):
            n = normed_of(exp_ref[lo:hi, :], mr3_ref, stream)
            ge_ref[lo:hi, :] = norm_back(
                pre3_ref[lo:hi, :], n, share_ref, mr3_ref, gain3_ref, mask_ref[lo:hi, :], stream
            ).astype(BF)
        part = dot_nt(ge_ref[...], w_ref[0])

        @pl.when(k == 0)
        def _():
            pre2_ref[...] = part

        @pl.when(k > 0)
        def _():
            pre2_ref[...] += part

        @pl.when(k == pl.num_programs(0) - 1)
        def _():
            for stream, lo, hi in parts(rows):
                n2 = normed_of(spa_ref[lo:hi, :], mr2_ref, stream)
                z2 = n2 * gain2_ref[...] + bias2_ref[...]
                pre2 = pre2_ref[lo:hi, :] * mask_ref[lo:hi, :] * slope(z2)
                pre2_ref[lo:hi, :] = pre2
                put_sums(stream, pre2, n2, sums_ref)

    return call(
        body,
        d_in // CH,
        [
            cols(rows),
            cols(rows),
            cols(4),
            cols(4),
            cols(1),
            full((rows, 1)),
            pl.BlockSpec((1, mid, CH), lambda k: (number, 0, k)),
            full((rows, mid)),
            full((4, mid)),
            full((1, mid)),
            full((1, mid)),
        ],
        [cols(rows), full((rows, mid)), full((4, mid))],
        [sds((rows, d_in), BF), sds((rows, mid)), sds((4, mid))],
        name="back_expand",
        flops=2 * rows * d_in * mid,
    )(pre3, exp, mr3, share3, gain3, mask, w_expand, spa, mr2, gain2, bias2)


def back_spatial(number, pre2, spa, mr2, share2, gain2, mask, w9, red, mr1, gain1, bias1):
    rows, mid = spa.shape

    def body(pre2_ref, spa_ref, mr2_ref, share_ref, gain2_ref, mask_ref, w_ref, red_ref, mr1_ref, gain1_ref, bias1_ref, gs_ref, pre1_ref, sums_ref, image, tile, patch):
        k = pl.program_id(0)

        @pl.when(k == 0)
        def _():
            pieces = []
            for stream, lo, hi in parts(rows):
                n = normed_of(spa_ref[lo:hi, :], mr2_ref, stream)
                pieces.append(
                    norm_back(pre2_ref[lo:hi, :], n, share_ref, mr2_ref, gain2_ref, mask_ref[lo:hi, :], stream)
                )
            value = jnp.concatenate(pieces, axis=0)
            gs_ref[...] = value.astype(BF)
            fill_patches(value, image, tile, patch, -1)
            pre1_ref[...] = jnp.zeros((rows, mid), F32)

        total = pre1_ref[...]
        for j in range(3):
            total += dot_nt(patch[3 * k + j], w_ref[0, j])
        pre1_ref[...] = total

        @pl.when(k == 2)
        def _():
            for stream, lo, hi in parts(rows):
                n1 = normed_of(red_ref[lo:hi, :], mr1_ref, stream)
                z1 = n1 * gain1_ref[...] + bias1_ref[...]
                pre1 = pre1_ref[lo:hi, :] * mask_ref[lo:hi, :] * slope(z1)
                pre1_ref[lo:hi, :] = pre1
                put_sums(stream, pre1, n1, sums_ref)

    return call(
        body,
        3,
        [
            full((rows, mid)),
            full((rows, mid)),
            full((4, mid)),
            full((4, mid)),
            full((1, mid)),
            full((rows, 1)),
            pl.BlockSpec((1, 3, mid, mid), lambda k: (number, k, 0, 0)),
            full((rows, mid)),
            full((4, mid)),
            full((1, mid)),
            full((1, mid)),
        ],
        [full((rows, mid)), full((rows, mid)), full((4, mid))],
        [sds((rows, mid), BF), sds((rows, mid)), sds((4, mid))],
        [
            pltpu.VMEM((IMG_ROWS + 48, mid), F32),
            pltpu.VMEM((rows - IMG_ROWS + 16, mid), F32),
            pltpu.VMEM((9, rows, mid), BF),
        ],
        name="back_spatial",
        flops=2 * rows * 9 * mid * mid,
    )(pre2, spa, mr2, share2, gain2, mask, w9, red, mr1, gain1, bias1)


def back_reduce(number, pre1, red, mr1, share1, gain1, mask, w_reduce, pre3, below):
    rows, mid = red.shape
    d_in = pre3.shape[1]

    def head(k, pre1_ref, red_ref, mr1_ref, share_ref, gain1_ref, mask_ref, gr_ref):
        @pl.when(k == 0)
        def _():
            for stream, lo, hi in parts(rows):
                n = normed_of(red_ref[lo:hi, :], mr1_ref, stream)
                gr_ref[lo:hi, :] = norm_back(
                    pre1_ref[lo:hi, :], n, share_ref, mr1_ref, gain1_ref, mask_ref[lo:hi, :], stream
                ).astype(BF)

    specs = [
        full((rows, mid)),
        full((rows, mid)),
        full((4, mid)),
        full((4, mid)),
        full((1, mid)),
        full((rows, 1)),
        pl.BlockSpec((1, CH, mid), lambda k: (number, k, 0)),
        cols(rows),
    ]
    args = [pre1, red, mr1, share1, gain1, mask, w_reduce, pre3]
    if below is None:

        def body(pre1_ref, red_ref, mr1_ref, share_ref, gain1_ref, mask_ref, w_ref, pre3_ref, gr_ref, out_ref):
            head(pl.program_id(0), pre1_ref, red_ref, mr1_ref, share_ref, gain1_ref, mask_ref, gr_ref)
            out_ref[...] = pre3_ref[...] + dot_nt(gr_ref[...], w_ref[0])

        return call(
            body,
            d_in // CH,
            specs,
            [full((rows, mid)), cols(rows)],
            [sds((rows, mid), BF), sds((rows, d_in))],
            name="back_reduce_last",
            flops=2 * rows * d_in * mid,
        )(*args)

    def body(pre1_ref, red_ref, mr1_ref, share_ref, gain1_ref, mask_ref, w_ref, pre3_ref, exp_ref, mr3_ref, gain3_ref, bias3_ref, act_ref, gr_ref, out_ref, sums_ref):
        head(pl.program_id(0), pre1_ref, red_ref, mr1_ref, share_ref, gain1_ref, mask_ref, gr_ref)
        grad = pre3_ref[...] + dot_nt(gr_ref[...], w_ref[0])
        for stream, lo, hi in parts(rows):
            n = normed_of(exp_ref[lo:hi, :], mr3_ref, stream)
            z = n * gain3_ref[...] + bias3_ref[...] + act_ref[lo:hi, :].astype(F32)
            pre = grad[lo:hi] * mask_ref[lo:hi, :] * slope(z)
            out_ref[lo:hi, :] = pre
            put_sums(stream, pre, n, sums_ref)

    return call(
        body,
        d_in // CH,
        specs + [cols(rows), cols(4), cols(1), cols(1), cols(rows)],
        [full((rows, mid)), cols(rows), cols(4)],
        [sds((rows, mid), BF), sds((rows, d_in)), sds((4, d_in))],
        name="back_reduce",
        flops=2 * rows * d_in * mid,
        transcendentals=rows * d_in,
    )(*args, *below)


def weight_dot(a, b):
    return lax.dot_general(a, b, (((0,), (0,)), ((), ())), preferred_element_type=F32)


def patches_xla(value):
    rows, width = value.shape
    image = value[:IMG_ROWS].reshape(MAP, MAPW, SLOTS, width)
    tile = value[IMG_ROWS:].reshape(-1, TILE, TILE, width)
    image = jnp.pad(image, ((1, 1), (1, 1), (0, 0), (0, 0)))
    tile = jnp.pad(tile, ((0, 0), (1, 1), (1, 1), (0, 0)))
    taps = []
    for i in range(3):
        for j in range(3):
            a = image[i : i + MAP, j : j + MAPW].reshape(IMG_ROWS, width)
            b = tile[:, i : i + TILE, j : j + TILE].reshape(-1, width)
            taps.append(jnp.concatenate([a, b], axis=0))
    return jnp.stack(taps, axis=1)


def to_rows(image, tile, rows):
    width = image.shape[-1]
    image = jnp.transpose(image, (1, 2, 0, 3))
    image = jnp.pad(image, ((0, 0), (0, 1), (0, 0), (0, 0))).reshape(IMG_ROWS, width)
    tile = tile.reshape(-1, width)
    pad = jnp.zeros((rows - IMG_ROWS - tile.shape[0], width), tile.dtype)
    return jnp.concatenate([image, tile, pad], axis=0)


def from_rows(value, tiles):
    width = value.shape[1]
    image = value[:IMG_ROWS].reshape(MAP, MAPW, SLOTS, width)[:, :MAP]
    image = jnp.transpose(image, (2, 0, 1, 3))
    tile = value[IMG_ROWS : IMG_ROWS + tiles * 4].reshape(tiles, TILE, TILE, width)
    return image, tile


def row_mask(map_sizes, rows):
    row = jnp.arange(MAP)
    col = jnp.arange(MAPW)
    inside = (row[:, None, None] < map_sizes[None, None, :]) & (col[None, :, None] < map_sizes[None, None, :])
    image = inside.astype(F32).reshape(IMG_ROWS)
    tile = jnp.repeat((map_sizes > 0).astype(F32), PIECES * TILE * TILE)
    pad = jnp.zeros((rows - IMG_ROWS - tile.shape[0],), F32)
    return jnp.concatenate([image, tile, pad])[:, None]


def per_device(
    grid,
    images,
    tile_maps,
    map_sizes,
    w_reduce,
    w_spatial,
    w_expand,
    gain_mid,
    bias_mid,
    gain_out,
    bias_out,
    grad_images,
    grad_tiles,
):
    tiles = tile_maps.shape[0]
    rows = -(-(IMG_ROWS + tiles * TILE * TILE) // 16) * 16
    mid = w_reduce.shape[2]
    mask = row_mask(map_sizes, rows)
    counts = jnp.stack([jnp.sum(mask[:IMG_ROWS]), jnp.sum(mask[IMG_ROWS:])])
    inv = 1.0 / jnp.maximum(counts, 1.0)
    sync = Sync(grid, counts)
    w9 = w_spatial.reshape(BLOCKS, 9, mid, mid)
    x = to_rows(images, tile_maps, rows)
    grad = to_rows(grad_images, grad_tiles, rows)

    def row(table, *at):
        return table[at][None]

    acts, lows, reds, spas, exps = [x], [x], [], [], []
    mr1, mr2, mr3, hid1, hid2 = [], [], [], [], []
    red, stats = reduce_first(x, w_reduce, mask, inv)
    for b in range(BLOCKS):
        reds.append(red)
        mr1.append(sync.moments(stats))
        hidden, spa, stats = spatial_stage(
            b, red, mr1[b], row(gain_mid, b, 0), row(bias_mid, b, 0), mask, w9, inv
        )
        hid1.append(hidden)
        spas.append(spa)
        mr2.append(sync.moments(stats))
        hidden, exp, stats = expand_stage(
            b, spa, mr2[b], row(gain_mid, b, 1), row(bias_mid, b, 1), mask, w_expand, inv
        )
        hid2.append(hidden)
        exps.append(exp)
        mr3.append(sync.moments(stats))
        if b + 1 < BLOCKS:
            out, low, red, stats = join_stage(
                b + 1, exp, mr3[b], row(gain_out, b), row(bias_out, b), acts[b], mask, w_reduce, inv
            )
            acts.append(out)
            lows.append(low)
    last = BLOCKS - 1
    out, pre3, sums3 = turn_stage(
        exps[last], mr3[last], row(gain_out, last), row(bias_out, last), acts[last], mask, grad
    )

    g_reduce, g_spatial, g_expand = [None] * BLOCKS, [None] * BLOCKS, [None] * BLOCKS
    g_gain, g_bias = [[None, None] for _ in range(BLOCKS)], [[None, None] for _ in range(BLOCKS)]
    g_gain3, g_bias3 = [None] * BLOCKS, [None] * BLOCKS
    for b in reversed(range(BLOCKS)):
        total = sync.sums(sums3)
        g_gain3[b], g_bias3[b] = total[1] + total[3], total[0] + total[2]
        ge, pre2, sums2 = back_expand(
            b, pre3, exps[b], mr3[b], sync.shares(total), row(gain_out, b), mask, w_expand,
            spas[b], mr2[b], row(gain_mid, b, 1), row(bias_mid, b, 1),
        )
        g_expand[b] = weight_dot(hid2[b], ge)
        total = sync.sums(sums2)
        g_gain[b][1], g_bias[b][1] = total[1] + total[3], total[0] + total[2]
        gs, pre1, sums1 = back_spatial(
            b, pre2, spas[b], mr2[b], sync.shares(total), row(gain_mid, b, 1), mask, w9,
            reds[b], mr1[b], row(gain_mid, b, 0), row(bias_mid, b, 0),
        )
        g_spatial[b] = weight_dot(patches_xla(hid1[b]).reshape(rows, 9 * mid), gs).reshape(3, 3, mid, mid)
        total = sync.sums(sums1)
        g_gain[b][0], g_bias[b][0] = total[1] + total[3], total[0] + total[2]
        below = None
        if b > 0:
            below = (exps[b - 1], mr3[b - 1], row(gain_out, b - 1), row(bias_out, b - 1), acts[b - 1])
        result = back_reduce(
            b, pre1, reds[b], mr1[b], sync.shares(total), row(gain_mid, b, 0), mask, w_reduce, pre3, below
        )
        g_reduce[b] = weight_dot(lows[b], result[0])
        if b > 0:
            pre3, sums3 = result[1], result[2]
        else:
            grad_in = result[1]

    shards = lax.psum(
        (
            lax.psum_scatter(jnp.stack(g_reduce), "narrow", scatter_dimension=1, tiled=True),
            lax.psum_scatter(jnp.stack(g_spatial), "narrow", scatter_dimension=3, tiled=True),
            lax.psum_scatter(jnp.stack(g_expand), "narrow", scatter_dimension=1, tiled=True),
        ),
        "wide",
    )
    out_images, out_tiles = from_rows(out, tiles)
    in_images, in_tiles = from_rows(grad_in, tiles)
    return (
        out_images,
        out_tiles,
        in_images,
        in_tiles,
        shards[0],
        shards[1],
        shards[2],
        jnp.stack([jnp.stack(g) for g in g_gain]),
        jnp.stack([jnp.stack(g) for g in g_bias]),
        jnp.stack(g_gain3),
        jnp.stack(g_bias3),
    )


def solution(mesh):
    both = ("wide", "narrow")
    batch = P(both, None, None, None)
    grid = Grid(mesh.shape["wide"], mesh.shape["narrow"])
    return jax.shard_map(
        functools.partial(per_device, grid),
        mesh=mesh,
        in_specs=(batch, batch, P(both), P(), P(), P(), P(), P(), P(), P(), batch, batch),
        out_specs=(
            batch,
            batch,
            batch,
            batch,
            P(None, "narrow", None),
            P(None, None, None, "narrow", None),
            P(None, "narrow", None),
            P(),
            P(),
            P(),
            P(),
        ),
        check_vma=False,
    )
```

```python
import functools

import jax
import jax.numpy as jnp
from jax import lax
from jax.experimental import pallas as pl
from jax.experimental.pallas import tpu as pltpu
from jax.sharding import PartitionSpec as P

BLOCKS = 2
MAP = 7
MAPW = 8
TILE = 2
PIECES = 9
SLOTS = 2
IMG_ROWS = MAP * MAPW * SLOTS
EPS = 1e-05
CH = 512
BF = jnp.bfloat16
F32 = jnp.float32
VMEM_LIMIT = 48 * 1024 * 1024
AXES = ("wide", "narrow")


class Grid:
    def __init__(self, wide, narrow):
        chips = wide // 2
        side = 1
        while side * side < chips:
            side *= 2
        self.y, self.x, self.c, self.z = chips // side, side, 2, narrow

    def index(self):
        wide = lax.axis_index("wide")
        core = wide % 2
        chip = wide // 2
        return chip // self.x, chip % self.x, core, lax.axis_index("narrow")

    def swap(self, value, dy=0, dx=0, dc=0, dz=0):
        pairs = []
        for y in range(self.y):
            for x in range(self.x):
                for c in range(self.c):
                    for z in range(self.z):
                        src = ((y * self.x + x) * 2 + c) * self.z + z
                        dst = (((y ^ dy) * self.x + (x ^ dx)) * 2 + (c ^ dc)) * self.z + (z ^ dz)
                        pairs.append((src, dst))
        return lax.ppermute(value, AXES, pairs)

    def phases(self):
        found = [[dict(dc=1)]]
        step = 1
        while step < max(self.x, self.y):
            group = []
            for dy in (0, step):
                for dx in (0, step):
                    if (dy or dx) and dy < self.y and dx < self.x:
                        group.append(dict(dy=dy, dx=dx))
            found.append(group)
            step *= 2
        self.far_groups = found[2:]
        found.append([dict(dz=k) for k in range(1, min(self.z, 4))])
        step = 4
        while step < self.z:
            found.append([dict(dz=step)])
            step *= 2
        return found

    def far(self):
        self.phases()
        return self.far_groups


def exchange(grid, payload, join):
    groups = grid.phases()
    for number, group in enumerate(groups):
        members = [payload] + [grid.swap(payload, **step) for step in group]
        if number + 1 < len(groups):
            payload = join(members)
    return members


def add_members(members):
    return sum(members[1:], members[0])


def read_moments(members, stream, width):
    at = slice(2 * stream, 2 * stream + 1)
    counts = [m[at, width : width + 1] for m in members]
    sums = [m[at, 0:width] for m in members]
    count = sum(counts[1:], counts[0])
    plain = sum(sums[1:], sums[0])
    mean = plain / count
    square = None
    for m, n, v in zip(members, counts, sums):
        gap = v / jnp.maximum(n, 1.0) - mean
        term = m[2 * stream + 1 : 2 * stream + 2, 0:width] + n * (gap * gap)
        square = term if square is None else square + term
    return count, plain, mean, square


def join_moments(members):
    width = members[0].shape[1] - 128
    size = len(members)

    def body(*refs):
        out_ref = refs[size]
        for stream in range(2):
            count, plain, _, square = read_moments(refs[:size], stream, width)
            out_ref[2 * stream : 2 * stream + 1, 0:width] = plain
            out_ref[2 * stream + 1 : 2 * stream + 2, 0:width] = square
            out_ref[2 * stream : 2 * stream + 2, width : width + 128] = jnp.broadcast_to(count, (2, 128))

    return pl.pallas_call(body, out_shape=sds((4, width + 128)), name="join_moments")(*members)


def put_statistics(members, out_ref):
    width = out_ref.shape[1]
    for stream in range(2):
        count, _, mean, square = read_moments(members, stream, width)
        out_ref[2 * stream : 2 * stream + 1, :] = mean
        out_ref[2 * stream + 1 : 2 * stream + 2, :] = lax.rsqrt(square / count + EPS)
        out_ref[4 + stream : 5 + stream, :] = jnp.broadcast_to(1.0 / count, (1, width))
    out_ref[6:8, :] = jnp.zeros((2, width), F32)


def put_shares(members, mr_ref, share_ref, both_ref):
    total = members[0][...]
    for m in members[1:]:
        total += m[...]
    for stream in range(2):
        inv = mr_ref[4 + stream : 5 + stream, :]
        share_ref[2 * stream : 2 * stream + 2, :] = total[2 * stream : 2 * stream + 2] * inv
    both_ref[...] = total[0:2] + total[2:4]


def parts(rows):
    return ((0, 0, IMG_ROWS), (1, IMG_ROWS, rows))


def sigmoid(v):
    return 0.5 * jnp.tanh(0.5 * v) + 0.5


def slope(v):
    s = sigmoid(v)
    return s * (1.0 + v * (1.0 - s))


def local_moments(value, mask_ref, stats_ref, at):
    width = value.shape[1]
    for stream, lo, hi in parts(value.shape[0]):
        v = value[lo:hi]
        m = mask_ref[lo:hi, :]
        count = jnp.sum(m, axis=0, keepdims=True)
        plain = jnp.sum(v * m, axis=0, keepdims=True)
        gap = (v - plain / jnp.maximum(count, 1.0)) * m
        stats_ref[2 * stream : 2 * stream + 1, pl.ds(at, width)] = plain
        stats_ref[2 * stream + 1 : 2 * stream + 2, pl.ds(at, width)] = jnp.sum(gap * gap, axis=0, keepdims=True)
        last = stats_ref.shape[1] - 128
        stats_ref[2 * stream : 2 * stream + 2, last : last + 128] = jnp.broadcast_to(count, (2, 128))


def normed_of(value, mr_ref, stream):
    return (value - mr_ref[2 * stream : 2 * stream + 1, :]) * mr_ref[2 * stream + 1 : 2 * stream + 2, :]


def shifted(image_ref, tile_ref, dy, dx, tile_rows):
    start = 24 + 2 * MAPW * dy + 2 * dx
    image = image_ref[start : start + IMG_ROWS, :]
    start = 8 + TILE * dy + dx
    tile = tile_ref[start : start + tile_rows, :]
    if dy or dx:
        place = lax.broadcasted_iota(jnp.int32, (tile_rows, 1), 0)
        ty = (place // TILE) % TILE + dy
        tx = place % TILE + dx
        valid = (ty >= 0) & (ty < TILE) & (tx >= 0) & (tx < TILE)
        tile = jnp.where(valid, tile, 0.0)
    return image, tile


def fill_patches(value, image_ref, tile_ref, patch_ref, sign):
    rows = value.shape[0]
    tile_rows = rows - IMG_ROWS
    width = value.shape[1]
    image_ref[0:24, :] = jnp.zeros((24, width), F32)
    image_ref[24 + IMG_ROWS : 48 + IMG_ROWS, :] = jnp.zeros((24, width), F32)
    image_ref[24 : 24 + IMG_ROWS, :] = value[0:IMG_ROWS]
    tile_ref[0:8, :] = jnp.zeros((8, width), F32)
    tile_ref[8 + tile_rows : 16 + tile_rows, :] = jnp.zeros((8, width), F32)
    tile_ref[8 : 8 + tile_rows, :] = value[IMG_ROWS:]
    for tap in range(9):
        dy, dx = tap // 3 - 1, tap % 3 - 1
        image, tile = shifted(image_ref, tile_ref, sign * dy, sign * dx, tile_rows)
        patch_ref[tap, 0:IMG_ROWS, :] = image.astype(BF)
        patch_ref[tap, IMG_ROWS:rows, :] = tile.astype(BF)


def dot(a, b):
    return jnp.dot(a, b, preferred_element_type=F32)


def dot_nt(a, b):
    return lax.dot_general(a, b, (((1,), (1,)), ((), ())), preferred_element_type=F32)


def full(shape):
    zeros = (0,) * len(shape)
    return pl.BlockSpec(shape, lambda k: zeros)


def cols(rows):
    return pl.BlockSpec((rows, CH), lambda k: (0, k))


def smem():
    return pl.BlockSpec(memory_space=pltpu.SMEM)


def call(body, steps, in_specs, out_specs, out_shape, scratch=(), name=None, flops=0, transcendentals=0):
    return pl.pallas_call(
        body,
        grid=(steps,),
        in_specs=in_specs,
        out_specs=out_specs,
        out_shape=out_shape,
        scratch_shapes=list(scratch),
        compiler_params=pltpu.CompilerParams(
            vmem_limit_bytes=VMEM_LIMIT, dimension_semantics=("arbitrary",)
        ),
        cost_estimate=pl.CostEstimate(flops=flops, bytes_accessed=4_000_000, transcendentals=transcendentals),
        name=name,
    )


def sds(shape, dtype=F32):
    return jax.ShapeDtypeStruct(shape, dtype)


def rounded(value):
    return value.astype(BF).astype(F32)


def payload_shape(width):
    return sds((4, width + 128))


def reduce_first(x, w_reduce, mask):
    rows, d_in = x.shape
    mid = w_reduce.shape[2]

    def body(x_ref, w_ref, mask_ref, red_ref, stats_ref):
        k = pl.program_id(0)
        part = dot(x_ref[...], w_ref[0])

        @pl.when(k == 0)
        def _():
            red_ref[...] = part

        @pl.when(k > 0)
        def _():
            red_ref[...] += part

        @pl.when(k == pl.num_programs(0) - 1)
        def _():
            local_moments(red_ref[...], mask_ref, stats_ref, 0)

    return call(
        body,
        d_in // CH,
        [cols(rows), pl.BlockSpec((1, CH, mid), lambda k: (0, k, 0)), full((rows, 1))],
        [full((rows, mid)), full((4, mid + 128))],
        [sds((rows, mid)), payload_shape(mid)],
        name="reduce_first",
        flops=2 * rows * d_in * mid,
    )(x, w_reduce, mask)


def spatial_stage(number, red, members, gain, bias, mask, w9, select):
    rows, mid = red.shape
    size = len(members)

    def body(red_ref, gain_ref, bias_ref, mask_ref, w_ref, select_ref, *refs):
        got, (mr_ref, keep_ref, send_ref, out_ref, stats_ref, image, tile, patch) = refs[:size], refs[size:]
        k = pl.program_id(0)

        @pl.when(k == 0)
        def _():
            put_statistics(got, mr_ref)
            pieces = []
            for stream, lo, hi in parts(rows):
                z = normed_of(red_ref[lo:hi, :], mr_ref, stream) * gain_ref[...] + bias_ref[...]
                pieces.append(z * sigmoid(z) * mask_ref[lo:hi, :])
            hidden = jnp.concatenate(pieces, axis=0)
            fill_patches(hidden, image, tile, patch, 1)
            halves = dot(hidden.astype(BF), select_ref[...])
            keep_ref[...] = halves[:, : mid // 2]
            send_ref[...] = halves[:, mid // 2 :]
            out_ref[...] = jnp.zeros((rows, mid), F32)

        total = out_ref[...]
        for j in range(3):
            total += dot(patch[3 * k + j], w_ref[0, j])
        out_ref[...] = total

        @pl.when(k == 2)
        def _():
            local_moments(out_ref[...], mask_ref, stats_ref, 0)

    return call(
        body,
        3,
        [
            full((rows, mid)),
            full((1, mid)),
            full((1, mid)),
            full((rows, 1)),
            pl.BlockSpec((1, 3, mid, mid), lambda k: (number, k, 0, 0)),
            full((mid, mid)),
        ]
        + [full((4, mid + 128))] * size,
        [
            full((8, mid)),
            full((rows, mid // 2)),
            full((rows, mid // 2)),
            full((rows, mid)),
            full((4, mid + 128)),
        ],
        [
            sds((8, mid)),
            sds((rows, mid // 2)),
            sds((rows, mid // 2)),
            sds((rows, mid)),
            payload_shape(mid),
        ],
        [
            pltpu.VMEM((IMG_ROWS + 48, mid), F32),
            pltpu.VMEM((rows - IMG_ROWS + 16, mid), F32),
            pltpu.VMEM((9, rows, mid), BF),
        ],
        name="spatial_stage",
        flops=2 * rows * 9 * mid * mid,
    )(red, gain, bias, mask, w9, select, *members)


def expand_stage(number, spa, members, gain, bias, mask, w_expand):
    rows, mid = spa.shape
    d_in = w_expand.shape[2]
    size = len(members)

    def body(spa_ref, gain_ref, bias_ref, mask_ref, w_ref, *refs):
        got, (mr_ref, hid_ref, out_ref, stats_ref) = refs[:size], refs[size:]
        k = pl.program_id(0)

        @pl.when(k == 0)
        def _():
            put_statistics(got, mr_ref)
            for stream, lo, hi in parts(rows):
                z = normed_of(spa_ref[lo:hi, :], mr_ref, stream) * gain_ref[...] + bias_ref[...]
                hid_ref[lo:hi, :] = rounded(z * sigmoid(z) * mask_ref[lo:hi, :])

        value = dot(hid_ref[...].astype(BF), w_ref[0])
        out_ref[...] = value
        local_moments(value, mask_ref, stats_ref, pl.multiple_of(k * CH, CH))

    return call(
        body,
        d_in // CH,
        [
            full((rows, mid)),
            full((1, mid)),
            full((1, mid)),
            full((rows, 1)),
            pl.BlockSpec((1, mid, CH), lambda k: (number, 0, k)),
        ]
        + [full((4, mid + 128))] * size,
        [full((8, mid)), full((rows, mid)), cols(rows), full((4, d_in + 128))],
        [sds((8, mid)), sds((rows, mid)), sds((rows, d_in)), payload_shape(d_in)],
        name="expand_stage",
        flops=2 * rows * d_in * mid,
    )(spa, gain, bias, mask, w_expand, *members)


def pick(ref, k, stream, row):
    return ref[2 * stream + row : 2 * stream + row + 1, pl.ds(pl.multiple_of(k * CH, CH), CH)]


def normed_at(value, mr_ref, k, stream):
    return (value - pick(mr_ref, k, stream, 0)) * pick(mr_ref, k, stream, 1)


def join_stage(number, exp, members, gain, bias, act, mask, w_reduce):
    rows, d_in = exp.shape
    mid = w_reduce.shape[2]
    size = len(members)

    def body(exp_ref, gain_ref, bias_ref, act_ref, mask_ref, w_ref, *refs):
        got, (mr_ref, out_ref, low_ref, red_ref, stats_ref) = refs[:size], refs[size:]
        k = pl.program_id(0)

        @pl.when(k == 0)
        def _():
            put_statistics(got, mr_ref)

        for stream, lo, hi in parts(rows):
            z = (
                normed_at(exp_ref[lo:hi, :], mr_ref, k, stream) * gain_ref[...]
                + bias_ref[...]
                + act_ref[lo:hi, :].astype(F32)
            )
            out = z * sigmoid(z) * mask_ref[lo:hi, :]
            out_ref[lo:hi, :] = out
            low_ref[lo:hi, :] = rounded(out)
        part = dot(low_ref[...].astype(BF), w_ref[0])

        @pl.when(k == 0)
        def _():
            red_ref[...] = part

        @pl.when(k > 0)
        def _():
            red_ref[...] += part

        @pl.when(k == pl.num_programs(0) - 1)
        def _():
            local_moments(red_ref[...], mask_ref, stats_ref, 0)

    return call(
        body,
        d_in // CH,
        [
            cols(rows),
            cols(1),
            cols(1),
            cols(rows),
            full((rows, 1)),
            pl.BlockSpec((1, CH, mid), lambda k: (number, k, 0)),
        ]
        + [full((4, d_in + 128))] * size,
        [full((8, d_in)), cols(rows), cols(rows), full((rows, mid)), full((4, mid + 128))],
        [sds((8, d_in)), sds((rows, d_in)), sds((rows, d_in)), sds((rows, mid)), payload_shape(mid)],
        name="join_stage",
        flops=2 * rows * d_in * mid,
        transcendentals=rows * d_in,
    )(exp, gain, bias, act, mask, w_reduce, *members)


def put_sums(stream, pre, normed, sums_ref):
    sums_ref[2 * stream : 2 * stream + 1, :] = jnp.sum(pre, axis=0, keepdims=True)
    sums_ref[2 * stream + 1 : 2 * stream + 2, :] = jnp.sum(pre * normed, axis=0, keepdims=True)


def turn_stage(exp, members, gain, bias, act, mask, grad):
    rows, d_in = exp.shape
    size = len(members)

    def body(exp_ref, gain_ref, bias_ref, act_ref, mask_ref, grad_ref, *refs):
        got, (mr_ref, out_ref, pre_ref, sums_ref) = refs[:size], refs[size:]
        k = pl.program_id(0)

        @pl.when(k == 0)
        def _():
            put_statistics(got, mr_ref)

        for stream, lo, hi in parts(rows):
            n = normed_at(exp_ref[lo:hi, :], mr_ref, k, stream)
            z = n * gain_ref[...] + bias_ref[...] + act_ref[lo:hi, :].astype(F32)
            s = sigmoid(z)
            m = mask_ref[lo:hi, :]
            out_ref[lo:hi, :] = z * s * m
            pre = grad_ref[lo:hi, :].astype(F32) * m * (s * (1.0 + z * (1.0 - s)))
            pre_ref[lo:hi, :] = pre
            put_sums(stream, pre, n, sums_ref)

    return call(
        body,
        d_in // CH,
        [cols(rows), cols(1), cols(1), cols(rows), full((rows, 1)), cols(rows)]
        + [full((4, d_in + 128))] * size,
        [full((8, d_in)), cols(rows), cols(rows), cols(4)],
        [sds((8, d_in)), sds((rows, d_in)), sds((rows, d_in)), sds((4, d_in))],
        name="turn_stage",
        flops=20 * rows * d_in,
        transcendentals=rows * d_in,
    )(exp, gain, bias, act, mask, grad, *members)


def norm_back(pre, normed, plain, cross, scale, mask):
    return mask * scale * (pre - plain - normed * cross)


def rows_of(ref, stream):
    return ref[2 * stream : 2 * stream + 1, :], ref[2 * stream + 1 : 2 * stream + 2, :]


def back_expand(number, me, pre3, exp, mr3, members, gain3, mask, w_expand, spa, mr2, gain2, bias2):
    rows, d_in = exp.shape
    mid = spa.shape[1]
    half = d_in // 2
    size = len(members)

    def body(me_ref, pre3_ref, exp_ref, mr3_ref, gain3_ref, mask_ref, w_ref, spa_ref, mr2_ref, gain2_ref, bias2_ref, *refs):
        got, (both_ref, keep_ref, send_ref, pre2_ref, sums_ref, share, grad) = refs[:size], refs[size:]
        k = pl.program_id(0)

        @pl.when(k == 0)
        def _():
            put_shares(got, mr3_ref, share, both_ref)

        for stream, lo, hi in parts(rows):
            n = normed_at(exp_ref[lo:hi, :], mr3_ref, k, stream)
            grad[lo:hi, :] = norm_back(
                pre3_ref[lo:hi, :],
                n,
                pick(share, k, stream, 0),
                pick(share, k, stream, 1),
                gain3_ref[...] * pick(mr3_ref, k, stream, 1),
                mask_ref[lo:hi, :],
            ).astype(BF)
        per_half = half // CH
        at = pl.ds(pl.multiple_of(lax.rem(k, per_half) * CH, CH), CH)
        mine = k // per_half == me_ref[0]

        @pl.when(mine)
        def _():
            keep_ref[:, at] = grad[...].astype(F32)

        @pl.when(jnp.logical_not(mine))
        def _():
            send_ref[:, at] = grad[...].astype(F32)

        part = dot_nt(grad[...], w_ref[0])

        @pl.when(k == 0)
        def _():
            pre2_ref[...] = part

        @pl.when(k > 0)
        def _():
            pre2_ref[...] += part

        @pl.when(k == pl.num_programs(0) - 1)
        def _():
            for stream, lo, hi in parts(rows):
                n2 = normed_of(spa_ref[lo:hi, :], mr2_ref, stream)
                z2 = n2 * gain2_ref[...] + bias2_ref[...]
                pre2 = pre2_ref[lo:hi, :] * mask_ref[lo:hi, :] * slope(z2)
                pre2_ref[lo:hi, :] = pre2
                put_sums(stream, pre2, n2, sums_ref)

    return call(
        body,
        d_in // CH,
        [
            smem(),
            cols(rows),
            cols(rows),
            full((8, d_in)),
            cols(1),
            full((rows, 1)),
            pl.BlockSpec((1, mid, CH), lambda k: (number, 0, k)),
            full((rows, mid)),
            full((8, mid)),
            full((1, mid)),
            full((1, mid)),
        ]
        + [full((4, d_in))] * size,
        [full((2, d_in)), full((rows, half)), full((rows, half)), full((rows, mid)), full((4, mid))],
        [sds((2, d_in)), sds((rows, half)), sds((rows, half)), sds((rows, mid)), sds((4, mid))],
        [pltpu.VMEM((4, d_in), F32), pltpu.VMEM((rows, CH), BF)],
        name="back_expand",
        flops=2 * rows * d_in * mid,
    )(me, pre3, exp, mr3, gain3, mask, w_expand, spa, mr2, gain2, bias2, *members)


def back_spatial(number, me, pre2, spa, mr2, members, gain2, mask, w9, red, mr1, gain1, bias1):
    rows, mid = spa.shape
    size = len(members)
    quarter = mid // 4

    def body(me_ref, pre2_ref, spa_ref, mr2_ref, gain2_ref, mask_ref, w_ref, red_ref, mr1_ref, gain1_ref, bias1_ref, *refs):
        got, rest = refs[:size], refs[size:]
        both_ref, gs_ref, pre1_ref, sums_ref, share, image, tile, patch = rest
        k = pl.program_id(0)

        @pl.when(k == 0)
        def _():
            put_shares(got, mr2_ref, share, both_ref)
            pieces = []
            for stream, lo, hi in parts(rows):
                n = normed_of(spa_ref[lo:hi, :], mr2_ref, stream)
                plain, cross = rows_of(share, stream)
                scale = gain2_ref[...] * mr2_ref[2 * stream + 1 : 2 * stream + 2, :]
                pieces.append(norm_back(pre2_ref[lo:hi, :], n, plain, cross, scale, mask_ref[lo:hi, :]))
            value = rounded(jnp.concatenate(pieces, axis=0))
            fill_patches(value, image, tile, patch, -1)
            pre1_ref[...] = value
            for m in range(4):
                at = pl.ds(pl.multiple_of((me_ref[1] ^ m) * quarter, quarter), quarter)
                gs_ref[m, :, :] = pre1_ref[:, at]
            pre1_ref[...] = jnp.zeros((rows, mid), F32)

        total = pre1_ref[...]
        for j in range(3):
            total += dot_nt(patch[3 * k + j], w_ref[0, j])
        pre1_ref[...] = total

        @pl.when(k == 2)
        def _():
            for stream, lo, hi in parts(rows):
                n1 = normed_of(red_ref[lo:hi, :], mr1_ref, stream)
                z1 = n1 * gain1_ref[...] + bias1_ref[...]
                pre1 = pre1_ref[lo:hi, :] * mask_ref[lo:hi, :] * slope(z1)
                pre1_ref[lo:hi, :] = pre1
                put_sums(stream, pre1, n1, sums_ref)

    return call(
        body,
        3,
        [
            smem(),
            full((rows, mid)),
            full((rows, mid)),
            full((8, mid)),
            full((1, mid)),
            full((rows, 1)),
            pl.BlockSpec((1, 3, mid, mid), lambda k: (number, k, 0, 0)),
            full((rows, mid)),
            full((8, mid)),
            full((1, mid)),
            full((1, mid)),
        ]
        + [full((4, mid))] * size,
        [full((2, mid)), full((4, rows, quarter)), full((rows, mid)), full((4, mid))],
        [sds((2, mid)), sds((4, rows, quarter)), sds((rows, mid)), sds((4, mid))],
        [
            pltpu.VMEM((4, mid), F32),
            pltpu.VMEM((IMG_ROWS + 48, mid), F32),
            pltpu.VMEM((rows - IMG_ROWS + 16, mid), F32),
            pltpu.VMEM((9, rows, mid), BF),
        ],
        name="back_spatial",
        flops=2 * rows * 9 * mid * mid,
    )(me, pre2, spa, mr2, gain2, mask, w9, red, mr1, gain1, bias1, *members)


def back_reduce(number, pre1, red, mr1, members, gain1, mask, w_reduce, pre3, below):
    rows, mid = red.shape
    d_in = pre3.shape[1]
    size = len(members)

    def head(k, got, pre1_ref, red_ref, mr1_ref, gain1_ref, mask_ref, both_ref, gr_ref, share):
        @pl.when(k == 0)
        def _():
            put_shares(got, mr1_ref, share, both_ref)
            for stream, lo, hi in parts(rows):
                n = normed_of(red_ref[lo:hi, :], mr1_ref, stream)
                plain, cross = rows_of(share, stream)
                scale = gain1_ref[...] * mr1_ref[2 * stream + 1 : 2 * stream + 2, :]
                gr_ref[lo:hi, :] = rounded(
                    norm_back(pre1_ref[lo:hi, :], n, plain, cross, scale, mask_ref[lo:hi, :])
                )

    specs = [
        full((rows, mid)),
        full((rows, mid)),
        full((8, mid)),
        full((1, mid)),
        full((rows, 1)),
        pl.BlockSpec((1, CH, mid), lambda k: (number, k, 0)),
        cols(rows),
    ]
    args = [pre1, red, mr1, gain1, mask, w_reduce, pre3]
    if below is None:

        def body(pre1_ref, red_ref, mr1_ref, gain1_ref, mask_ref, w_ref, pre3_ref, *refs):
            got, (both_ref, gr_ref, out_ref, share) = refs[:size], refs[size:]
            head(pl.program_id(0), got, pre1_ref, red_ref, mr1_ref, gain1_ref, mask_ref, both_ref, gr_ref, share)
            out_ref[...] = pre3_ref[...] + dot_nt(gr_ref[...].astype(BF), w_ref[0])

        return call(
            body,
            d_in // CH,
            specs + [full((4, mid))] * size,
            [full((2, mid)), full((rows, mid)), cols(rows)],
            [sds((2, mid)), sds((rows, mid)), sds((rows, d_in))],
            [pltpu.VMEM((4, mid), F32)],
            name="back_reduce_last",
            flops=2 * rows * d_in * mid,
        )(*args, *members)

    def body(pre1_ref, red_ref, mr1_ref, gain1_ref, mask_ref, w_ref, pre3_ref, exp_ref, mr3_ref, gain3_ref, bias3_ref, act_ref, *refs):
        got, (both_ref, gr_ref, out_ref, sums_ref, share) = refs[:size], refs[size:]
        k = pl.program_id(0)
        head(k, got, pre1_ref, red_ref, mr1_ref, gain1_ref, mask_ref, both_ref, gr_ref, share)
        grad = pre3_ref[...] + dot_nt(gr_ref[...].astype(BF), w_ref[0])
        for stream, lo, hi in parts(rows):
            n = normed_at(exp_ref[lo:hi, :], mr3_ref, k, stream)
            z = n * gain3_ref[...] + bias3_ref[...] + act_ref[lo:hi, :].astype(F32)
            pre = grad[lo:hi] * mask_ref[lo:hi, :] * slope(z)
            out_ref[lo:hi, :] = pre
            put_sums(stream, pre, n, sums_ref)

    return call(
        body,
        d_in // CH,
        specs + [cols(rows), full((8, d_in)), cols(1), cols(1), cols(rows)] + [full((4, mid))] * size,
        [full((2, mid)), full((rows, mid)), cols(rows), cols(4)],
        [sds((2, mid)), sds((rows, mid)), sds((rows, d_in)), sds((4, d_in))],
        [pltpu.VMEM((4, mid), F32)],
        name="back_reduce",
        flops=2 * rows * d_in * mid,
        transcendentals=rows * d_in,
    )(*args, *below, *members)


def dot_tn(a, b):
    return lax.dot_general(a, b, (((0,), (0,)), ((), ())), preferred_element_type=F32)


def spot(index, size):
    place, bit = 0, 1
    while bit < size:
        place = place * 2 + (index // bit) % 2
        bit *= 2
    return place


def weight_call(body, args, shape, flops, scratch=(), name=None):
    vmem = pl.BlockSpec(memory_space=pltpu.VMEM)
    return pl.pallas_call(
        body,
        in_specs=[smem()] + [vmem] * (len(args) - 1),
        out_specs=vmem,
        out_shape=sds(shape),
        scratch_shapes=list(scratch),
        compiler_params=pltpu.CompilerParams(vmem_limit_bytes=VMEM_LIMIT),
        cost_estimate=pl.CostEstimate(flops=flops, bytes_accessed=4_000_000, transcendentals=0),
        name=name,
    )(*args)


def weight_expand(me, own, peer, keep, got, nz):
    rows, mid = own.shape
    half = keep.shape[1]
    step = half // 4
    deep = mid // nz

    def body(me_ref, own_ref, peer_ref, keep_ref, got_ref, out_ref):
        a = jnp.concatenate([own_ref[...].astype(BF), peer_ref[...].astype(BF)], axis=0)
        for m in range(4):
            at = pl.ds(pl.multiple_of((me_ref[3] ^ m) * step, step), step)
            b = jnp.concatenate([keep_ref[:, at].astype(BF), got_ref[:, at].astype(BF)], axis=0)
            value = dot_tn(a, b)
            for z in range(nz):
                place = spot(me_ref[2] ^ z, nz)
                for t in range(step // 128):
                    out_ref[m * (step // 128) + t, place] = value[z * deep : (z + 1) * deep, t * 128 : (t + 1) * 128]

    return weight_call(
        body,
        (me, own, peer, keep, got),
        (half // 128, nz, deep, 128),
        4 * rows * mid * half,
        name="weight_expand",
    )


def weight_reduce(me, own, peer, keep, got, nz):
    rows, width = own.shape
    mid = keep.shape[1]
    step = mid // 4
    deep = width // nz

    def body(me_ref, own_ref, peer_ref, keep_ref, got_ref, out_ref):
        b = jnp.concatenate([keep_ref[...].astype(BF), got_ref[...].astype(BF)], axis=0)
        for z in range(nz):
            at = slice(z * deep, (z + 1) * deep)
            a = jnp.concatenate([own_ref[:, at].astype(BF), peer_ref[:, at].astype(BF)], axis=0)
            value = dot_tn(a, b)
            place = spot(me_ref[2] ^ z, nz)
            for m in range(4):
                out_ref[me_ref[1] ^ m, place] = value[:, m * step : (m + 1) * step]

    return weight_call(
        body,
        (me, own, peer, keep, got),
        (4, nz, deep, step),
        4 * rows * mid * width,
        name="weight_reduce",
    )


def weight_spatial(me, hidden, near, far, nz):
    both, half = hidden[0].shape
    rows = both // 2
    width = near.shape[2]
    deep = half // nz

    def body(me_ref, h0, h1, h2, h3, near_ref, far_ref, out_ref, image, tile, patch):
        for m in range(4):
            for core, ref in enumerate((near_ref, far_ref)):
                tile_rows = rows - IMG_ROWS
                at = (2 * m + core) * rows
                image[0:24, :] = jnp.zeros((24, width), F32)
                image[24 + IMG_ROWS : 48 + IMG_ROWS, :] = jnp.zeros((24, width), F32)
                image[24 : 24 + IMG_ROWS, :] = ref[m, 0:IMG_ROWS, :]
                tile[0:8, :] = jnp.zeros((8, width), F32)
                tile[8 + tile_rows : 16 + tile_rows, :] = jnp.zeros((8, width), F32)
                tile[8 : 8 + tile_rows, :] = ref[m, IMG_ROWS:rows, :]
                for tap in range(9):
                    dy, dx = tap // 3 - 1, tap % 3 - 1
                    part, rest = shifted(image, tile, -dy, -dx, tile_rows)
                    patch[at : at + IMG_ROWS, tap * width : (tap + 1) * width] = part.astype(BF)
                    patch[at + IMG_ROWS : at + rows, tap * width : (tap + 1) * width] = rest.astype(BF)
        a = jnp.concatenate([r[...].astype(BF) for r in (h0, h1, h2, h3)], axis=0)
        for tap in range(9):
            value = dot_tn(a, patch[:, tap * width : (tap + 1) * width])
            for z in range(nz):
                out_ref[spot(me_ref[2] ^ z, nz), tap] = value[z * deep : (z + 1) * deep]

    return weight_call(
        body,
        (me, *hidden, near, far),
        (nz, 9, deep, width),
        2 * 8 * rows * 9 * half * width,
        [
            pltpu.VMEM((IMG_ROWS + 48, width), F32),
            pltpu.VMEM((rows - IMG_ROWS + 16, width), F32),
            pltpu.VMEM((8 * rows, 9 * width), BF),
        ],
        name="weight_spatial",
    )


class Collect:
    def __init__(self, grid, me, core):
        self.grid, self.me, self.core = grid, me, core

    def over_z(self, value, axis):
        step = 1
        while step < self.grid.z:
            size = value.shape[axis] // 2
            keep = lax.slice_in_dim(value, 0, size, axis=axis)
            send = lax.slice_in_dim(value, size, 2 * size, axis=axis)
            value = keep + self.grid.swap(send, dz=step)
            step *= 2
        return lax.squeeze(value, (axis,))

    def over_plane(self, value, order):
        for name in order:
            size = value.shape[0] // 2
            value = value[:size] + self.grid.swap(value[size:], **{name: 1})
        return value

    def expand(self, own, peer, keep, send):
        got = self.grid.swap(send, dc=1)
        value = weight_expand(self.me, own, peer, keep, got, self.grid.z)
        return self.over_z(self.over_plane(value, ("dx", "dy")), 1)

    def reduce(self, own, peer, grad):
        got = self.grid.swap(grad, dc=1)
        value = weight_reduce(self.me, own, peer, grad, got, self.grid.z)
        return self.over_z(self.over_plane(value, ("dy", "dx")), 1)

    def spatial(self, hidden, grad):
        near = jnp.stack([grad[0]] + [self.grid.swap(grad[m], dy=m >> 1, dx=m & 1) for m in (1, 2, 3)])
        far = self.grid.swap(near, dc=1)
        return self.over_z(weight_spatial(self.me, hidden, near, far, self.grid.z), 0)

    def gather(self, pieces):
        flat = jnp.concatenate([p.reshape(-1, 128) for p in pieces], axis=0)
        for group in self.grid.far():
            flat = flat + sum(self.grid.swap(flat, **step) for step in group)
        own = jnp.stack([flat] + [self.grid.swap(flat, dy=m >> 1, dx=m & 1) for m in (1, 2, 3)])
        return own, self.grid.swap(own, dc=1)


def place_slices(me, number, own, other, shapes, before):
    (e_rows, d_in), (r_rows, mid), (s_rows, _) = shapes
    length = own.shape[1]
    e_len, r_len = 2 * e_rows, r_rows // 2
    dims = ((BLOCKS, r_rows, mid), (BLOCKS, 9, s_rows, mid), (BLOCKS, e_rows, d_in))

    def body(me_ref, own_ref, other_ref, *refs):
        red_ref, spa_ref, exp_ref = refs[-3:]

        def put(ref):
            for t in range(2):
                exp_ref[0, :, t * 128 : (t + 1) * 128] = ref[0, t * e_rows : (t + 1) * e_rows, :]
            red_ref[0] = ref[0, e_len : e_len + r_len, :]
            for tap in range(9):
                at = e_len + r_len + tap * (s_rows // 2)
                spa_ref[0, tap] = ref[0, at : at + s_rows // 2, :]

        mine = pl.program_id(0) // 4 == me_ref[0]

        @pl.when(mine)
        def _():
            put(own_ref)

        @pl.when(jnp.logical_not(mine))
        def _():
            put(other_ref)

    def piece(a, me):
        return (a % 4) ^ me[1], 0, 0

    def e_place(a, me):
        return number, 0, (a // 4) * 4 + (a % 2) * 2 + (a // 2) % 2

    in_specs = [pl.BlockSpec((1, length, 128), piece)] * 2
    out_specs = [
        pl.BlockSpec((1, r_rows // 2, 128), lambda a, me: (number, a // 4, a % 4)),
        pl.BlockSpec((1, 9, s_rows // 2, 128), lambda a, me: (number, 0, a // 4, a % 4)),
        pl.BlockSpec((1, e_rows, 256), e_place),
    ]
    args = (me, own, other)
    aliases = {}
    if before is not None:
        in_specs = in_specs + [pl.BlockSpec(memory_space=pl.ANY)] * 3
        args = args + before
        aliases = {3: 0, 4: 1, 5: 2}
    return pl.pallas_call(
        body,
        grid_spec=pltpu.PrefetchScalarGridSpec(
            num_scalar_prefetch=1, grid=(8,), in_specs=in_specs, out_specs=out_specs
        ),
        out_shape=[sds(d) for d in dims],
        input_output_aliases=aliases,
        compiler_params=pltpu.CompilerParams(dimension_semantics=("arbitrary",)),
        name="place_slices",
    )(*args)


def to_rows(image, tile, rows):
    width = image.shape[-1]
    image = jnp.transpose(image, (1, 2, 0, 3))
    image = jnp.pad(image, ((0, 0), (0, 1), (0, 0), (0, 0))).reshape(IMG_ROWS, width)
    tile = tile.reshape(-1, width)
    pad = jnp.zeros((rows - IMG_ROWS - tile.shape[0], width), tile.dtype)
    return jnp.concatenate([image, tile, pad], axis=0)


def from_rows(value, tiles):
    width = value.shape[1]
    image = value[:IMG_ROWS].reshape(MAP, MAPW, SLOTS, width)[:, :MAP]
    image = jnp.transpose(image, (2, 0, 1, 3))
    tile = value[IMG_ROWS : IMG_ROWS + tiles * 4].reshape(tiles, TILE, TILE, width)
    return image, tile


def row_mask(map_sizes, rows):
    row = jnp.arange(MAP)
    col = jnp.arange(MAPW)
    inside = (row[:, None, None] < map_sizes[None, None, :]) & (col[None, :, None] < map_sizes[None, None, :])
    image = inside.astype(F32).reshape(IMG_ROWS)
    tile = jnp.repeat((map_sizes > 0).astype(F32), PIECES * TILE * TILE)
    pad = jnp.zeros((rows - IMG_ROWS - tile.shape[0],), F32)
    return jnp.concatenate([image, tile, pad])[:, None]


def core_halves(value, core, nz):
    deep = value.shape[1] // (2 * nz)
    low = [value[:, 2 * z * deep : (2 * z + 1) * deep] for z in range(nz)]
    high = [value[:, (2 * z + 1) * deep : (2 * z + 2) * deep] for z in range(nz)]
    low, high = jnp.concatenate(low, axis=1), jnp.concatenate(high, axis=1)
    keep = jnp.where(core == 0, low, high).astype(F32)
    send = jnp.where(core == 0, high, low).astype(F32)
    return keep, send


def core_select(core, mid, nz):
    deep = mid // (2 * nz)
    at = jnp.arange(mid)
    side = at // (mid // 2)
    inner = at % (mid // 2)
    source = (inner // deep) * 2 * deep + (side ^ core) * deep + inner % deep
    return (jnp.arange(mid)[:, None] == source[None, :]).astype(BF)


def per_device(
    grid,
    images,
    tile_maps,
    map_sizes,
    w_reduce,
    w_spatial,
    w_expand,
    gain_mid,
    bias_mid,
    gain_out,
    bias_out,
    grad_images,
    grad_tiles,
):
    tiles = tile_maps.shape[0]
    rows = -(-(IMG_ROWS + tiles * TILE * TILE) // 16) * 16
    d_in, mid = w_reduce.shape[1:]
    nz = grid.z
    y, x, core, z = grid.index()
    chip = (y % 2) * 2 + x % 2
    turned = (x % 2) * 2 + y % 2
    me = jnp.stack([core, chip, z, turned]).astype(jnp.int32)
    mask = row_mask(map_sizes, rows)
    w9 = w_spatial.reshape(BLOCKS, 9, mid, mid)
    start = to_rows(images, tile_maps, rows)
    grad = to_rows(grad_images, grad_tiles, rows)
    select = core_select(core, mid, nz)
    collect = Collect(grid, me, core)

    def row(table, *at):
        return table[at][None]

    def moments(stats):
        return exchange(grid, stats, join_moments)

    def sums(value):
        return exchange(grid, value, add_members)

    acts, lows, reds, spas, exps = [start], [], [], [], []
    mr1, mr2, mr3, hid1, hid2 = [], [], [], [], []
    red, stats = reduce_first(start, w_reduce, mask)
    low = start
    for b in range(BLOCKS):
        keep, send = core_halves(low, core, nz)
        lows.append((keep, grid.swap(send, dc=1)))
        reds.append(red)
        mr, keep, send, spa, stats = spatial_stage(
            b, red, moments(stats), row(gain_mid, b, 0), row(bias_mid, b, 0), mask, w9, select
        )
        mr1.append(mr)
        hidden = jnp.concatenate([keep, grid.swap(send, dc=1)], axis=0)
        hid1.append([hidden] + [grid.swap(hidden, dy=m >> 1, dx=m & 1) for m in (1, 2, 3)])
        spas.append(spa)
        mr, hidden, exp, stats = expand_stage(
            b, spa, moments(stats), row(gain_mid, b, 1), row(bias_mid, b, 1), mask, w_expand
        )
        mr2.append(mr)
        hid2.append((hidden, grid.swap(hidden, dc=1)))
        exps.append(exp)
        if b + 1 < BLOCKS:
            mr, out, low, red, stats = join_stage(
                b + 1, exp, moments(stats), row(gain_out, b), row(bias_out, b), acts[b], mask, w_reduce
            )
            mr3.append(mr)
            acts.append(out)
    last = BLOCKS - 1
    mr, out, pre3, sums3 = turn_stage(
        exps[last], moments(stats), row(gain_out, last), row(bias_out, last), acts[last], mask, grad
    )
    mr3.append(mr)

    both1, both2, both3 = [None] * BLOCKS, [None] * BLOCKS, [None] * BLOCKS
    shapes = ((mid // nz, d_in), (d_in // nz, mid), (mid // nz, mid))
    slices = None
    for b in reversed(range(BLOCKS)):
        both3[b], keep, send, pre2, sums2 = back_expand(
            b, me, pre3, exps[b], mr3[b], sums(sums3), row(gain_out, b), mask, w_expand,
            spas[b], mr2[b], row(gain_mid, b, 1), row(bias_mid, b, 1),
        )
        part_e = collect.expand(*hid2[b], keep, send)
        both2[b], gs, pre1, sums1 = back_spatial(
            b, me, pre2, spas[b], mr2[b], sums(sums2), row(gain_mid, b, 1), mask, w9,
            reds[b], mr1[b], row(gain_mid, b, 0), row(bias_mid, b, 0),
        )
        part_s = collect.spatial(hid1[b], gs)
        below = None
        if b > 0:
            below = (exps[b - 1], mr3[b - 1], row(gain_out, b - 1), row(bias_out, b - 1), acts[b - 1])
        result = back_reduce(
            b, pre1, reds[b], mr1[b], sums(sums1), row(gain_mid, b, 0), mask, w_reduce, pre3, below
        )
        both1[b] = result[0]
        part_r = collect.reduce(*lows[b], result[1])
        own, other = collect.gather((part_e, part_r, part_s))
        slices = place_slices(me, b, own, other, shapes, slices)
        if b > 0:
            pre3, sums3 = result[2], result[3]
        else:
            grad_in = result[2]

    out_images, out_tiles = from_rows(out, tiles)
    in_images, in_tiles = from_rows(grad_in, tiles)
    g_reduce, g_spatial, g_expand = slices

    def table(at):
        return jnp.stack([jnp.stack([both1[b][at], both2[b][at]]) for b in range(BLOCKS)])

    return (
        out_images,
        out_tiles,
        in_images,
        in_tiles,
        g_reduce,
        g_spatial.reshape(BLOCKS, 3, 3, mid // nz, mid),
        g_expand,
        table(1),
        table(0),
        jnp.stack([both3[b][1] for b in range(BLOCKS)]),
        jnp.stack([both3[b][0] for b in range(BLOCKS)]),
    )


def solution(mesh):
    both = ("wide", "narrow")
    batch = P(both, None, None, None)
    grid = Grid(mesh.shape["wide"], mesh.shape["narrow"])
    return jax.shard_map(
        functools.partial(per_device, grid),
        mesh=mesh,
        in_specs=(batch, batch, P(both), P(), P(), P(), P(), P(), P(), P(), batch, batch),
        out_specs=(
            batch,
            batch,
            batch,
            batch,
            P(None, "narrow", None),
            P(None, None, None, "narrow", None),
            P(None, "narrow", None),
            P(),
            P(),
            P(),
            P(),
        ),
        check_vma=False,
    )
```

```python
import functools

import jax
import jax.numpy as jnp
from jax import lax
from jax.experimental import pallas as pl
from jax.experimental.pallas import tpu as pltpu
from jax.sharding import PartitionSpec as P

BLOCKS = 2
MAP = 7
MAPW = 8
TILE = 2
PIECES = 9
SLOTS = 2
IMG_ROWS = MAP * MAPW * SLOTS
EPS = 1e-05
CH = 512
BF = jnp.bfloat16
F32 = jnp.float32
VMEM_LIMIT = 16 * 1024 * 1024
AXES = ("wide", "narrow")
ROOM = 640 * 1024


class Grid:
    def __init__(self, wide, narrow):
        chips = wide // 2
        side = 1
        while side * side < chips:
            side *= 2
        self.y, self.x, self.c, self.z = chips // side, side, 2, narrow

    def index(self):
        wide = lax.axis_index("wide")
        core = wide % 2
        chip = wide // 2
        return chip // self.x, chip % self.x, core, lax.axis_index("narrow")

    def swap(self, value, dy=0, dx=0, dc=0, dz=0):
        pairs = []
        for y in range(self.y):
            for x in range(self.x):
                for c in range(self.c):
                    for z in range(self.z):
                        src = ((y * self.x + x) * 2 + c) * self.z + z
                        dst = (((y ^ dy) * self.x + (x ^ dx)) * 2 + (c ^ dc)) * self.z + (z ^ dz)
                        pairs.append((src, dst))
        return lax.ppermute(value, AXES, pairs)

    def plane(self, value):
        if self.y * self.x == 4:
            return lax.all_gather(value, "wide")
        groups = {}
        for y in range(self.y):
            for x in range(self.x):
                for c in range(2):
                    groups.setdefault((y // 2, x // 2), []).append((y * self.x + x) * 2 + c)
        return lax.all_gather(value, "wide", axis_index_groups=list(groups.values()))

    def phases(self):
        found = [[dict(dc=1)]]
        step = 1
        while step < max(self.x, self.y):
            group = []
            for dy in (0, step):
                for dx in (0, step):
                    if (dy or dx) and dy < self.y and dx < self.x:
                        group.append(dict(dy=dy, dx=dx))
            found.append(group)
            step *= 2
        self.far_groups = found[2:]
        found.append([dict(dz=k) for k in range(1, min(self.z, 4))])
        step = 4
        while step < self.z:
            found.append([dict(dz=step)])
            step *= 2
        return found

    def far(self):
        self.phases()
        return self.far_groups


class Bulk:
    def __init__(self, grid, room):
        self.grid, self.room = grid, room
        self.waiting = []
        self.flying = {"plane": [], "deep": [], "spare": []}
        self.late = []

    def move(self, value, step):
        return step(value) if callable(step) else self.grid.swap(value, **step)

    def add(self, flow):
        self.advance(flow, None)

    def advance(self, flow, value):
        while True:
            try:
                kind, pieces = flow.send(value)
            except StopIteration:
                return
            if kind != "core":
                self.waiting.append((flow, kind, pieces))
                return
            value = [self.move(v, step) for v, step in pieces]

    def load(self, pieces):
        used = {}
        for value, step in pieces:
            for name in () if callable(step) else step:
                used[name] = used.get(name, 0) + value.size * 4
        return used

    def open(self, kinds, arrays):
        used, chosen, rest = {}, [], []
        for item in self.waiting:
            if item[1] in kinds:
                load = self.load(item[2])
                if all(used.get(n, 0) + load[n] <= self.room for n in load):
                    for n in load:
                        used[n] = used.get(n, 0) + load[n]
                    chosen.append(item)
                    continue
                for n in load:
                    used[n] = max(used.get(n, 0), self.room)
            rest.append(item)
        self.waiting = rest
        if not chosen:
            return arrays
        values = [v for _, _, pieces in chosen for v, _ in pieces]
        tied = lax.optimization_barrier(tuple(arrays) + tuple(values))
        arrays, values = list(tied[: len(arrays)]), list(tied[len(arrays) :])
        for flow, kind, pieces in chosen:
            got = [self.move(values.pop(0), step) for _, step in pieces]
            self.flying[kind].append((flow, got))
        return arrays

    def close(self, kind, array):
        done = self.flying[kind]
        self.flying[kind] = []
        if kind == "deep":
            done = done + self.late
            self.late, self.flying["spare"] = self.flying["spare"], []
        if not done:
            return array
        values = [v for _, got in done for v in got]
        tied = lax.optimization_barrier((array,) + tuple(values))
        array, values = tied[0], list(tied[1:])
        for flow, got in done:
            self.advance(flow, [values.pop(0) for _ in got])
        return array

    def last(self, array):
        return self.close("deep", self.close("plane", array))

    def finish(self):
        while self.waiting or self.late or self.flying["spare"]:
            batch, self.waiting = self.waiting, []
            flown = self.late
            self.late, self.flying["spare"] = self.flying["spare"], []
            for flow, kind, pieces in batch:
                got = [self.move(v, step) for v, step in pieces]
                if kind == "spare":
                    self.flying["spare"].append((flow, got))
                else:
                    flown = flown + [(flow, got)]
            values = [v for _, got in flown for v in got]
            if len(values) > 1:
                values = lax.optimization_barrier(values)
            values = list(values)
            for flow, got in flown:
                self.advance(flow, [values.pop(0) for _ in got])


def exchange(grid, bulk, payload, join):
    groups = grid.phases()
    for number, group in enumerate(groups):
        if number == 1:
            payload = bulk.close("plane", payload)
        if number + 1 == len(groups):
            (payload,) = bulk.open(("plane",), [payload])
            payload = bulk.close("deep", payload)
        members = [payload] + [grid.swap(payload, **step) for step in group]
        if number + 1 < len(groups):
            payload = join(members)
    return bulk.open(("deep", "spare"), members)


def add_members(members):
    return sum(members[1:], members[0])


def join_moments(members):
    count = sum(m[2] for m in members)
    plain = sum(m[0] for m in members)
    mean = plain / count
    square = sum(m[1] for m in members)
    for m in members:
        gap = m[0] / jnp.maximum(m[2], 1.0) - mean
        square = square + m[2] * (gap * gap)
    return jnp.stack([plain, square, count])


def put_rows(ref, at, stream, value, first=0):
    base = stream * (ref.shape[1] // 2)
    for j in range(value.shape[1] // 128):
        ref[at, pl.ds(base + first + j, 1), :] = value[:, j * 128 : (j + 1) * 128]


def as_row(value):
    return jnp.concatenate([value[j : j + 1] for j in range(value.shape[0])], axis=1)


def put_statistics(members, out_ref):
    counts = [m[2] for m in members]
    sums = [m[0] for m in members]
    count = sum(counts[1:], counts[0])
    mean = sum(sums[1:], sums[0]) / count
    square = None
    for m, n, v in zip(members, counts, sums):
        gap = v / jnp.maximum(n, 1.0) - mean
        term = m[1] + n * (gap * gap)
        square = term if square is None else square + term
    rstd = lax.rsqrt(square / count + EPS)
    inv = 1.0 / count
    half = mean.shape[0] // 2
    for stream in range(2):
        at = slice(stream * half, (stream + 1) * half)
        out_ref[2 * stream : 2 * stream + 1, :] = as_row(mean[at])
        out_ref[2 * stream + 1 : 2 * stream + 2, :] = as_row(rstd[at])
        out_ref[4 + stream : 5 + stream, :] = as_row(inv[at])
    out_ref[6:8, :] = jnp.zeros((2, out_ref.shape[1]), F32)


def put_shares(members, mr_ref, share_ref, both_ref):
    half = members[0].shape[1] // 2
    for kind in range(2):
        total = members[0][kind]
        for m in members[1:]:
            total += m[kind]
        for stream in range(2):
            value = as_row(total[stream * half : (stream + 1) * half])
            share_ref[2 * stream + kind : 2 * stream + kind + 1, :] = value * mr_ref[4 + stream : 5 + stream, :]
        both_ref[kind : kind + 1, :] = as_row(total[:half] + total[half:])


def parts(rows):
    return ((0, 0, IMG_ROWS), (1, IMG_ROWS, rows))


def sigmoid(v):
    return 0.5 * jnp.tanh(0.5 * v) + 0.5


def slope(v):
    s = sigmoid(v)
    return s * (1.0 + v * (1.0 - s))


def local_moments(value, mask_ref, stats_ref, first):
    width = value.shape[1]
    for stream, lo, hi in parts(value.shape[0]):
        v = value[lo:hi]
        m = mask_ref[lo:hi, :]
        count = jnp.sum(m, axis=0, keepdims=True)
        plain = jnp.sum(v * m, axis=0, keepdims=True)
        gap = (v - plain / jnp.maximum(count, 1.0)) * m
        put_rows(stats_ref, 0, stream, plain, first)
        put_rows(stats_ref, 1, stream, jnp.sum(gap * gap, axis=0, keepdims=True), first)
        put_rows(stats_ref, 2, stream, jnp.broadcast_to(count, (1, width)), first)


def normed_of(value, mr_ref, stream):
    return (value - mr_ref[2 * stream : 2 * stream + 1, :]) * mr_ref[2 * stream + 1 : 2 * stream + 2, :]


def shifted(image_ref, tile_ref, dy, dx, tile_rows):
    start = 24 + 2 * MAPW * dy + 2 * dx
    image = image_ref[start : start + IMG_ROWS, :]
    start = 8 + TILE * dy + dx
    tile = tile_ref[start : start + tile_rows, :]
    if dy or dx:
        place = lax.broadcasted_iota(jnp.int32, (tile_rows, 1), 0)
        ty = (place // TILE) % TILE + dy
        tx = place % TILE + dx
        valid = (ty >= 0) & (ty < TILE) & (tx >= 0) & (tx < TILE)
        tile = jnp.where(valid, tile, 0.0)
    return image, tile


def fill_patches(value, image_ref, tile_ref, patch_ref, sign):
    rows = value.shape[0]
    tile_rows = rows - IMG_ROWS
    width = value.shape[1]
    image_ref[0:24, :] = jnp.zeros((24, width), F32)
    image_ref[24 + IMG_ROWS : 48 + IMG_ROWS, :] = jnp.zeros((24, width), F32)
    image_ref[24 : 24 + IMG_ROWS, :] = value[0:IMG_ROWS]
    tile_ref[0:8, :] = jnp.zeros((8, width), F32)
    tile_ref[8 + tile_rows : 16 + tile_rows, :] = jnp.zeros((8, width), F32)
    tile_ref[8 : 8 + tile_rows, :] = value[IMG_ROWS:]
    for tap in range(9):
        dy, dx = tap // 3 - 1, tap % 3 - 1
        image, tile = shifted(image_ref, tile_ref, sign * dy, sign * dx, tile_rows)
        patch_ref[tap, 0:IMG_ROWS, :] = image.astype(BF)
        patch_ref[tap, IMG_ROWS:rows, :] = tile.astype(BF)


def dot(a, b):
    return jnp.dot(a, b, preferred_element_type=F32)


def dot_nt(a, b):
    return lax.dot_general(a, b, (((1,), (1,)), ((), ())), preferred_element_type=F32)


def full(shape):
    zeros = (0,) * len(shape)
    return pl.BlockSpec(shape, lambda k: zeros)


def cols(rows):
    return pl.BlockSpec((rows, CH), lambda k: (0, k))


def smem():
    return pl.BlockSpec(memory_space=pltpu.SMEM)


def call(body, steps, in_specs, out_specs, out_shape, scratch=(), name=None, flops=0, transcendentals=0):
    return pl.pallas_call(
        body,
        grid=(steps,),
        in_specs=in_specs,
        out_specs=out_specs,
        out_shape=out_shape,
        scratch_shapes=list(scratch),
        compiler_params=pltpu.CompilerParams(
            vmem_limit_bytes=VMEM_LIMIT, dimension_semantics=("arbitrary",)
        ),
        cost_estimate=pl.CostEstimate(flops=0, bytes_accessed=0, transcendentals=0),
        name=name,
    )


def sds(shape, dtype=F32):
    return jax.ShapeDtypeStruct(shape, dtype)


def near(shape, dtype=F32):
    return pltpu.VMEM(shape, dtype)


def stay(value):
    return pltpu.with_memory_space_constraint(value, pltpu.VMEM)


def mid_rows(table_ref, block, place):
    at = 2 * block + place
    return table_ref.at[at : at + 1], table_ref.at[2 * BLOCKS + at : 2 * BLOCKS + at + 1]


def out_rows(table_ref, block):
    return table_ref.at[block : block + 1], table_ref.at[BLOCKS + block : BLOCKS + block + 1]


def rounded(value):
    return value.astype(BF).astype(F32)


def payload(width, kinds=3):
    return (kinds, 2 * width // 128, 128)


def reduce_first(x, w_reduce, mask):
    rows, d_in = x.shape
    mid = w_reduce.shape[2]

    def body(x_ref, w_ref, mask_ref, red_ref, stats_ref):
        k = pl.program_id(0)
        part = dot(x_ref[...], w_ref[0])

        @pl.when(k == 0)
        def _():
            red_ref[...] = part

        @pl.when(k > 0)
        def _():
            red_ref[...] += part

        @pl.when(k == pl.num_programs(0) - 1)
        def _():
            local_moments(red_ref[...], mask_ref, stats_ref, 0)

    return call(
        body,
        d_in // CH,
        [cols(rows), pl.BlockSpec((1, CH, mid), lambda k: (0, k, 0)), full((rows, 1))],
        [full((rows, mid)), full(payload(mid))],
        [near((rows, mid)), near(payload(mid))],
        name="reduce_first",
        flops=2 * rows * d_in * mid,
    )(x, w_reduce, mask)


def spatial_stage(number, red, members, table, mask, w9, select):
    rows, mid = red.shape
    size = len(members)

    def body(red_ref, table_ref, mask_ref, w_ref, select_ref, *refs):
        gain_ref, bias_ref = mid_rows(table_ref, number, 0)
        got, (mr_ref, hid_ref, out_ref, stats_ref, image, tile, patch) = refs[:size], refs[size:]
        k = pl.program_id(0)

        @pl.when(k == 0)
        def _():
            put_statistics(got, mr_ref)
            pieces = []
            for stream, lo, hi in parts(rows):
                z = normed_of(red_ref[lo:hi, :], mr_ref, stream) * gain_ref[...] + bias_ref[...]
                pieces.append(z * sigmoid(z) * mask_ref[lo:hi, :])
            hidden = jnp.concatenate(pieces, axis=0)
            fill_patches(hidden, image, tile, patch, 1)
            hid_ref[...] = dot(hidden.astype(BF), select_ref[...])
            out_ref[...] = jnp.zeros((rows, mid), F32)

        total = out_ref[...]
        for j in range(3):
            total += dot(patch[3 * k + j], w_ref[0, j])
        out_ref[...] = total

        @pl.when(k == 2)
        def _():
            local_moments(out_ref[...], mask_ref, stats_ref, 0)

    return call(
        body,
        3,
        [
            full((rows, mid)),
            full(table.shape),
            full((rows, 1)),
            pl.BlockSpec((1, 3, mid, mid), lambda k: (number, k, 0, 0)),
            full((mid, mid)),
        ]
        + [full(payload(mid))] * size,
        [
            full((8, mid)),
            full((rows, mid)),
            full((rows, mid)),
            full(payload(mid)),
        ],
        [
            near((8, mid)),
            near((rows, mid)),
            near((rows, mid)),
            near(payload(mid)),
        ],
        [
            pltpu.VMEM((IMG_ROWS + 48, mid), F32),
            pltpu.VMEM((rows - IMG_ROWS + 16, mid), F32),
            pltpu.VMEM((9, rows, mid), BF),
        ],
        name="spatial_stage",
        flops=2 * rows * 9 * mid * mid,
    )(red, table, mask, w9, select, *members)


def expand_stage(number, spa, members, table, mask, w_expand):
    rows, mid = spa.shape
    d_in = w_expand.shape[2]
    size = len(members)

    def body(spa_ref, table_ref, mask_ref, w_ref, *refs):
        gain_ref, bias_ref = mid_rows(table_ref, number, 1)
        got, (mr_ref, hid_ref, out_ref, stats_ref) = refs[:size], refs[size:]
        k = pl.program_id(0)

        @pl.when(k == 0)
        def _():
            put_statistics(got, mr_ref)
            for stream, lo, hi in parts(rows):
                z = normed_of(spa_ref[lo:hi, :], mr_ref, stream) * gain_ref[...] + bias_ref[...]
                hid_ref[lo:hi, :] = rounded(z * sigmoid(z) * mask_ref[lo:hi, :])

        value = dot(hid_ref[...].astype(BF), w_ref[0])
        out_ref[...] = value
        local_moments(value, mask_ref, stats_ref, k * (CH // 128))

    return call(
        body,
        d_in // CH,
        [
            full((rows, mid)),
            full(table.shape),
            full((rows, 1)),
            pl.BlockSpec((1, mid, CH), lambda k: (number, 0, k)),
        ]
        + [full(payload(mid))] * size,
        [full((8, mid)), full((rows, mid)), cols(rows), full(payload(d_in))],
        [near((8, mid)), near((rows, mid)), near((rows, d_in)), near(payload(d_in))],
        name="expand_stage",
        flops=2 * rows * d_in * mid,
    )(spa, table, mask, w_expand, *members)


def pick(ref, k, stream, row):
    return ref[2 * stream + row : 2 * stream + row + 1, pl.ds(pl.multiple_of(k * CH, CH), CH)]


def normed_at(value, mr_ref, k, stream):
    return (value - pick(mr_ref, k, stream, 0)) * pick(mr_ref, k, stream, 1)


def join_stage(number, exp, members, table, act, mask, w_reduce):
    rows, d_in = exp.shape
    mid = w_reduce.shape[2]
    size = len(members)

    def body(exp_ref, table_ref, act_ref, mask_ref, w_ref, *refs):
        gain_ref, bias_ref = out_rows(table_ref, number - 1)
        got, (mr_ref, out_ref, low_ref, red_ref, stats_ref) = refs[:size], refs[size:]
        k = pl.program_id(0)

        @pl.when(k == 0)
        def _():
            put_statistics(got, mr_ref)

        for stream, lo, hi in parts(rows):
            z = (
                normed_at(exp_ref[lo:hi, :], mr_ref, k, stream) * gain_ref[...]
                + bias_ref[...]
                + act_ref[lo:hi, :].astype(F32)
            )
            out = z * sigmoid(z) * mask_ref[lo:hi, :]
            out_ref[lo:hi, :] = out
            low_ref[lo:hi, :] = rounded(out)
        part = dot(low_ref[...].astype(BF), w_ref[0])

        @pl.when(k == 0)
        def _():
            red_ref[...] = part

        @pl.when(k > 0)
        def _():
            red_ref[...] += part

        @pl.when(k == pl.num_programs(0) - 1)
        def _():
            local_moments(red_ref[...], mask_ref, stats_ref, 0)

    return call(
        body,
        d_in // CH,
        [
            cols(rows),
            cols(table.shape[0]),
            cols(rows),
            full((rows, 1)),
            pl.BlockSpec((1, CH, mid), lambda k: (number, k, 0)),
        ]
        + [full(payload(d_in))] * size,
        [full((8, d_in)), cols(rows), cols(rows), full((rows, mid)), full(payload(mid))],
        [near((8, d_in)), near((rows, d_in)), near((rows, d_in)), near((rows, mid)), near(payload(mid))],
        name="join_stage",
        flops=2 * rows * d_in * mid,
        transcendentals=rows * d_in,
    )(exp, table, act, mask, w_reduce, *members)


def put_sums(stream, pre, normed, sums_ref, first=0):
    put_rows(sums_ref, 0, stream, jnp.sum(pre, axis=0, keepdims=True), first)
    put_rows(sums_ref, 1, stream, jnp.sum(pre * normed, axis=0, keepdims=True), first)


def turn_stage(number, exp, members, table, act, mask, grad):
    rows, d_in = exp.shape
    size = len(members)

    def body(exp_ref, table_ref, act_ref, mask_ref, grad_ref, *refs):
        gain_ref, bias_ref = out_rows(table_ref, number)
        got, (mr_ref, out_ref, pre_ref, sums_ref) = refs[:size], refs[size:]
        k = pl.program_id(0)

        @pl.when(k == 0)
        def _():
            put_statistics(got, mr_ref)

        for stream, lo, hi in parts(rows):
            n = normed_at(exp_ref[lo:hi, :], mr_ref, k, stream)
            z = n * gain_ref[...] + bias_ref[...] + act_ref[lo:hi, :].astype(F32)
            s = sigmoid(z)
            m = mask_ref[lo:hi, :]
            out_ref[lo:hi, :] = z * s * m
            pre = grad_ref[lo:hi, :].astype(F32) * m * (s * (1.0 + z * (1.0 - s)))
            pre_ref[lo:hi, :] = pre
            put_sums(stream, pre, n, sums_ref, k * (CH // 128))

    return call(
        body,
        d_in // CH,
        [cols(rows), cols(table.shape[0]), cols(rows), full((rows, 1)), cols(rows)]
        + [full(payload(d_in))] * size,
        [full((8, d_in)), cols(rows), cols(rows), full(payload(d_in, 2))],
        [near((8, d_in)), near((rows, d_in)), near((rows, d_in)), near(payload(d_in, 2))],
        name="turn_stage",
        flops=20 * rows * d_in,
        transcendentals=rows * d_in,
    )(exp, table, act, mask, grad, *members)


def norm_back(pre, normed, plain, cross, scale, mask):
    return mask * scale * (pre - plain - normed * cross)


def rows_of(ref, stream):
    return ref[2 * stream : 2 * stream + 1, :], ref[2 * stream + 1 : 2 * stream + 2, :]


def back_expand(number, me, pre3, exp, mr3, members, outer, mask, w_expand, spa, mr2, table):
    rows, d_in = exp.shape
    mid = spa.shape[1]
    half = d_in // 2
    size = len(members)

    def body(me_ref, pre3_ref, exp_ref, mr3_ref, outer_ref, mask_ref, w_ref, spa_ref, mr2_ref, table_ref, *refs):
        gain3_ref, _ = out_rows(outer_ref, number)
        gain2_ref, bias2_ref = mid_rows(table_ref, number, 1)
        got, (both_ref, keep_ref, send_ref, pre2_ref, sums_ref, share, grad) = refs[:size], refs[size:]
        k = pl.program_id(0)

        @pl.when(k == 0)
        def _():
            put_shares(got, mr3_ref, share, both_ref)

        for stream, lo, hi in parts(rows):
            n = normed_at(exp_ref[lo:hi, :], mr3_ref, k, stream)
            grad[lo:hi, :] = norm_back(
                pre3_ref[lo:hi, :],
                n,
                pick(share, k, stream, 0),
                pick(share, k, stream, 1),
                gain3_ref[...] * pick(mr3_ref, k, stream, 1),
                mask_ref[lo:hi, :],
            ).astype(BF)
        per_half = half // CH
        at = pl.ds(pl.multiple_of(lax.rem(k, per_half) * CH, CH), CH)
        mine = k // per_half == me_ref[0]

        @pl.when(mine)
        def _():
            keep_ref[:, at] = grad[...].astype(F32)

        @pl.when(jnp.logical_not(mine))
        def _():
            send_ref[:, at] = grad[...].astype(F32)

        part = dot_nt(grad[...], w_ref[0])

        @pl.when(k == 0)
        def _():
            pre2_ref[...] = part

        @pl.when(k > 0)
        def _():
            pre2_ref[...] += part

        @pl.when(k == pl.num_programs(0) - 1)
        def _():
            for stream, lo, hi in parts(rows):
                n2 = normed_of(spa_ref[lo:hi, :], mr2_ref, stream)
                z2 = n2 * gain2_ref[...] + bias2_ref[...]
                pre2 = pre2_ref[lo:hi, :] * mask_ref[lo:hi, :] * slope(z2)
                pre2_ref[lo:hi, :] = pre2
                put_sums(stream, pre2, n2, sums_ref)

    return call(
        body,
        d_in // CH,
        [
            smem(),
            cols(rows),
            cols(rows),
            full((8, d_in)),
            cols(outer.shape[0]),
            full((rows, 1)),
            pl.BlockSpec((1, mid, CH), lambda k: (number, 0, k)),
            full((rows, mid)),
            full((8, mid)),
            full(table.shape),
        ]
        + [full(payload(d_in, 2))] * size,
        [full((2, d_in)), full((rows, half)), full((rows, half)), full((rows, mid)), full(payload(mid, 2))],
        [near((2, d_in)), near((rows, half)), near((rows, half)), near((rows, mid)), near(payload(mid, 2))],
        [pltpu.VMEM((4, d_in), F32), pltpu.VMEM((rows, CH), BF)],
        name="back_expand",
        flops=2 * rows * d_in * mid,
    )(me, pre3, exp, mr3, outer, mask, w_expand, spa, mr2, table, *members)


def back_spatial(number, me, pre2, spa, mr2, members, table, mask, w9, red, mr1):
    rows, mid = spa.shape
    size = len(members)
    quarter = mid // 4

    def body(me_ref, pre2_ref, spa_ref, mr2_ref, table_ref, mask_ref, w_ref, red_ref, mr1_ref, *refs):
        gain2_ref, _ = mid_rows(table_ref, number, 1)
        gain1_ref, bias1_ref = mid_rows(table_ref, number, 0)
        got, rest = refs[:size], refs[size:]
        both_ref, gs0, gs1, gs2, gs3, pre1_ref, sums_ref, share, image, tile, patch = rest
        k = pl.program_id(0)

        @pl.when(k == 0)
        def _():
            put_shares(got, mr2_ref, share, both_ref)
            pieces = []
            for stream, lo, hi in parts(rows):
                n = normed_of(spa_ref[lo:hi, :], mr2_ref, stream)
                plain, cross = rows_of(share, stream)
                scale = gain2_ref[...] * mr2_ref[2 * stream + 1 : 2 * stream + 2, :]
                pieces.append(norm_back(pre2_ref[lo:hi, :], n, plain, cross, scale, mask_ref[lo:hi, :]))
            value = rounded(jnp.concatenate(pieces, axis=0))
            fill_patches(value, image, tile, patch, -1)
            pre1_ref[...] = value
            for m, ref in enumerate((gs0, gs1, gs2, gs3)):
                at = pl.ds(pl.multiple_of((me_ref[1] ^ m) * quarter, quarter), quarter)
                ref[...] = pre1_ref[:, at]
            pre1_ref[...] = jnp.zeros((rows, mid), F32)

        total = pre1_ref[...]
        for j in range(3):
            total += dot_nt(patch[3 * k + j], w_ref[0, j])
        pre1_ref[...] = total

        @pl.when(k == 2)
        def _():
            for stream, lo, hi in parts(rows):
                n1 = normed_of(red_ref[lo:hi, :], mr1_ref, stream)
                z1 = n1 * gain1_ref[...] + bias1_ref[...]
                pre1 = pre1_ref[lo:hi, :] * mask_ref[lo:hi, :] * slope(z1)
                pre1_ref[lo:hi, :] = pre1
                put_sums(stream, pre1, n1, sums_ref)

    return call(
        body,
        3,
        [
            smem(),
            full((rows, mid)),
            full((rows, mid)),
            full((8, mid)),
            full(table.shape),
            full((rows, 1)),
            pl.BlockSpec((1, 3, mid, mid), lambda k: (number, k, 0, 0)),
            full((rows, mid)),
            full((8, mid)),
        ]
        + [full(payload(mid, 2))] * size,
        [full((2, mid))] + [full((rows, quarter))] * 4 + [full((rows, mid)), full(payload(mid, 2))],
        [near((2, mid))] + [near((rows, quarter))] * 4 + [near((rows, mid)), near(payload(mid, 2))],
        [
            pltpu.VMEM((4, mid), F32),
            pltpu.VMEM((IMG_ROWS + 48, mid), F32),
            pltpu.VMEM((rows - IMG_ROWS + 16, mid), F32),
            pltpu.VMEM((9, rows, mid), BF),
        ],
        name="back_spatial",
        flops=2 * rows * 9 * mid * mid,
    )(me, pre2, spa, mr2, table, mask, w9, red, mr1, *members)


def back_reduce(number, pre1, red, mr1, members, table, mask, w_reduce, pre3, below):
    rows, mid = red.shape
    d_in = pre3.shape[1]
    size = len(members)

    def head(k, got, pre1_ref, red_ref, mr1_ref, table_ref, mask_ref, both_ref, gr_ref, share, low):
        gain1_ref, _ = mid_rows(table_ref, number, 0)

        @pl.when(k == 0)
        def _():
            put_shares(got, mr1_ref, share, both_ref)
            for stream, lo, hi in parts(rows):
                n = normed_of(red_ref[lo:hi, :], mr1_ref, stream)
                plain, cross = rows_of(share, stream)
                scale = gain1_ref[...] * mr1_ref[2 * stream + 1 : 2 * stream + 2, :]
                low[lo:hi, :] = norm_back(pre1_ref[lo:hi, :], n, plain, cross, scale, mask_ref[lo:hi, :]).astype(BF)
            gr_ref[...] = low[...].astype(F32)

    specs = [
        full((rows, mid)),
        full((rows, mid)),
        full((8, mid)),
        full(table.shape),
        full((rows, 1)),
        pl.BlockSpec((1, CH, mid), lambda k: (number, k, 0)),
        cols(rows),
    ]
    args = [pre1, red, mr1, table, mask, w_reduce, pre3]
    scratch = [pltpu.VMEM((4, mid), F32), pltpu.VMEM((rows, mid), BF)]
    if below is None:

        def body(pre1_ref, red_ref, mr1_ref, table_ref, mask_ref, w_ref, pre3_ref, *refs):
            got, (both_ref, gr_ref, out_ref, share, low) = refs[:size], refs[size:]
            k = pl.program_id(0)
            head(k, got, pre1_ref, red_ref, mr1_ref, table_ref, mask_ref, both_ref, gr_ref, share, low)
            out_ref[...] = pre3_ref[...] + dot_nt(low[...], w_ref[0])

        return call(
            body,
            d_in // CH,
            specs + [full(payload(mid, 2))] * size,
            [full((2, mid)), full((rows, mid)), cols(rows)],
            [near((2, mid)), near((rows, mid)), near((rows, d_in))],
            scratch,
            name="back_reduce_last",
            flops=2 * rows * d_in * mid,
        )(*args, *members)

    def body(pre1_ref, red_ref, mr1_ref, table_ref, mask_ref, w_ref, pre3_ref, exp_ref, mr3_ref, outer_ref, act_ref, *refs):
        gain3_ref, bias3_ref = out_rows(outer_ref, number - 1)
        got, (both_ref, gr_ref, out_ref, sums_ref, share, low) = refs[:size], refs[size:]
        k = pl.program_id(0)
        head(k, got, pre1_ref, red_ref, mr1_ref, table_ref, mask_ref, both_ref, gr_ref, share, low)
        grad = pre3_ref[...] + dot_nt(low[...], w_ref[0])
        for stream, lo, hi in parts(rows):
            n = normed_at(exp_ref[lo:hi, :], mr3_ref, k, stream)
            z = n * gain3_ref[...] + bias3_ref[...] + act_ref[lo:hi, :].astype(F32)
            pre = grad[lo:hi] * mask_ref[lo:hi, :] * slope(z)
            out_ref[lo:hi, :] = pre
            put_sums(stream, pre, n, sums_ref, k * (CH // 128))

    return call(
        body,
        d_in // CH,
        specs + [cols(rows), full((8, d_in)), cols(below[2].shape[0]), cols(rows)] + [full(payload(mid, 2))] * size,
        [full((2, mid)), full((rows, mid)), cols(rows), full(payload(d_in, 2))],
        [near((2, mid)), near((rows, mid)), near((rows, d_in)), near(payload(d_in, 2))],
        scratch,
        name="back_reduce",
        flops=2 * rows * d_in * mid,
        transcendentals=rows * d_in,
    )(*args, *below, *members)


def dot_tn(a, b):
    return lax.dot_general(a, b, (((0,), (0,)), ((), ())), preferred_element_type=F32)


def spot(index, size):
    place, bit = 0, 1
    while bit < size:
        place = place * 2 + (index // bit) % 2
        bit *= 2
    return place


def weight_expand(me, own, peer, keep, got, nz, plain):
    rows, mid = own.shape
    half = keep.shape[1]
    step = half // 4
    deep = mid // nz

    def body(me_ref, own_ref, peer_ref, keep_ref, got_ref, x_keep, x_send, y_keep, y_send):
        a = jnp.concatenate([own_ref[...].astype(BF), peer_ref[...].astype(BF)], axis=0)
        for m in range(4):
            at = pl.ds(pl.multiple_of((me_ref[3] ^ m) * step, step), step)
            b = jnp.concatenate([keep_ref[:, at].astype(BF), got_ref[:, at].astype(BF)], axis=0)
            value = dot_tn(a, b)
            x_ref = x_keep if m < 2 else x_send
            y_ref = y_keep if m % 2 == 0 else y_send
            for z in range(nz):
                place = z if plain else spot(me_ref[2] ^ z, nz)
                x_ref[m % 2, place] = value[z * deep : (z + 1) * deep, 0:128]
                y_ref[m // 2, place] = value[z * deep : (z + 1) * deep, 128:256]

    vmem = pl.BlockSpec(memory_space=pltpu.VMEM)
    return pl.pallas_call(
        body,
        in_specs=[smem()] + [vmem] * 4,
        out_specs=[vmem] * 4,
        out_shape=[sds((2, nz, deep, 128))] * 4,
        compiler_params=pltpu.CompilerParams(vmem_limit_bytes=VMEM_LIMIT),
        cost_estimate=pl.CostEstimate(flops=0, bytes_accessed=0, transcendentals=0),
        name="weight_expand",
    )(me, own, peer, keep, got)


def slice_outputs(nz, shape, plain):
    if plain:
        return [sds((nz,) + shape)]
    return [sds((nz // 2,) + shape)] * 2


def put_slices(me_ref, total, outs, nz, deep, plain, put):
    for p in range(nz):
        z = p if plain else me_ref[2] ^ spot(p, nz)
        rows = total[pl.ds(pl.multiple_of(z * deep, deep), deep), :]
        part, at = (0, p) if plain else divmod(p, nz // 2)
        put(outs[part], at, rows)


def weight_reduce(me, own, peer, keep, got, nz, plain):
    rows, width = own.shape
    mid = keep.shape[1]
    step = mid // 4
    deep = width // nz
    part = deep // 2

    def body(me_ref, own_ref, peer_ref, keep_ref, got_ref, x_keep, x_send, y_keep, y_send, total):
        b = jnp.concatenate([keep_ref[...].astype(BF), got_ref[...].astype(BF)], axis=0)
        for z in range(nz):
            at = slice(z * deep, (z + 1) * deep)
            a = jnp.concatenate([own_ref[:, at].astype(BF), peer_ref[:, at].astype(BF)], axis=0)
            total[...] = dot_tn(a, b)
            place = z if plain else spot(me_ref[2] ^ z, nz)
            for m in range(4):
                column = me_ref[1] ^ ((m % 2) * 2 + m // 2)
                value = total[:, pl.ds(pl.multiple_of(column * step, step), step)]
                (x_keep if m < 2 else x_send)[m % 2, place] = value[:part]
                (y_keep if m % 2 == 0 else y_send)[m // 2, place] = value[part:]

    vmem = pl.BlockSpec(memory_space=pltpu.VMEM)
    return pl.pallas_call(
        body,
        in_specs=[smem()] + [vmem] * 4,
        out_specs=[vmem] * 4,
        out_shape=[sds((2, nz, part, step))] * 4,
        scratch_shapes=[pltpu.VMEM((deep, mid), F32)],
        compiler_params=pltpu.CompilerParams(vmem_limit_bytes=VMEM_LIMIT),
        cost_estimate=pl.CostEstimate(flops=0, bytes_accessed=0, transcendentals=0),
        name="weight_reduce",
    )(me, own, peer, keep, got)


def weight_spatial(me, hidden, near, far, nz, plain):
    _, rows, mid = hidden.shape
    width = near.shape[2]
    half = mid // 2
    deep = half // nz
    tile_rows = rows - IMG_ROWS
    shapes = slice_outputs(nz, (9, deep, width), plain)

    def body(me_ref, hidden_ref, near_ref, far_ref, *refs):
        outs, (image, tile, left, patch, total) = refs[:-5], refs[-5:]
        k = pl.program_id(0)
        m = (k // 2) ^ me_ref[1]
        mine = lax.rem(k, 2) == me_ref[0]

        @pl.when(k == 0)
        def _():
            image[...] = jnp.zeros_like(image)
            tile[...] = jnp.zeros_like(tile)

        value = jnp.where(mine, near_ref[m], far_ref[m])
        image[24 : 24 + IMG_ROWS, :] = value[0:IMG_ROWS]
        tile[8 : 8 + tile_rows, :] = value[IMG_ROWS:rows]
        for tap in range(9):
            dy, dx = tap // 3 - 1, tap % 3 - 1
            part, rest = shifted(image, tile, -dy, -dx, tile_rows)
            patch[k, 0:IMG_ROWS, tap * width : (tap + 1) * width] = part.astype(BF)
            patch[k, IMG_ROWS:rows, tap * width : (tap + 1) * width] = rest.astype(BF)
        at = pl.ds(pl.multiple_of(jnp.where(mine, 0, half), half), half)
        left[k] = hidden_ref[0, :, at].astype(BF)

        @pl.when(k == 7)
        def _():
            a = left[...].reshape(8 * rows, half)
            total[...] = dot_tn(a, patch[...].reshape(8 * rows, 9 * width))

            def put(ref, at, value):
                for tap in range(9):
                    ref[at, tap] = value[:, tap * width : (tap + 1) * width]

            put_slices(me_ref, total, outs, nz, deep, plain, put)

    return call(
        body,
        8,
        [
            smem(),
            pl.BlockSpec((1, rows, mid), lambda k: (k, 0, 0)),
            full(near.shape),
            full(far.shape),
        ],
        [full(v.shape) for v in shapes],
        shapes,
        [
            pltpu.VMEM((IMG_ROWS + 48, width), F32),
            pltpu.VMEM((tile_rows + 16, width), F32),
            pltpu.VMEM((8, rows, half), BF),
            pltpu.VMEM((8, rows, 9 * width), BF),
            pltpu.VMEM((half, 9 * width), F32),
        ],
        name="weight_spatial",
        flops=16 * rows * 9 * half * width,
    )(me, hidden, near, far)


class Collect:
    def __init__(self, grid, me, spare):
        self.grid, self.me, self.spare = grid, me, spare

    def over_z(self, keep, send):
        step = 1
        while True:
            (got,) = yield "deep", [(send, dict(dz=step))]
            step *= 2
            if step == self.grid.z:
                return keep[0] + got[0]
            half = keep.shape[0] // 2
            keep, send = keep[:half] + got[:half], keep[half:] + got[half:]

    def scatter(self, value):
        return lax.psum_scatter(value, "narrow", scatter_dimension=0, tiled=True)[0]

    def by_halves(self, kernel, own, peer, keep, send, out, after=None):
        (got,) = yield "core", [(send, dict(dc=1))]
        if after is not None:
            got, _ = lax.optimization_barrier((got, after()[0]))
        x_keep, x_send, y_keep, y_send = kernel(self.me, own, peer, keep, got, self.grid.z, self.spare)
        got = yield "plane", [(x_send, dict(dx=1)), (y_send, dict(dy=1))]
        x_last, y_last = x_keep[1:] + got[0][1:], y_keep[1:] + got[1][1:]
        x_keep, y_keep = x_keep[:1] + got[0][:1], y_keep[:1] + got[1][:1]
        got = yield "plane", [(x_last, dict(dy=1)), (y_last, dict(dx=1))]
        if self.spare:
            value = jnp.concatenate([x_keep[0] + got[0][0], y_keep[0] + got[1][0]], axis=1)
            (piece,) = yield "spare", [(value, self.scatter)]
            out.append(piece)
            return
        half = self.grid.z // 2

        def side(at):
            return jnp.concatenate([x_keep[0, at] + got[0][0, at], y_keep[0, at] + got[1][0, at]], axis=1)

        piece = yield from self.over_z(side(slice(0, half)), side(slice(half, 2 * half)))
        out.append(piece)

    def by_rows(self, kernel, rows_of_plane, grad, out):
        got = yield "plane", [(grad[1], dict(dx=1)), (grad[2], dict(dy=1)), (grad[3], dict(dy=1, dx=1))]
        near = jnp.stack([grad[0]] + list(got))
        (far,) = yield "core", [(near, dict(dc=1))]
        result = kernel(self.me, rows_of_plane, near, far, self.grid.z, self.spare)
        self.marks = result
        if self.spare:
            (piece,) = yield "spare", [(result[0], self.scatter)]
            out.append(piece)
        else:
            piece = yield from self.over_z(*result)
            out.append(piece)

    def flat(self, pieces):
        flat = jnp.concatenate([p[0].reshape(-1, 128) for p in pieces], axis=0)
        for group in self.grid.far():
            flat = flat + sum(self.grid.swap(flat, **step) for step in group)
        return flat

    def gather(self, pieces, out):
        (got,) = yield "spare", [(self.flat(pieces), self.grid.plane)]
        out.append(got)

    def chips(self, flat):
        return [flat] + [self.grid.swap(flat, dy=m >> 1, dx=m & 1) for m in (1, 2, 3)]

    def cores(self, values):
        return values + [self.grid.swap(v, dc=1) for v in values]


def place_slices(me, number, gathered, shapes, before):
    (e_rows, d_in), (r_rows, mid), (s_rows, _) = shapes
    dims = ((BLOCKS, r_rows, mid), (BLOCKS, 9, s_rows, mid), (BLOCKS, e_rows, d_in))
    size = len(gathered)
    r_len, s_len = r_rows // 2, s_rows // 2

    def body(me_ref, *refs):
        got = refs[:size]
        outs, (red, spa, exp, sems, out_sems) = refs[-8:-5], refs[-5:]

        def aligned(value, unit):
            return value if isinstance(value, int) else pl.multiple_of(value, unit)

        copies = []
        for a in range(8):
            if size == 2:
                core, chip = a % 2, a // 2
                source, source_r = got[0].at[a], got[1].at[a]
            else:
                core = me_ref[0] if a < 4 else 1 - me_ref[0]
                chip = (a % 4) ^ me_ref[1]
                source, source_r = got[a], got[8 + a]
            column = core * 4 + (chip % 2) * 2 + chip // 2
            moves = []
            for t in range(2):
                at = aligned(column * 256 + t * 128, 128)
                moves.append((source.at[pl.ds(t * e_rows, e_rows), :], exp.at[:, pl.ds(at, 128)]))
            at = aligned(chip * 128, 128)
            row = aligned(core * r_len, r_len)
            moves.append((source_r, red.at[pl.ds(row, r_len), pl.ds(at, 128)]))
            row = aligned(core * s_len, s_len)
            for tap in range(9):
                moves.append(
                    (
                        source.at[pl.ds(2 * e_rows + tap * s_len, s_len), :],
                        spa.at[tap, pl.ds(row, s_len), pl.ds(at, 128)],
                    )
                )
            copies += [pltpu.make_async_copy(src, dst, sems.at[a, i]) for i, (src, dst) in enumerate(moves)]
        for copy in copies:
            copy.start()
        for copy in copies:
            copy.wait()
        copies = [
            pltpu.make_async_copy(src, dst.at[number], out_sems.at[i])
            for i, (src, dst) in enumerate(zip((red, spa, exp), outs))
        ]
        for copy in copies:
            copy.start()
        for copy in copies:
            copy.wait()

    anywhere = pl.BlockSpec(memory_space=pl.ANY)
    args = (me,) + tuple(gathered)
    aliases = {}
    if before is not None:
        aliases = {len(args) + i: i for i in range(3)}
        args = args + tuple(before)
    return pl.pallas_call(
        body,
        in_specs=[smem()] + [anywhere] * (len(args) - 1),
        out_specs=[anywhere] * 3,
        out_shape=[sds(d) for d in dims],
        scratch_shapes=[pltpu.VMEM(d[1:], F32) for d in dims]
        + [pltpu.SemaphoreType.DMA((8, 12)), pltpu.SemaphoreType.DMA((3,))],
        input_output_aliases=aliases,
        compiler_params=pltpu.CompilerParams(vmem_limit_bytes=VMEM_LIMIT),
        name="place_slices",
    )(*args)


def to_rows(image, tile, rows):
    width = image.shape[-1]
    image = jnp.transpose(image, (1, 2, 0, 3))
    image = jnp.pad(image, ((0, 0), (0, 1), (0, 0), (0, 0))).reshape(IMG_ROWS, width)
    tile = tile.reshape(-1, width)
    pad = jnp.zeros((rows - IMG_ROWS - tile.shape[0], width), tile.dtype)
    return jnp.concatenate([image, tile, pad], axis=0)


def from_rows(value, tiles):
    width = value.shape[1]
    image = value[:IMG_ROWS].reshape(MAP, MAPW, SLOTS, width)[:, :MAP]
    image = jnp.transpose(image, (2, 0, 1, 3))
    tile = value[IMG_ROWS : IMG_ROWS + tiles * 4].reshape(tiles, TILE, TILE, width)
    return image, tile


def row_mask(map_sizes, rows):
    row = jnp.arange(MAP)
    col = jnp.arange(MAPW)
    inside = (row[:, None, None] < map_sizes[None, None, :]) & (col[None, :, None] < map_sizes[None, None, :])
    image = inside.astype(F32).reshape(IMG_ROWS)
    tile = jnp.repeat((map_sizes > 0).astype(F32), PIECES * TILE * TILE)
    pad = jnp.zeros((rows - IMG_ROWS - tile.shape[0],), F32)
    return jnp.concatenate([image, tile, pad])[:, None]


def core_halves(value, core, nz):
    deep = value.shape[1] // (2 * nz)
    low = [value[:, 2 * z * deep : (2 * z + 1) * deep] for z in range(nz)]
    high = [value[:, (2 * z + 1) * deep : (2 * z + 2) * deep] for z in range(nz)]
    low, high = jnp.concatenate(low, axis=1), jnp.concatenate(high, axis=1)
    keep = jnp.where(core == 0, low, high).astype(F32)
    send = jnp.where(core == 0, high, low).astype(F32)
    return keep, send


def core_select(core, mid, nz):
    deep = mid // (2 * nz)
    at = jnp.arange(mid)
    side = at // (mid // 2)
    inner = at % (mid // 2)
    source = (inner // deep) * 2 * deep + (side ^ core) * deep + inner % deep
    return (jnp.arange(mid)[:, None] == source[None, :]).astype(BF)


def per_device(
    grid,
    images,
    tile_maps,
    map_sizes,
    w_reduce,
    w_spatial,
    w_expand,
    gain_mid,
    bias_mid,
    gain_out,
    bias_out,
    grad_images,
    grad_tiles,
):
    tiles = tile_maps.shape[0]
    rows = -(-(IMG_ROWS + tiles * TILE * TILE) // 16) * 16
    d_in, mid = w_reduce.shape[1:]
    nz = grid.z
    y, x, core, z = grid.index()
    chip = (y % 2) * 2 + x % 2
    turned = (x % 2) * 2 + y % 2
    me = jnp.stack([core, chip, z, turned]).astype(jnp.int32)
    mask = row_mask(map_sizes, rows)
    w9 = w_spatial.reshape(BLOCKS, 9, mid, mid)
    start = to_rows(images, tile_maps, rows)
    grad = to_rows(grad_images, grad_tiles, rows)
    select = core_select(core, mid, nz)
    collect = [Collect(grid, me, b > 0) for b in range(BLOCKS)]
    bulk = Bulk(grid, ROOM)

    table = stay(jnp.concatenate([gain_mid.reshape(-1, mid), bias_mid.reshape(-1, mid)]))
    outer = stay(jnp.concatenate([gain_out, bias_out]))
    w_reduce, w9, w_expand = stay(w_reduce), stay(w9), stay(w_expand)

    def moments(stats):
        return exchange(grid, bulk, stats, join_moments)

    def sums(value):
        return exchange(grid, bulk, value, add_members)

    acts, lows, reds, spas, exps = [start], [], [], [], []
    mr1, mr2, mr3, hid1, hid2 = [], [], [], [], []
    red, stats = reduce_first(start, w_reduce, mask)
    low = start
    for b in range(BLOCKS):
        reds.append(red)
        mr, hidden, spa, stats = spatial_stage(
            b, red, moments(stats), table, mask, w9, select
        )
        mr1.append(mr)
        hid1.append(pltpu.with_memory_space_constraint(grid.plane(hidden), pltpu.HBM))
        keep, send = core_halves(low, core, nz)
        peer = grid.swap(send, dc=1)
        stats, keep, peer = lax.optimization_barrier((stats, keep, peer))
        lows.append((keep, peer))
        spas.append(spa)
        mr, hidden, exp, stats = expand_stage(
            b, spa, moments(stats), table, mask, w_expand
        )
        mr2.append(mr)
        hid2.append((hidden, grid.swap(hidden, dc=1)))
        exps.append(exp)
        if b + 1 < BLOCKS:
            mr, out, low, red, stats = join_stage(
                b + 1, exp, moments(stats), outer, acts[b], mask, w_reduce
            )
            mr3.append(mr)
            acts.append(out)
    last = BLOCKS - 1
    mr, out, pre3, sums3 = turn_stage(
        last, exps[last], moments(stats), outer, acts[last], mask, grad
    )
    mr3.append(mr)

    both1, both2, both3 = [None] * BLOCKS, [None] * BLOCKS, [None] * BLOCKS
    shapes = ((mid // nz, d_in), (d_in // nz, mid), (mid // nz, mid))
    pieces = [([], [], []) for _ in range(BLOCKS)]
    whole = [[[], []] for _ in range(BLOCKS)]

    def then(flow, b):
        yield from flow
        part_e, part_r, part_s = pieces[b]
        if b > 0 and part_e and part_s and not started[b][0]:
            started[b][0] = True
            bulk.add(collect[b].gather((part_e, part_s), whole[b][0]))
        if b > 0 and part_r and not started[b][1]:
            started[b][1] = True
            bulk.add(collect[b].gather((part_r,), whole[b][1]))

    started = [[False, False] for _ in range(BLOCKS)]
    for b in reversed(range(BLOCKS)):
        both3[b], keep, send, pre2, sums2 = back_expand(
            b, me, pre3, exps[b], mr3[b], sums(sums3), outer, mask, w_expand,
            spas[b], mr2[b], table,
        )
        bulk.add(then(collect[b].by_halves(weight_expand, *hid2[b], keep, send, pieces[b][0]), b))
        both2[b], *gs, pre1, sums1 = back_spatial(
            b, me, pre2, spas[b], mr2[b], sums(sums2), table, mask, w9,
            reds[b], mr1[b],
        )
        bulk.add(then(collect[b].by_rows(weight_spatial, hid1[b], gs, pieces[b][2]), b))
        below = None
        if b > 0:
            below = (exps[b - 1], mr3[b - 1], outer, acts[b - 1])
        result = back_reduce(
            b, pre1, reds[b], mr1[b], sums(sums1), table, mask, w_reduce, pre3, below
        )
        both1[b] = result[0]
        gr = result[1]
        after = None
        if b == 0:
            gr = bulk.last(gr)
            after = lambda: collect[0].marks
        bulk.add(then(collect[b].by_halves(weight_reduce, *lows[b], gr, gr, pieces[b][1], after), b))
        if b > 0:
            pre3, sums3 = result[2], result[3]
        else:
            grad_in = result[2]

    bulk.finish()
    slices = None
    for b in reversed(range(BLOCKS)):
        part_e, part_r, part_s = pieces[b]
        if b > 0:
            gathered = whole[b][0] + whole[b][1]
        else:
            first = collect[b].chips(collect[b].flat((part_e, part_s)))
            second = collect[b].chips(collect[b].flat((part_r,)))
            slices, first = lax.optimization_barrier((slices, first))
            gathered = collect[b].cores(first) + collect[b].cores(second)
        slices = place_slices(me, b, gathered, shapes, slices)
    out_images, out_tiles = from_rows(out, tiles)
    in_images, in_tiles = from_rows(grad_in, tiles)
    g_reduce, g_spatial, g_expand = slices

    def pair(at):
        return jnp.stack([jnp.stack([both1[b][at], both2[b][at]]) for b in range(BLOCKS)])

    return (
        out_images,
        out_tiles,
        in_images,
        in_tiles,
        g_reduce,
        g_spatial.reshape(BLOCKS, 3, 3, mid // nz, mid),
        g_expand,
        pair(1),
        pair(0),
        jnp.stack([both3[b][1] for b in range(BLOCKS)]),
        jnp.stack([both3[b][0] for b in range(BLOCKS)]),
    )


def solution(mesh):
    both = ("wide", "narrow")
    batch = P(both, None, None, None)
    grid = Grid(mesh.shape["wide"], mesh.shape["narrow"])
    return jax.shard_map(
        functools.partial(per_device, grid),
        mesh=mesh,
        in_specs=(batch, batch, P(both), P(), P(), P(), P(), P(), P(), P(), batch, batch),
        out_specs=(
            batch,
            batch,
            batch,
            batch,
            P(None, "narrow", None),
            P(None, None, None, "narrow", None),
            P(None, "narrow", None),
            P(),
            P(),
            P(),
            P(),
        ),
        check_vma=False,
    )
```

```python
import functools

import jax
import jax.numpy as jnp
from jax import lax
from jax.experimental import pallas as pl
from jax.experimental.pallas import tpu as pltpu
from jax.sharding import PartitionSpec as P

BLOCKS = 2
MAP = 7
MAPW = 8
TILE = 2
PIECES = 9
SLOTS = 2
IMG_ROWS = MAP * MAPW * SLOTS
EPS = 1e-05
CH = 512
BF = jnp.bfloat16
F32 = jnp.float32
VMEM_LIMIT = 16 * 1024 * 1024
AXES = ("wide", "narrow")
ROOM = 640 * 1024


class Grid:
    def __init__(self, wide, narrow):
        chips = wide // 2
        side = 1
        while side * side < chips:
            side *= 2
        self.y, self.x, self.c, self.z = chips // side, side, 2, narrow

    def index(self):
        wide = lax.axis_index("wide")
        core = wide % 2
        chip = wide // 2
        return chip // self.x, chip % self.x, core, lax.axis_index("narrow")

    def swap(self, value, dy=0, dx=0, dc=0, dz=0):
        pairs = []
        for y in range(self.y):
            for x in range(self.x):
                for c in range(self.c):
                    for z in range(self.z):
                        src = ((y * self.x + x) * 2 + c) * self.z + z
                        dst = (((y ^ dy) * self.x + (x ^ dx)) * 2 + (c ^ dc)) * self.z + (z ^ dz)
                        pairs.append((src, dst))
        return lax.ppermute(value, AXES, pairs)

    def plane(self, value):
        if self.y * self.x == 4:
            return lax.all_gather(value, "wide")
        groups = {}
        for y in range(self.y):
            for x in range(self.x):
                for c in range(2):
                    groups.setdefault((y // 2, x // 2), []).append((y * self.x + x) * 2 + c)
        return lax.all_gather(value, "wide", axis_index_groups=list(groups.values()))

    def phases(self):
        found = [[dict(dc=1)]]
        step = 1
        while step < max(self.x, self.y):
            group = []
            for dy in (0, step):
                for dx in (0, step):
                    if (dy or dx) and dy < self.y and dx < self.x:
                        group.append(dict(dy=dy, dx=dx))
            found.append(group)
            step *= 2
        self.far_groups = found[2:]
        found.append([dict(dz=k) for k in range(1, min(self.z, 4))])
        step = 4
        while step < self.z:
            found.append([dict(dz=step)])
            step *= 2
        return found

    def far(self):
        self.phases()
        return self.far_groups


class Bulk:
    def __init__(self, grid, room):
        self.grid, self.room = grid, room
        self.waiting = []
        self.flying = {"plane": [], "tight": [], "deep": [], "spare": []}
        self.late = []
        self.names = {}

    def move(self, value, step):
        return step(value) if callable(step) else self.grid.swap(value, **step)

    def add(self, name, flow):
        self.names[flow] = name
        self.advance(flow, None)

    def advance(self, flow, value):
        while True:
            try:
                kind, pieces = flow.send(value)
            except StopIteration:
                return
            if kind != "core":
                self.waiting.append((flow, kind, pieces))
                return
            value = [self.move(v, step) for v, step in pieces]

    def load(self, pieces):
        used = {}
        for value, step in pieces:
            for name in () if callable(step) else step:
                used[name] = used.get(name, 0) + value.size * 4
        return used

    def open(self, kinds, arrays):
        used, chosen, rest = {}, [], []
        for item in self.waiting:
            if item[1] in kinds:
                load = self.load(item[2])
                if all(used.get(n, 0) + load[n] <= self.room for n in load):
                    for n in load:
                        used[n] = used.get(n, 0) + load[n]
                    chosen.append(item)
                    continue
                for n in load:
                    used[n] = max(used.get(n, 0), self.room)
            rest.append(item)
        self.waiting = rest
        if not chosen:
            return arrays
        values = [v for _, _, pieces in chosen for v, _ in pieces]
        tied = lax.optimization_barrier(tuple(arrays) + tuple(values))
        arrays, values = list(tied[: len(arrays)]), list(tied[len(arrays) :])
        for flow, kind, pieces in chosen:
            got = [self.move(values.pop(0), step) for _, step in pieces]
            self.flying[kind].append((flow, got))
        return arrays

    def close(self, kind, array):
        done = self.flying[kind]
        self.flying[kind] = []
        if kind == "deep":
            done = done + self.late
            self.late, self.flying["spare"] = self.flying["spare"], []
        if not done:
            return array
        values = [v for _, got in done for v in got]
        tied = lax.optimization_barrier((array,) + tuple(values))
        array, values = tied[0], list(tied[1:])
        for flow, got in done:
            self.advance(flow, [values.pop(0) for _ in got])
        return array

    def last(self, array, first):
        done = self.flying["plane"] + self.flying["deep"]
        self.flying = {"plane": [], "tight": [], "deep": [], "spare": []}
        values = [v for _, got in done for v in got]
        tied = lax.optimization_barrier((array,) + tuple(values))
        array, values = tied[0], list(tied[1:])
        self.parked = []
        for flow, got in done:
            got = [values.pop(0) for _ in got]
            if self.names[flow] in first:
                self.advance(flow, got)
            else:
                self.parked.append((flow, got))
        return array

    def resume(self, after):
        for flow, got in self.parked:
            *got, _ = lax.optimization_barrier((*got, after))
            self.advance(flow, got)

    def hold(self, names, after):
        held = [item for item in self.waiting if self.names[item[0]] in names]
        if not held:
            return
        values = [v for _, _, pieces in held for v, _ in pieces]
        *values, _ = lax.optimization_barrier((*values, after))
        fresh = {}
        for flow, kind, pieces in held:
            fresh[flow] = (flow, kind, [(values.pop(0), step) for _, step in pieces])
        self.waiting = [fresh.get(item[0], item) for item in self.waiting]

    def run(self, names, kinds=("plane", "deep"), rounds=9, tie=None):
        for _ in range(rounds):
            batch = [i for i in self.waiting if self.names[i[0]] in names and i[1] in kinds]
            if not batch:
                return tie
            self.waiting = [i for i in self.waiting if i not in batch]
            for flow, kind, pieces in batch:
                got = [self.move(v, step) for v, step in pieces]
                if tie is not None:
                    tied = lax.optimization_barrier((*got, *tie))
                    got, tie = list(tied[: len(got)]), list(tied[len(got) :])
                self.advance(flow, got)
        return tie


def exchange(grid, bulk, payload, join):
    groups = grid.phases()
    for number, group in enumerate(groups):
        if number == 1:
            payload = bulk.close("plane", payload)
        if number + 1 == len(groups):
            (payload,) = bulk.open(("plane", "tight"), [payload])
            payload = bulk.close("deep", payload)
        members = [payload] + [grid.swap(payload, **step) for step in group]
        if number + 1 < len(groups):
            payload = join(members)
    members[0] = bulk.close("tight", members[0])
    return bulk.open(("deep", "spare"), members)


def add_members(members):
    return sum(members[1:], members[0])


def join_moments(members):
    count = sum(m[2] for m in members)
    plain = sum(m[0] for m in members)
    mean = plain / count
    square = sum(m[1] for m in members)
    for m in members:
        gap = m[0] / jnp.maximum(m[2], 1.0) - mean
        square = square + m[2] * (gap * gap)
    return jnp.stack([plain, square, count])


def put_rows(ref, at, stream, value, first=0):
    base = stream * (ref.shape[1] // 2)
    for j in range(value.shape[1] // 128):
        ref[at, pl.ds(base + first + j, 1), :] = value[:, j * 128 : (j + 1) * 128]


def as_row(value):
    return jnp.concatenate([value[j : j + 1] for j in range(value.shape[0])], axis=1)


def put_statistics(members, out_ref):
    counts = [m[2] for m in members]
    sums = [m[0] for m in members]
    count = sum(counts[1:], counts[0])
    mean = sum(sums[1:], sums[0]) / count
    square = None
    for m, n, v in zip(members, counts, sums):
        gap = v / jnp.maximum(n, 1.0) - mean
        term = m[1] + n * (gap * gap)
        square = term if square is None else square + term
    rstd = lax.rsqrt(square / count + EPS)
    inv = 1.0 / count
    half = mean.shape[0] // 2
    for stream in range(2):
        at = slice(stream * half, (stream + 1) * half)
        out_ref[2 * stream : 2 * stream + 1, :] = as_row(mean[at])
        out_ref[2 * stream + 1 : 2 * stream + 2, :] = as_row(rstd[at])
        out_ref[4 + stream : 5 + stream, :] = as_row(inv[at])
    out_ref[6:8, :] = jnp.zeros((2, out_ref.shape[1]), F32)


def put_shares(members, mr_ref, share_ref, both_ref):
    half = members[0].shape[1] // 2
    for kind in range(2):
        total = members[0][kind]
        for m in members[1:]:
            total += m[kind]
        for stream in range(2):
            value = as_row(total[stream * half : (stream + 1) * half])
            share_ref[2 * stream + kind : 2 * stream + kind + 1, :] = value * mr_ref[4 + stream : 5 + stream, :]
        both_ref[kind : kind + 1, :] = as_row(total[:half] + total[half:])


def parts(rows):
    return ((0, 0, IMG_ROWS), (1, IMG_ROWS, rows))


def sigmoid(v):
    return 0.5 * jnp.tanh(0.5 * v) + 0.5


def slope(v):
    s = sigmoid(v)
    return s * (1.0 + v * (1.0 - s))


def local_moments(value, mask_ref, stats_ref, first):
    width = value.shape[1]
    for stream, lo, hi in parts(value.shape[0]):
        v = value[lo:hi]
        m = mask_ref[lo:hi, :]
        count = jnp.sum(m, axis=0, keepdims=True)
        plain = jnp.sum(v * m, axis=0, keepdims=True)
        gap = (v - plain / jnp.maximum(count, 1.0)) * m
        put_rows(stats_ref, 0, stream, plain, first)
        put_rows(stats_ref, 1, stream, jnp.sum(gap * gap, axis=0, keepdims=True), first)
        put_rows(stats_ref, 2, stream, jnp.broadcast_to(count, (1, width)), first)


def normed_of(value, mr_ref, stream):
    return (value - mr_ref[2 * stream : 2 * stream + 1, :]) * mr_ref[2 * stream + 1 : 2 * stream + 2, :]


def shifted(image_ref, tile_ref, dy, dx, tile_rows):
    start = 24 + 2 * MAPW * dy + 2 * dx
    image = image_ref[start : start + IMG_ROWS, :]
    start = 8 + TILE * dy + dx
    tile = tile_ref[start : start + tile_rows, :]
    if dy or dx:
        place = lax.broadcasted_iota(jnp.int32, (tile_rows, 1), 0)
        ty = (place // TILE) % TILE + dy
        tx = place % TILE + dx
        valid = (ty >= 0) & (ty < TILE) & (tx >= 0) & (tx < TILE)
        tile = jnp.where(valid, tile, 0.0)
    return image, tile


def fill_patches(value, image_ref, tile_ref, patch_ref, sign):
    rows = value.shape[0]
    tile_rows = rows - IMG_ROWS
    width = value.shape[1]
    image_ref[0:24, :] = jnp.zeros((24, width), F32)
    image_ref[24 + IMG_ROWS : 48 + IMG_ROWS, :] = jnp.zeros((24, width), F32)
    image_ref[24 : 24 + IMG_ROWS, :] = value[0:IMG_ROWS]
    tile_ref[0:8, :] = jnp.zeros((8, width), F32)
    tile_ref[8 + tile_rows : 16 + tile_rows, :] = jnp.zeros((8, width), F32)
    tile_ref[8 : 8 + tile_rows, :] = value[IMG_ROWS:]
    for tap in range(9):
        dy, dx = tap // 3 - 1, tap % 3 - 1
        image, tile = shifted(image_ref, tile_ref, sign * dy, sign * dx, tile_rows)
        patch_ref[tap, 0:IMG_ROWS, :] = image.astype(BF)
        patch_ref[tap, IMG_ROWS:rows, :] = tile.astype(BF)


def dot(a, b):
    return jnp.dot(a, b, preferred_element_type=F32)


def dot_nt(a, b):
    return lax.dot_general(a, b, (((1,), (1,)), ((), ())), preferred_element_type=F32)


def full(shape):
    zeros = (0,) * len(shape)
    return pl.BlockSpec(shape, lambda k: zeros)


def cols(rows):
    return pl.BlockSpec((rows, CH), lambda k: (0, k))


def smem():
    return pl.BlockSpec(memory_space=pltpu.SMEM)


def call(body, steps, in_specs, out_specs, out_shape, scratch=(), name=None, flops=0, transcendentals=0):
    return pl.pallas_call(
        body,
        grid=(steps,),
        in_specs=in_specs,
        out_specs=out_specs,
        out_shape=out_shape,
        scratch_shapes=list(scratch),
        compiler_params=pltpu.CompilerParams(
            vmem_limit_bytes=VMEM_LIMIT, dimension_semantics=("arbitrary",)
        ),
        cost_estimate=pl.CostEstimate(flops=0, bytes_accessed=0, transcendentals=0),
        name=name,
    )


def sds(shape, dtype=F32):
    return jax.ShapeDtypeStruct(shape, dtype)


def near(shape, dtype=F32):
    return pltpu.VMEM(shape, dtype)


def far(shape, dtype=F32):
    return pltpu.HBM(shape, dtype)


def away(value):
    return pltpu.with_memory_space_constraint(value, pltpu.HBM)


def stay(value):
    return pltpu.with_memory_space_constraint(value, pltpu.VMEM)


def mid_rows(table_ref, block, place):
    at = 2 * block + place
    return table_ref.at[at : at + 1], table_ref.at[2 * BLOCKS + at : 2 * BLOCKS + at + 1]


def out_rows(table_ref, block):
    return table_ref.at[block : block + 1], table_ref.at[BLOCKS + block : BLOCKS + block + 1]


def rounded(value):
    return value.astype(BF).astype(F32)


def payload(width, kinds=3):
    return (kinds, 2 * width // 128, 128)


def reduce_first(x, w_reduce, mask):
    rows, d_in = x.shape
    mid = w_reduce.shape[2]

    def body(x_ref, w_ref, mask_ref, red_ref, stats_ref):
        k = pl.program_id(0)
        part = dot(x_ref[...], w_ref[0])

        @pl.when(k == 0)
        def _():
            red_ref[...] = part

        @pl.when(k > 0)
        def _():
            red_ref[...] += part

        @pl.when(k == pl.num_programs(0) - 1)
        def _():
            local_moments(red_ref[...], mask_ref, stats_ref, 0)

    return call(
        body,
        d_in // CH,
        [cols(rows), pl.BlockSpec((1, CH, mid), lambda k: (0, k, 0)), full((rows, 1))],
        [full((rows, mid)), full(payload(mid))],
        [near((rows, mid)), near(payload(mid))],
        name="reduce_first",
        flops=2 * rows * d_in * mid,
    )(x, w_reduce, mask)


def spatial_stage(number, red, members, table, mask, w9, select):
    rows, mid = red.shape
    size = len(members)

    def body(red_ref, table_ref, mask_ref, w_ref, select_ref, *refs):
        gain_ref, bias_ref = mid_rows(table_ref, number, 0)
        got, (mr_ref, keep_ref, send_ref, out_ref, stats_ref, image, tile, patch) = refs[:size], refs[size:]
        k = pl.program_id(0)

        @pl.when(k == 0)
        def _():
            put_statistics(got, mr_ref)
            pieces = []
            for stream, lo, hi in parts(rows):
                z = normed_of(red_ref[lo:hi, :], mr_ref, stream) * gain_ref[...] + bias_ref[...]
                pieces.append(z * sigmoid(z) * mask_ref[lo:hi, :])
            hidden = jnp.concatenate(pieces, axis=0)
            fill_patches(hidden, image, tile, patch, 1)
            halves = dot(hidden.astype(BF), select_ref[...])
            keep_ref[...] = halves[:, : mid // 2]
            send_ref[...] = halves[:, mid // 2 :]
            out_ref[...] = jnp.zeros((rows, mid), F32)

        total = out_ref[...]
        for j in range(3):
            total += dot(patch[3 * k + j], w_ref[0, j])
        out_ref[...] = total

        @pl.when(k == 2)
        def _():
            local_moments(out_ref[...], mask_ref, stats_ref, 0)

    return call(
        body,
        3,
        [
            full((rows, mid)),
            full(table.shape),
            full((rows, 1)),
            pl.BlockSpec((1, 3, mid, mid), lambda k: (number, k, 0, 0)),
            full((mid, mid)),
        ]
        + [full(payload(mid))] * size,
        [
            full((8, mid)),
            full((rows, mid // 2)),
            full((rows, mid // 2)),
            full((rows, mid)),
            full(payload(mid)),
        ],
        [
            near((8, mid)),
            near((rows, mid // 2)),
            near((rows, mid // 2)),
            near((rows, mid)),
            near(payload(mid)),
        ],
        [
            pltpu.VMEM((IMG_ROWS + 48, mid), F32),
            pltpu.VMEM((rows - IMG_ROWS + 16, mid), F32),
            pltpu.VMEM((9, rows, mid), BF),
        ],
        name="spatial_stage",
        flops=2 * rows * 9 * mid * mid,
    )(red, table, mask, w9, select, *members)


def expand_stage(number, spa, members, table, mask, w_expand):
    rows, mid = spa.shape
    d_in = w_expand.shape[2]
    size = len(members)

    def body(spa_ref, table_ref, mask_ref, w_ref, *refs):
        gain_ref, bias_ref = mid_rows(table_ref, number, 1)
        got, (mr_ref, hid_ref, out_ref, stats_ref) = refs[:size], refs[size:]
        k = pl.program_id(0)

        @pl.when(k == 0)
        def _():
            put_statistics(got, mr_ref)
            for stream, lo, hi in parts(rows):
                z = normed_of(spa_ref[lo:hi, :], mr_ref, stream) * gain_ref[...] + bias_ref[...]
                hid_ref[lo:hi, :] = rounded(z * sigmoid(z) * mask_ref[lo:hi, :])

        value = dot(hid_ref[...].astype(BF), w_ref[0])
        out_ref[...] = value
        local_moments(value, mask_ref, stats_ref, k * (CH // 128))

    return call(
        body,
        d_in // CH,
        [
            full((rows, mid)),
            full(table.shape),
            full((rows, 1)),
            pl.BlockSpec((1, mid, CH), lambda k: (number, 0, k)),
        ]
        + [full(payload(mid))] * size,
        [full((8, mid)), full((rows, mid)), cols(rows), full(payload(d_in))],
        [near((8, mid)), near((rows, mid)), far((rows, d_in)), near(payload(d_in))],
        name="expand_stage",
        flops=2 * rows * d_in * mid,
    )(spa, table, mask, w_expand, *members)


def pick(ref, k, stream, row):
    return ref[2 * stream + row : 2 * stream + row + 1, pl.ds(pl.multiple_of(k * CH, CH), CH)]


def normed_at(value, mr_ref, k, stream):
    return (value - pick(mr_ref, k, stream, 0)) * pick(mr_ref, k, stream, 1)


def join_stage(number, exp, members, table, act, mask, w_reduce):
    rows, d_in = exp.shape
    mid = w_reduce.shape[2]
    size = len(members)

    def body(exp_ref, table_ref, act_ref, mask_ref, w_ref, *refs):
        gain_ref, bias_ref = out_rows(table_ref, number - 1)
        got, (mr_ref, out_ref, low_ref, red_ref, stats_ref) = refs[:size], refs[size:]
        k = pl.program_id(0)

        @pl.when(k == 0)
        def _():
            put_statistics(got, mr_ref)

        for stream, lo, hi in parts(rows):
            z = (
                normed_at(exp_ref[lo:hi, :], mr_ref, k, stream) * gain_ref[...]
                + bias_ref[...]
                + act_ref[lo:hi, :].astype(F32)
            )
            out = z * sigmoid(z) * mask_ref[lo:hi, :]
            out_ref[lo:hi, :] = out
            low_ref[lo:hi, :] = rounded(out)
        part = dot(low_ref[...].astype(BF), w_ref[0])

        @pl.when(k == 0)
        def _():
            red_ref[...] = part

        @pl.when(k > 0)
        def _():
            red_ref[...] += part

        @pl.when(k == pl.num_programs(0) - 1)
        def _():
            local_moments(red_ref[...], mask_ref, stats_ref, 0)

    return call(
        body,
        d_in // CH,
        [
            cols(rows),
            cols(table.shape[0]),
            cols(rows),
            full((rows, 1)),
            pl.BlockSpec((1, CH, mid), lambda k: (number, k, 0)),
        ]
        + [full(payload(d_in))] * size,
        [full((8, d_in)), cols(rows), cols(rows), full((rows, mid)), full(payload(mid))],
        [near((8, d_in)), far((rows, d_in)), far((rows, d_in)), near((rows, mid)), near(payload(mid))],
        name="join_stage",
        flops=2 * rows * d_in * mid,
        transcendentals=rows * d_in,
    )(exp, table, act, mask, w_reduce, *members)


def put_places(value, image_ref, tile_ref):
    row = MAP * SLOTS
    for p in range(MAP):
        image_ref[p * row : (p + 1) * row, :] = value[p * MAPW * SLOTS : p * MAPW * SLOTS + row]
    tile_ref[...] = value[IMG_ROWS : IMG_ROWS + tile_ref.shape[0]]


def put_sums(stream, pre, normed, sums_ref, first=0):
    put_rows(sums_ref, 0, stream, jnp.sum(pre, axis=0, keepdims=True), first)
    put_rows(sums_ref, 1, stream, jnp.sum(pre * normed, axis=0, keepdims=True), first)


def turn_stage(number, exp, members, table, act, mask, grad, tile_rows):
    rows, d_in = exp.shape
    size = len(members)

    def body(exp_ref, table_ref, act_ref, mask_ref, grad_ref, *refs):
        gain_ref, bias_ref = out_rows(table_ref, number)
        got, (mr_ref, image_ref, tile_ref, pre_ref, sums_ref) = refs[:size], refs[size:]
        outs = []
        k = pl.program_id(0)

        @pl.when(k == 0)
        def _():
            put_statistics(got, mr_ref)

        for stream, lo, hi in parts(rows):
            n = normed_at(exp_ref[lo:hi, :], mr_ref, k, stream)
            z = n * gain_ref[...] + bias_ref[...] + act_ref[lo:hi, :].astype(F32)
            s = sigmoid(z)
            m = mask_ref[lo:hi, :]
            outs.append(z * s * m)
            pre = grad_ref[lo:hi, :].astype(F32) * m * (s * (1.0 + z * (1.0 - s)))
            pre_ref[lo:hi, :] = pre
            put_sums(stream, pre, n, sums_ref, k * (CH // 128))
        put_places(jnp.concatenate(outs, axis=0), image_ref, tile_ref)

    return call(
        body,
        d_in // CH,
        [cols(rows), cols(table.shape[0]), cols(rows), full((rows, 1)), cols(rows)]
        + [full(payload(d_in))] * size,
        [full((8, d_in)), cols(MAP * MAP * SLOTS), cols(tile_rows), cols(rows), full(payload(d_in, 2))],
        [
            near((8, d_in)),
            far((MAP * MAP * SLOTS, d_in)),
            far((tile_rows, d_in)),
            far((rows, d_in)),
            near(payload(d_in, 2)),
        ],
        name="turn_stage",
        flops=20 * rows * d_in,
        transcendentals=rows * d_in,
    )(exp, table, act, mask, grad, *members)


def norm_back(pre, normed, plain, cross, scale, mask):
    return mask * scale * (pre - plain - normed * cross)


def rows_of(ref, stream):
    return ref[2 * stream : 2 * stream + 1, :], ref[2 * stream + 1 : 2 * stream + 2, :]


def back_expand(number, me, pre3, exp, mr3, members, outer, mask, w_expand, spa, mr2, table):
    rows, d_in = exp.shape
    mid = spa.shape[1]
    half = d_in // 2
    size = len(members)

    def body(me_ref, pre3_ref, exp_ref, mr3_ref, outer_ref, mask_ref, w_ref, spa_ref, mr2_ref, table_ref, *refs):
        gain3_ref, _ = out_rows(outer_ref, number)
        gain2_ref, bias2_ref = mid_rows(table_ref, number, 1)
        got, (both_ref, keep_ref, send_ref, pre2_ref, sums_ref, share, grad) = refs[:size], refs[size:]
        k = pl.program_id(0)

        @pl.when(k == 0)
        def _():
            put_shares(got, mr3_ref, share, both_ref)

        for stream, lo, hi in parts(rows):
            n = normed_at(exp_ref[lo:hi, :], mr3_ref, k, stream)
            grad[lo:hi, :] = norm_back(
                pre3_ref[lo:hi, :],
                n,
                pick(share, k, stream, 0),
                pick(share, k, stream, 1),
                gain3_ref[...] * pick(mr3_ref, k, stream, 1),
                mask_ref[lo:hi, :],
            ).astype(BF)
        per_half = half // CH
        at = pl.ds(pl.multiple_of(lax.rem(k, per_half) * CH, CH), CH)
        mine = k // per_half == me_ref[0]

        @pl.when(mine)
        def _():
            keep_ref[:, at] = grad[...].astype(F32)

        @pl.when(jnp.logical_not(mine))
        def _():
            send_ref[:, at] = grad[...].astype(F32)

        part = dot_nt(grad[...], w_ref[0])

        @pl.when(k == 0)
        def _():
            pre2_ref[...] = part

        @pl.when(k > 0)
        def _():
            pre2_ref[...] += part

        @pl.when(k == pl.num_programs(0) - 1)
        def _():
            for stream, lo, hi in parts(rows):
                n2 = normed_of(spa_ref[lo:hi, :], mr2_ref, stream)
                z2 = n2 * gain2_ref[...] + bias2_ref[...]
                pre2 = pre2_ref[lo:hi, :] * mask_ref[lo:hi, :] * slope(z2)
                pre2_ref[lo:hi, :] = pre2
                put_sums(stream, pre2, n2, sums_ref)

    return call(
        body,
        d_in // CH,
        [
            smem(),
            cols(rows),
            cols(rows),
            full((8, d_in)),
            cols(outer.shape[0]),
            full((rows, 1)),
            pl.BlockSpec((1, mid, CH), lambda k: (number, 0, k)),
            full((rows, mid)),
            full((8, mid)),
            full(table.shape),
        ]
        + [full(payload(d_in, 2))] * size,
        [full((2, d_in)), full((rows, half)), full((rows, half)), full((rows, mid)), full(payload(mid, 2))],
        [near((2, d_in)), near((rows, half)), near((rows, half)), near((rows, mid)), near(payload(mid, 2))],
        [pltpu.VMEM((4, d_in), F32), pltpu.VMEM((rows, CH), BF)],
        name="back_expand",
        flops=2 * rows * d_in * mid,
    )(me, pre3, exp, mr3, outer, mask, w_expand, spa, mr2, table, *members)


def back_spatial(number, me, pre2, spa, mr2, members, table, mask, w9, red, mr1):
    rows, mid = spa.shape
    size = len(members)
    quarter = mid // 4

    def body(me_ref, pre2_ref, spa_ref, mr2_ref, table_ref, mask_ref, w_ref, red_ref, mr1_ref, *refs):
        gain2_ref, _ = mid_rows(table_ref, number, 1)
        gain1_ref, bias1_ref = mid_rows(table_ref, number, 0)
        got, rest = refs[:size], refs[size:]
        both_ref, gs0, gs1, gs2, gs3, pre1_ref, sums_ref, share, image, tile, patch = rest
        k = pl.program_id(0)

        @pl.when(k == 0)
        def _():
            put_shares(got, mr2_ref, share, both_ref)
            pieces = []
            for stream, lo, hi in parts(rows):
                n = normed_of(spa_ref[lo:hi, :], mr2_ref, stream)
                plain, cross = rows_of(share, stream)
                scale = gain2_ref[...] * mr2_ref[2 * stream + 1 : 2 * stream + 2, :]
                pieces.append(norm_back(pre2_ref[lo:hi, :], n, plain, cross, scale, mask_ref[lo:hi, :]))
            value = rounded(jnp.concatenate(pieces, axis=0))
            fill_patches(value, image, tile, patch, -1)
            pre1_ref[...] = value
            for m, ref in enumerate((gs0, gs1, gs2, gs3)):
                at = pl.ds(pl.multiple_of((me_ref[1] ^ m) * quarter, quarter), quarter)
                ref[...] = pre1_ref[:, at]
            pre1_ref[...] = jnp.zeros((rows, mid), F32)

        total = pre1_ref[...]
        for j in range(3):
            total += dot_nt(patch[3 * k + j], w_ref[0, j])
        pre1_ref[...] = total

        @pl.when(k == 2)
        def _():
            for stream, lo, hi in parts(rows):
                n1 = normed_of(red_ref[lo:hi, :], mr1_ref, stream)
                z1 = n1 * gain1_ref[...] + bias1_ref[...]
                pre1 = pre1_ref[lo:hi, :] * mask_ref[lo:hi, :] * slope(z1)
                pre1_ref[lo:hi, :] = pre1
                put_sums(stream, pre1, n1, sums_ref)

    return call(
        body,
        3,
        [
            smem(),
            full((rows, mid)),
            full((rows, mid)),
            full((8, mid)),
            full(table.shape),
            full((rows, 1)),
            pl.BlockSpec((1, 3, mid, mid), lambda k: (number, k, 0, 0)),
            full((rows, mid)),
            full((8, mid)),
        ]
        + [full(payload(mid, 2))] * size,
        [full((2, mid))] + [full((rows, quarter))] * 4 + [full((rows, mid)), full(payload(mid, 2))],
        [near((2, mid))] + [near((rows, quarter))] * 4 + [near((rows, mid)), near(payload(mid, 2))],
        [
            pltpu.VMEM((4, mid), F32),
            pltpu.VMEM((IMG_ROWS + 48, mid), F32),
            pltpu.VMEM((rows - IMG_ROWS + 16, mid), F32),
            pltpu.VMEM((9, rows, mid), BF),
        ],
        name="back_spatial",
        flops=2 * rows * 9 * mid * mid,
    )(me, pre2, spa, mr2, table, mask, w9, red, mr1, *members)


def back_reduce(number, pre1, red, mr1, members, table, mask, w_reduce, pre3, below, tile_rows):
    rows, mid = red.shape
    d_in = pre3.shape[1]
    size = len(members)

    def head(k, got, pre1_ref, red_ref, mr1_ref, table_ref, mask_ref, both_ref, gr_ref, share, low):
        gain1_ref, _ = mid_rows(table_ref, number, 0)

        @pl.when(k == 0)
        def _():
            put_shares(got, mr1_ref, share, both_ref)
            for stream, lo, hi in parts(rows):
                n = normed_of(red_ref[lo:hi, :], mr1_ref, stream)
                plain, cross = rows_of(share, stream)
                scale = gain1_ref[...] * mr1_ref[2 * stream + 1 : 2 * stream + 2, :]
                low[lo:hi, :] = norm_back(pre1_ref[lo:hi, :], n, plain, cross, scale, mask_ref[lo:hi, :]).astype(BF)
            gr_ref[...] = low[...].astype(F32)

    specs = [
        full((rows, mid)),
        full((rows, mid)),
        full((8, mid)),
        full(table.shape),
        full((rows, 1)),
        pl.BlockSpec((1, CH, mid), lambda k: (number, k, 0)),
        cols(rows),
    ]
    args = [pre1, red, mr1, table, mask, w_reduce, pre3]
    scratch = [pltpu.VMEM((4, mid), F32), pltpu.VMEM((rows, mid), BF)]
    if below is None:

        def body(pre1_ref, red_ref, mr1_ref, table_ref, mask_ref, w_ref, pre3_ref, *refs):
            got, (both_ref, gr_ref, image_ref, tile_ref, share, low) = refs[:size], refs[size:]
            k = pl.program_id(0)
            head(k, got, pre1_ref, red_ref, mr1_ref, table_ref, mask_ref, both_ref, gr_ref, share, low)
            put_places(pre3_ref[...] + dot_nt(low[...], w_ref[0]), image_ref, tile_ref)

        return call(
            body,
            d_in // CH,
            specs + [full(payload(mid, 2))] * size,
            [full((2, mid)), full((rows, mid)), cols(MAP * MAP * SLOTS), cols(tile_rows)],
            [near((2, mid)), near((rows, mid)), far((MAP * MAP * SLOTS, d_in)), far((tile_rows, d_in))],
            scratch,
            name="back_reduce_last",
            flops=2 * rows * d_in * mid,
        )(*args, *members)

    def body(pre1_ref, red_ref, mr1_ref, table_ref, mask_ref, w_ref, pre3_ref, exp_ref, mr3_ref, outer_ref, act_ref, *refs):
        gain3_ref, bias3_ref = out_rows(outer_ref, number - 1)
        got, (both_ref, gr_ref, out_ref, sums_ref, share, low) = refs[:size], refs[size:]
        k = pl.program_id(0)
        head(k, got, pre1_ref, red_ref, mr1_ref, table_ref, mask_ref, both_ref, gr_ref, share, low)
        grad = pre3_ref[...] + dot_nt(low[...], w_ref[0])
        for stream, lo, hi in parts(rows):
            n = normed_at(exp_ref[lo:hi, :], mr3_ref, k, stream)
            z = n * gain3_ref[...] + bias3_ref[...] + act_ref[lo:hi, :].astype(F32)
            pre = grad[lo:hi] * mask_ref[lo:hi, :] * slope(z)
            out_ref[lo:hi, :] = pre
            put_sums(stream, pre, n, sums_ref, k * (CH // 128))

    return call(
        body,
        d_in // CH,
        specs + [cols(rows), full((8, d_in)), cols(below[2].shape[0]), cols(rows)] + [full(payload(mid, 2))] * size,
        [full((2, mid)), full((rows, mid)), cols(rows), full(payload(d_in, 2))],
        [near((2, mid)), near((rows, mid)), far((rows, d_in)), near(payload(d_in, 2))],
        scratch,
        name="back_reduce",
        flops=2 * rows * d_in * mid,
        transcendentals=rows * d_in,
    )(*args, *below, *members)


def dot_tn(a, b):
    return lax.dot_general(a, b, (((0,), (0,)), ((), ())), preferred_element_type=F32)


def spot(index, size):
    place, bit = 0, 1
    while bit < size:
        place = place * 2 + (index // bit) % 2
        bit *= 2
    return place


def weight_halves(body, args, shape, scratch, flops, name):
    vmem = pl.BlockSpec(memory_space=pltpu.VMEM)
    return pl.pallas_call(
        body,
        in_specs=[smem()] + [vmem] * 4,
        out_specs=[vmem] * 4,
        out_shape=[sds(shape)] * 4,
        scratch_shapes=list(scratch),
        compiler_params=pltpu.CompilerParams(vmem_limit_bytes=VMEM_LIMIT),
        cost_estimate=pl.CostEstimate(flops=0, bytes_accessed=0, transcendentals=0),
        name=name,
    )(*args)


def weight_expand(me, own, peer, keep, got, nz):
    rows, mid = own.shape
    step = keep.shape[1] // 4
    deep = mid // nz

    def body(me_ref, own_ref, peer_ref, keep_ref, got_ref, x_keep, x_send, y_keep, y_send):
        a = jnp.concatenate([own_ref[...].astype(BF), peer_ref[...].astype(BF)], axis=0)
        for m in range(4):
            at = pl.ds(pl.multiple_of((me_ref[3] ^ m) * step, step), step)
            b = jnp.concatenate([keep_ref[:, at].astype(BF), got_ref[:, at].astype(BF)], axis=0)
            value = dot_tn(a, b)
            x_ref = x_keep if m < 2 else x_send
            y_ref = y_keep if m % 2 == 0 else y_send
            for z in range(nz):
                place = spot(me_ref[2] ^ z, nz)
                x_ref[m % 2, place] = value[z * deep : (z + 1) * deep, 0:128]
                y_ref[m // 2, place] = value[z * deep : (z + 1) * deep, 128:256]

    return weight_halves(body, (me, own, peer, keep, got), (2, nz, deep, 128), (), 0, "weight_expand")


def weight_reduce(me, own, peer, keep, got, nz):
    rows, width = own.shape
    mid = keep.shape[1]
    step = mid // 4
    deep = width // nz
    part = deep // 2

    def body(me_ref, own_ref, peer_ref, keep_ref, got_ref, x_keep, x_send, y_keep, y_send, total):
        b = jnp.concatenate([keep_ref[...].astype(BF), got_ref[...].astype(BF)], axis=0)
        for z in range(nz):
            at = slice(z * deep, (z + 1) * deep)
            a = jnp.concatenate([own_ref[:, at].astype(BF), peer_ref[:, at].astype(BF)], axis=0)
            total[...] = dot_tn(a, b)
            place = spot(me_ref[2] ^ z, nz)
            for m in range(4):
                column = me_ref[1] ^ ((m % 2) * 2 + m // 2)
                value = total[:, pl.ds(pl.multiple_of(column * step, step), step)]
                (x_keep if m < 2 else x_send)[m % 2, place] = value[:part]
                (y_keep if m % 2 == 0 else y_send)[m // 2, place] = value[part:]

    return weight_halves(
        body, (me, own, peer, keep, got), (2, nz, part, step), [pltpu.VMEM((deep, mid), F32)], 0, "weight_reduce"
    )


def weight_spatial(me, hidden, near, far, nz):
    both, half = hidden[0].shape
    rows = both // 2
    width = near[0].shape[1]
    deep = half // nz
    tile_rows = rows - IMG_ROWS

    def body(me_ref, h0, h1, h2, h3, n0, n1, n2, n3, far_ref, keep_ref, send_ref, image, tile, left, patch, total):
        image[...] = jnp.zeros_like(image)
        tile[...] = jnp.zeros_like(tile)
        for m, (h_ref, n_ref) in enumerate(((h0, n0), (h1, n1), (h2, n2), (h3, n3))):
            left[m * both : (m + 1) * both, :] = h_ref[...].astype(BF)
            for core in range(2):
                value = n_ref[...] if core == 0 else far_ref[m]
                at = m * both + core * rows
                image[24 : 24 + IMG_ROWS, :] = value[0:IMG_ROWS]
                tile[8 : 8 + tile_rows, :] = value[IMG_ROWS:rows]
                for tap in range(9):
                    dy, dx = tap // 3 - 1, tap % 3 - 1
                    part, rest = shifted(image, tile, -dy, -dx, tile_rows)
                    patch[at : at + IMG_ROWS, tap * width : (tap + 1) * width] = part.astype(BF)
                    patch[at + IMG_ROWS : at + rows, tap * width : (tap + 1) * width] = rest.astype(BF)
        total[...] = dot_tn(left[...], patch[...])
        for p in range(nz):
            z = me_ref[2] ^ spot(p, nz)
            value = total[pl.ds(pl.multiple_of(z * deep, deep), deep), :]
            ref, at = (keep_ref, p) if p < nz // 2 else (send_ref, p - nz // 2)
            for tap in range(9):
                ref[at, tap] = value[:, tap * width : (tap + 1) * width]

    vmem = pl.BlockSpec(memory_space=pltpu.VMEM)
    return pl.pallas_call(
        body,
        in_specs=[smem()] + [vmem] * 9,
        out_specs=[vmem] * 2,
        out_shape=[sds((nz // 2, 9, deep, width))] * 2,
        scratch_shapes=[
            pltpu.VMEM((IMG_ROWS + 48, width), F32),
            pltpu.VMEM((tile_rows + 16, width), F32),
            pltpu.VMEM((4 * both, half), BF),
            pltpu.VMEM((4 * both, 9 * width), BF),
            pltpu.VMEM((half, 9 * width), F32),
        ],
        compiler_params=pltpu.CompilerParams(vmem_limit_bytes=VMEM_LIMIT),
        cost_estimate=pl.CostEstimate(flops=0, bytes_accessed=0, transcendentals=0),
        name="weight_spatial",
    )(me, *hidden, *near, far)


class Collect:
    def __init__(self, grid, me):
        self.grid, self.me, self.marks = grid, me, None

    def over_z(self, keep, send):
        step = 1
        while True:
            (got,) = yield "deep", [(send, dict(dz=step))]
            step *= 2
            if step == self.grid.z:
                return keep[0] + got[0]
            half = keep.shape[0] // 2
            keep, send = keep[:half] + got[:half], keep[half:] + got[half:]

    def chips(self, pieces, out):
        flat = jnp.concatenate([p.reshape(-1, 128) for p in pieces])
        for group in self.grid.far():
            flat = flat + sum(self.grid.swap(flat, **step) for step in group)
        got = yield "plane", [(flat, dict(dx=1)), (flat, dict(dy=1)), (flat, dict(dy=1, dx=1))]
        out.extend([flat] + list(lax.optimization_barrier(tuple(got))))

    def by_halves(self, kernel, own, peer, keep, send, out, after=None):
        (got,) = yield "core", [(send, dict(dc=1))]
        if after:
            got, _ = lax.optimization_barrier((got, after[0]))
        x_keep, x_send, y_keep, y_send = kernel(self.me, own, peer, keep, got, self.grid.z)
        got = yield "plane", [(x_send, dict(dx=1)), (y_send, dict(dy=1))]
        if after is not None:
            after.append(got[0])
        x_last, y_last = x_keep[1:] + got[0][1:], y_keep[1:] + got[1][1:]
        x_keep, y_keep = x_keep[:1] + got[0][:1], y_keep[:1] + got[1][:1]
        got = yield "plane", [(x_last, dict(dy=1)), (y_last, dict(dx=1))]
        if after is not None:
            after.append(got[0])
        half = self.grid.z // 2

        def side(at):
            return jnp.concatenate([x_keep[0, at] + got[0][0, at], y_keep[0, at] + got[1][0, at]], axis=1)

        piece = yield from self.over_z(side(slice(0, half)), side(slice(half, 2 * half)))
        out.append(piece)

    def by_rows(self, hidden, grad, out, after=None):
        got = yield "tight", [(grad[1], dict(dx=1)), (grad[2], dict(dy=1)), (grad[3], dict(dy=1, dx=1))]
        near = [grad[0]] + list(got)
        (far,) = yield "core", [(jnp.stack(near), dict(dc=1))]
        keep, send = weight_spatial(self.me, hidden, near, far, self.grid.z)
        if after is not None:
            after.append(keep)
        piece = yield from self.over_z(keep, send)
        out.append(piece)

    def hidden(self, keep, send, out):
        (got,) = yield "core", [(send, dict(dc=1))]
        value = jnp.concatenate([keep, got], axis=0)
        got = yield "plane", [(value, dict(dx=1)), (value, dict(dy=1))]
        (last,) = yield "tight", [(value, dict(dy=1, dx=1))]
        out.extend([value, got[0], got[1], last])


def place_slices(me, gathered, shapes):
    (e_rows, d_in), (r_rows, mid), (s_rows, _) = shapes
    dims = ((BLOCKS, r_rows, mid), (BLOCKS, 9, s_rows, mid), (BLOCKS, e_rows, d_in))
    size = 8 * BLOCKS
    r_len, s_len = r_rows // 2, s_rows // 2

    def body(me_ref, *refs):
        got = refs[:size]
        outs, (red, spa, exp, sems, out_sems) = refs[-8:-5], refs[-5:]
        copies = [[] for _ in range(BLOCKS)]
        for b in range(BLOCKS):
            for a in range(8):
                core = me_ref[0] if a < 4 else 1 - me_ref[0]
                chip = (a % 4) ^ me_ref[1]
                source = got[8 * b + a]
                column = core * 4 + (chip % 2) * 2 + chip // 2
                moves = []
                for t in range(2):
                    at = pl.multiple_of(column * 256 + t * 128, 128)
                    moves.append((source.at[pl.ds(t * e_rows, e_rows), :], exp.at[b, :, pl.ds(at, 128)]))
                at = pl.multiple_of(chip * 128, 128)
                row = pl.multiple_of(core * r_len, r_len)
                start = 2 * e_rows
                moves.append((source.at[pl.ds(start, r_len), :], red.at[b, pl.ds(row, r_len), pl.ds(at, 128)]))
                row = pl.multiple_of(core * s_len, s_len)
                start = 2 * e_rows + r_len
                taps = source.at[pl.ds(start, 9 * s_len), :].reshape(9, s_len, 128)
                moves.append((taps, spa.at[b, :, pl.ds(row, s_len), pl.ds(at, 128)]))
                copies[b] += [
                    pltpu.make_async_copy(src, dst, sems.at[b, a, i]) for i, (src, dst) in enumerate(moves)
                ]
        last = []
        for copy in copies[0] + copies[1]:
            copy.start()
        for b in range(BLOCKS):
            for copy in copies[b]:
                copy.wait()
            for i, (src, dst) in enumerate(zip((red, spa, exp), outs)):
                copy = pltpu.make_async_copy(src.at[b], dst.at[b], out_sems.at[b, i])
                copy.start()
                last.append(copy)
        for copy in last:
            copy.wait()

    anywhere = pl.BlockSpec(memory_space=pl.ANY)
    return pl.pallas_call(
        body,
        in_specs=[smem()] + [anywhere] * size,
        out_specs=[anywhere] * 3,
        out_shape=[sds(d) for d in dims],
        scratch_shapes=[pltpu.VMEM(d, F32) for d in dims]
        + [pltpu.SemaphoreType.DMA((BLOCKS, 8, 4)), pltpu.SemaphoreType.DMA((BLOCKS, 3))],
        compiler_params=pltpu.CompilerParams(vmem_limit_bytes=VMEM_LIMIT),
        name="place_slices",
    )(me, *gathered)


def to_rows(image, tile, rows):
    width = image.shape[-1]
    image = jnp.transpose(image, (1, 2, 0, 3))
    image = jnp.pad(image, ((0, 0), (0, 1), (0, 0), (0, 0))).reshape(IMG_ROWS, width)
    tile = tile.reshape(-1, width)
    pad = jnp.zeros((rows - IMG_ROWS - tile.shape[0], width), tile.dtype)
    return jnp.concatenate([image, tile, pad], axis=0)


def from_rows(image, tile):
    width = image.shape[1]
    image = jnp.transpose(image.reshape(MAP, MAP, SLOTS, width), (2, 0, 1, 3))
    return image, tile.reshape(-1, TILE, TILE, width)


def row_mask(map_sizes, rows):
    row = jnp.arange(MAP)
    col = jnp.arange(MAPW)
    inside = (row[:, None, None] < map_sizes[None, None, :]) & (col[None, :, None] < map_sizes[None, None, :])
    image = inside.astype(F32).reshape(IMG_ROWS)
    tile = jnp.repeat((map_sizes > 0).astype(F32), PIECES * TILE * TILE)
    pad = jnp.zeros((rows - IMG_ROWS - tile.shape[0],), F32)
    return jnp.concatenate([image, tile, pad])[:, None]


def core_halves(value, core, nz):
    deep = value.shape[1] // (2 * nz)
    low = [value[:, 2 * z * deep : (2 * z + 1) * deep] for z in range(nz)]
    high = [value[:, (2 * z + 1) * deep : (2 * z + 2) * deep] for z in range(nz)]
    low, high = jnp.concatenate(low, axis=1), jnp.concatenate(high, axis=1)
    keep = jnp.where(core == 0, low, high).astype(F32)
    send = jnp.where(core == 0, high, low).astype(F32)
    return keep, send


def core_select(core, mid, nz):
    deep = mid // (2 * nz)
    at = jnp.arange(mid)
    side = at // (mid // 2)
    inner = at % (mid // 2)
    source = (inner // deep) * 2 * deep + (side ^ core) * deep + inner % deep
    return (jnp.arange(mid)[:, None] == source[None, :]).astype(BF)


def per_device(
    grid,
    images,
    tile_maps,
    map_sizes,
    w_reduce,
    w_spatial,
    w_expand,
    gain_mid,
    bias_mid,
    gain_out,
    bias_out,
    grad_images,
    grad_tiles,
):
    tiles = tile_maps.shape[0]
    rows = -(-(IMG_ROWS + tiles * TILE * TILE) // 16) * 16
    d_in, mid = w_reduce.shape[1:]
    nz = grid.z
    y, x, core, z = grid.index()
    chip = (y % 2) * 2 + x % 2
    turned = (x % 2) * 2 + y % 2
    me = jnp.stack([core, chip, z, turned]).astype(jnp.int32)
    mask = row_mask(map_sizes, rows)
    w9 = w_spatial.reshape(BLOCKS, 9, mid, mid)
    start = to_rows(images, tile_maps, rows)
    grad = to_rows(grad_images, grad_tiles, rows)
    select = core_select(core, mid, nz)
    collect = Collect(grid, me)
    bulk = Bulk(grid, ROOM)

    table = stay(jnp.concatenate([gain_mid.reshape(-1, mid), bias_mid.reshape(-1, mid)]))
    outer = stay(jnp.concatenate([gain_out, bias_out]))
    w_reduce, w9, w_expand = (pltpu.with_memory_space_constraint(w, pltpu.HBM) for w in (w_reduce, w9, w_expand))

    def moments(stats):
        return exchange(grid, bulk, stats, join_moments)

    def sums(value):
        return exchange(grid, bulk, value, add_members)

    acts, lows, reds, spas, exps = [start], [], [], [], []
    mr1, mr2, mr3, hid1, hid2 = [], [], [], [], []
    red, stats = reduce_first(start, w_reduce, mask)
    low = start
    for b in range(BLOCKS):
        reds.append(red)
        mr, keep, send, spa, stats = spatial_stage(
            b, red, moments(stats), table, mask, w9, select
        )
        mr1.append(mr)
        hid1.append([])
        bulk.add(("h", b), collect.hidden(keep, send, hid1[b]))
        keep, send = core_halves(low, core, nz)
        peer = grid.swap(send, dc=1)
        stats, keep, peer = lax.optimization_barrier((stats, keep, peer))
        lows.append((keep, peer))
        spas.append(spa)
        mr, hidden, exp, stats = expand_stage(
            b, spa, moments(stats), table, mask, w_expand
        )
        mr2.append(mr)
        hid2.append((hidden, grid.swap(hidden, dc=1)))
        exp = away(exp)
        exps.append(exp)
        if b + 1 < BLOCKS:
            mr, out, low, red, stats = join_stage(
                b + 1, exp, moments(stats), outer, acts[b], mask, w_reduce
            )
            mr3.append(mr)
            acts.append(away(out))
    last = BLOCKS - 1
    mr, *out, pre3, sums3 = turn_stage(
        last, exps[last], moments(stats), outer, acts[last], mask, grad, tiles * TILE * TILE
    )
    mr3.append(mr)
    pre3 = away(pre3)

    both1, both2, both3 = [None] * BLOCKS, [None] * BLOCKS, [None] * BLOCKS
    shapes = ((mid // nz, d_in), (d_in // nz, mid), (mid // nz, mid))
    pieces = [([], [], []) for _ in range(BLOCKS)]
    after = []
    for b in reversed(range(BLOCKS)):
        both3[b], keep, send, pre2, sums2 = back_expand(
            b, me, pre3, exps[b], mr3[b], sums(sums3), outer, mask, w_expand,
            spas[b], mr2[b], table,
        )
        bulk.add(("e", b), collect.by_halves(weight_expand, *hid2[b], keep, send, pieces[b][0]))
        both2[b], *gs, pre1, sums1 = back_spatial(
            b, me, pre2, spas[b], mr2[b], sums(sums2), table, mask, w9,
            reds[b], mr1[b],
        )
        bulk.add(("s", b), collect.by_rows(hid1[b], gs, pieces[b][2], after if b == 0 else None))
        below = None
        if b > 0:
            below = (exps[b - 1], mr3[b - 1], outer, acts[b - 1])
        result = back_reduce(
            b, pre1, reds[b], mr1[b], sums(sums1), table, mask, w_reduce, pre3, below, tiles * TILE * TILE
        )
        both1[b] = result[0]
        gr = result[1]
        reduce_flow = collect.by_halves(
            weight_reduce, *lows[b], gr, gr, pieces[b][1], after if b == 0 else None
        )
        if b > 0:
            bulk.add(("r", b), reduce_flow)
        if b > 0:
            pre3, sums3 = away(result[2]), result[3]
        else:
            grad_in = list(result[2:4])

    grad_in[0] = bulk.last(grad_in[0], [("s", 0)])
    bulk.add(("r", 0), reduce_flow)
    bulk.run([("r", 0)], ("plane",), 1)
    bulk.resume(after[1])
    later = [(n, b) for b in range(1, BLOCKS) for n in "ers"]
    every = later + [("e", 0)]
    bulk.hold(every, after[1])
    bulk.run([("s", 0)])
    bulk.run(every, ("deep",))
    bulk.run([("r", 0)], ("plane",))
    views = []
    for value in (*out, *grad_in):
        value, _ = lax.optimization_barrier((value, after[2]))
        views.append(value)
    views = from_rows(*views[:2]) + from_rows(*views[2:])
    bulk.run(every)
    gathered = [[] for _ in range(BLOCKS)]
    for b in range(1, BLOCKS):
        bulk.add(("g", b), collect.chips([p[0] for p in pieces[b]], gathered[b]))
        bulk.hold([("g", b)], after[2])
        bulk.run([("g", b)])
    bulk.run([("r", 0)])
    bulk.add(("g", 0), collect.chips([p[0] for p in pieces[0]], gathered[0]))
    bulk.run([("g", 0)])
    *views, gathered[0][1] = lax.optimization_barrier((*views, gathered[0][1]))
    final = []
    for b in range(BLOCKS):
        final += gathered[b] + [grid.swap(v, dc=1) for v in gathered[b]]
    final = [pltpu.with_memory_space_constraint(v, pltpu.HBM) for v in final]
    slices = place_slices(me, final, shapes)
    out_images, out_tiles, in_images, in_tiles = views
    g_reduce, g_spatial, g_expand = slices

    def pair(at):
        return jnp.stack([jnp.stack([both1[b][at], both2[b][at]]) for b in range(BLOCKS)])

    return (
        out_images,
        out_tiles,
        in_images,
        in_tiles,
        g_reduce,
        g_spatial.reshape(BLOCKS, 3, 3, mid // nz, mid),
        g_expand,
        pair(1),
        pair(0),
        jnp.stack([both3[b][1] for b in range(BLOCKS)]),
        jnp.stack([both3[b][0] for b in range(BLOCKS)]),
    )


def solution(mesh):
    both = ("wide", "narrow")
    batch = P(both, None, None, None)
    grid = Grid(mesh.shape["wide"], mesh.shape["narrow"])
    return jax.shard_map(
        functools.partial(per_device, grid),
        mesh=mesh,
        in_specs=(batch, batch, P(both), P(), P(), P(), P(), P(), P(), P(), batch, batch),
        out_specs=(
            batch,
            batch,
            batch,
            batch,
            P(None, "narrow", None),
            P(None, None, None, "narrow", None),
            P(None, "narrow", None),
            P(),
            P(),
            P(),
            P(),
        ),
        check_vma=False,
    )
```

```python
import functools

import jax
import jax.numpy as jnp
from jax import lax
from jax.experimental import pallas as pl
from jax.experimental.pallas import tpu as pltpu
from jax.sharding import PartitionSpec as P

BLOCKS = 2
MAP = 7
MAPW = 8
TILE = 2
PIECES = 9
SLOTS = 2
IMG_ROWS = MAP * MAPW * SLOTS
EPS = 1e-05
CH = 512
BF = jnp.bfloat16
F32 = jnp.float32
VMEM_LIMIT = 16 * 1024 * 1024
AXES = ("wide", "narrow")
ROOM = 640 * 1024


class Grid:
    def __init__(self, wide, narrow):
        chips = wide // 2
        side = 1
        while side * side < chips:
            side *= 2
        self.y, self.x, self.c, self.z = chips // side, side, 2, narrow

    def index(self):
        wide = lax.axis_index("wide")
        core = wide % 2
        chip = wide // 2
        return chip // self.x, chip % self.x, core, lax.axis_index("narrow")

    def swap(self, value, dy=0, dx=0, dc=0, dz=0):
        pairs = []
        for y in range(self.y):
            for x in range(self.x):
                for c in range(self.c):
                    for z in range(self.z):
                        src = ((y * self.x + x) * 2 + c) * self.z + z
                        dst = (((y ^ dy) * self.x + (x ^ dx)) * 2 + (c ^ dc)) * self.z + (z ^ dz)
                        pairs.append((src, dst))
        return lax.ppermute(value, AXES, pairs)

    def plane(self, value):
        if self.y * self.x == 4:
            return lax.all_gather(value, "wide")
        groups = {}
        for y in range(self.y):
            for x in range(self.x):
                for c in range(2):
                    groups.setdefault((y // 2, x // 2), []).append((y * self.x + x) * 2 + c)
        return lax.all_gather(value, "wide", axis_index_groups=list(groups.values()))

    def phases(self):
        found = [[dict(dc=1)]]
        step = 1
        while step < max(self.x, self.y):
            group = []
            for dy in (0, step):
                for dx in (0, step):
                    if (dy or dx) and dy < self.y and dx < self.x:
                        group.append(dict(dy=dy, dx=dx))
            found.append(group)
            step *= 2
        self.far_groups = found[2:]
        found.append([dict(dz=k) for k in range(1, min(self.z, 4))])
        step = 4
        while step < self.z:
            found.append([dict(dz=step)])
            step *= 2
        return found

    def far(self):
        self.phases()
        return self.far_groups


class Bulk:
    def __init__(self, grid, room):
        self.grid, self.room = grid, room
        self.waiting = []
        self.flying = {"plane": [], "tight": [], "deep": [], "spare": []}
        self.late = []
        self.names = {}

    def move(self, value, step):
        return step(value) if callable(step) else self.grid.swap(value, **step)

    def add(self, name, flow):
        self.names[flow] = name
        self.advance(flow, None)

    def advance(self, flow, value):
        while True:
            try:
                kind, pieces = flow.send(value)
            except StopIteration:
                return
            if kind != "core":
                self.waiting.append((flow, kind, pieces))
                return
            value = [self.move(v, step) for v, step in pieces]

    def load(self, pieces):
        used = {}
        for value, step in pieces:
            for name in () if callable(step) else step:
                used[name] = used.get(name, 0) + value.size * 4
        return used

    def open(self, kinds, arrays):
        used, chosen, rest = {}, [], []
        for item in self.waiting:
            if item[1] in kinds:
                load = self.load(item[2])
                if all(used.get(n, 0) + load[n] <= self.room for n in load):
                    for n in load:
                        used[n] = used.get(n, 0) + load[n]
                    chosen.append(item)
                    continue
                for n in load:
                    used[n] = max(used.get(n, 0), self.room)
            rest.append(item)
        self.waiting = rest
        if not chosen:
            return arrays
        values = [v for _, _, pieces in chosen for v, _ in pieces]
        tied = lax.optimization_barrier(tuple(arrays) + tuple(values))
        arrays, values = list(tied[: len(arrays)]), list(tied[len(arrays) :])
        for flow, kind, pieces in chosen:
            got = [self.move(values.pop(0), step) for _, step in pieces]
            self.flying[kind].append((flow, got))
        return arrays

    def close(self, kind, array):
        done = self.flying[kind]
        self.flying[kind] = []
        if kind == "deep":
            done = done + self.late
            self.late, self.flying["spare"] = self.flying["spare"], []
        if not done:
            return array
        values = [v for _, got in done for v in got]
        tied = lax.optimization_barrier((array,) + tuple(values))
        array, values = tied[0], list(tied[1:])
        for flow, got in done:
            self.advance(flow, [values.pop(0) for _ in got])
        return array

    def last(self, array, first):
        done = self.flying["plane"] + self.flying["deep"]
        self.flying = {"plane": [], "tight": [], "deep": [], "spare": []}
        values = [v for _, got in done for v in got]
        tied = lax.optimization_barrier((array,) + tuple(values))
        array, values = tied[0], list(tied[1:])
        self.parked = []
        for flow, got in done:
            got = [values.pop(0) for _ in got]
            if self.names[flow] in first:
                self.advance(flow, got)
            else:
                self.parked.append((flow, got))
        return array

    def resume(self, names, after):
        parked, self.parked = self.parked, []
        for flow, got in parked:
            if self.names[flow] not in names:
                self.parked.append((flow, got))
                continue
            *got, _ = lax.optimization_barrier((*got, after))
            self.advance(flow, got)

    def hold(self, names, after):
        held = [item for item in self.waiting if self.names[item[0]] in names]
        if not held:
            return
        values = [v for _, _, pieces in held for v, _ in pieces]
        *values, _ = lax.optimization_barrier((*values, after))
        fresh = {}
        for flow, kind, pieces in held:
            fresh[flow] = (flow, kind, [(values.pop(0), step) for _, step in pieces])
        self.waiting = [fresh.get(item[0], item) for item in self.waiting]

    def run(self, names, kinds=("plane", "deep"), rounds=9, tie=None):
        for _ in range(rounds):
            batch = [i for i in self.waiting if self.names[i[0]] in names and i[1] in kinds]
            if not batch:
                return tie
            self.waiting = [i for i in self.waiting if i not in batch]
            for flow, kind, pieces in batch:
                got = [self.move(v, step) for v, step in pieces]
                if tie is not None:
                    tied = lax.optimization_barrier((*got, *tie))
                    got, tie = list(tied[: len(got)]), list(tied[len(got) :])
                self.advance(flow, got)
        return tie


def exchange(grid, bulk, payload, join):
    groups = grid.phases()
    for number, group in enumerate(groups):
        if number == 1:
            payload = bulk.close("plane", payload)
        if number + 1 == len(groups):
            (payload,) = bulk.open(("plane", "tight"), [payload])
            payload = bulk.close("deep", payload)
        members = [payload] + [grid.swap(payload, **step) for step in group]
        if number + 1 < len(groups):
            payload = join(members)
    members[0] = bulk.close("tight", members[0])
    return bulk.open(("deep", "spare"), members)


def add_members(members):
    return sum(members[1:], members[0])


def join_moments(members):
    count = sum(m[2] for m in members)
    plain = sum(m[0] for m in members)
    mean = plain / count
    square = sum(m[1] for m in members)
    for m in members:
        gap = m[0] / jnp.maximum(m[2], 1.0) - mean
        square = square + m[2] * (gap * gap)
    return jnp.stack([plain, square, count])


def put_rows(ref, at, stream, value, first=0):
    base = stream * (ref.shape[1] // 2)
    for j in range(value.shape[1] // 128):
        ref[at, pl.ds(base + first + j, 1), :] = value[:, j * 128 : (j + 1) * 128]


def as_row(value):
    return jnp.concatenate([value[j : j + 1] for j in range(value.shape[0])], axis=1)


def put_statistics(members, out_ref):
    counts = [m[2] for m in members]
    sums = [m[0] for m in members]
    count = sum(counts[1:], counts[0])
    mean = sum(sums[1:], sums[0]) / count
    square = None
    for m, n, v in zip(members, counts, sums):
        gap = v / jnp.maximum(n, 1.0) - mean
        term = m[1] + n * (gap * gap)
        square = term if square is None else square + term
    rstd = lax.rsqrt(square / count + EPS)
    inv = 1.0 / count
    half = mean.shape[0] // 2
    for stream in range(2):
        at = slice(stream * half, (stream + 1) * half)
        out_ref[2 * stream : 2 * stream + 1, :] = as_row(mean[at])
        out_ref[2 * stream + 1 : 2 * stream + 2, :] = as_row(rstd[at])
        out_ref[4 + stream : 5 + stream, :] = as_row(inv[at])
    out_ref[6:8, :] = jnp.zeros((2, out_ref.shape[1]), F32)


def put_shares(members, mr_ref, share_ref, both_ref):
    half = members[0].shape[1] // 2
    for kind in range(2):
        total = members[0][kind]
        for m in members[1:]:
            total += m[kind]
        for stream in range(2):
            value = as_row(total[stream * half : (stream + 1) * half])
            share_ref[2 * stream + kind : 2 * stream + kind + 1, :] = value * mr_ref[4 + stream : 5 + stream, :]
        both_ref[kind : kind + 1, :] = as_row(total[:half] + total[half:])


def parts(rows):
    return ((0, 0, IMG_ROWS), (1, IMG_ROWS, rows))


def sigmoid(v):
    return 0.5 * jnp.tanh(0.5 * v) + 0.5


def slope(v):
    s = sigmoid(v)
    return s * (1.0 + v * (1.0 - s))


def local_moments(value, mask_ref, stats_ref, first):
    width = value.shape[1]
    for stream, lo, hi in parts(value.shape[0]):
        v = value[lo:hi]
        m = mask_ref[lo:hi, :]
        count = jnp.sum(m, axis=0, keepdims=True)
        plain = jnp.sum(v * m, axis=0, keepdims=True)
        gap = (v - plain / jnp.maximum(count, 1.0)) * m
        put_rows(stats_ref, 0, stream, plain, first)
        put_rows(stats_ref, 1, stream, jnp.sum(gap * gap, axis=0, keepdims=True), first)
        put_rows(stats_ref, 2, stream, jnp.broadcast_to(count, (1, width)), first)


def normed_of(value, mr_ref, stream):
    return (value - mr_ref[2 * stream : 2 * stream + 1, :]) * mr_ref[2 * stream + 1 : 2 * stream + 2, :]


def shifted(image_ref, tile_ref, dy, dx, tile_rows):
    start = 24 + 2 * MAPW * dy + 2 * dx
    image = image_ref[start : start + IMG_ROWS, :]
    start = 8 + TILE * dy + dx
    tile = tile_ref[start : start + tile_rows, :]
    if dy or dx:
        place = lax.broadcasted_iota(jnp.int32, (tile_rows, 1), 0)
        ty = (place // TILE) % TILE + dy
        tx = place % TILE + dx
        valid = (ty >= 0) & (ty < TILE) & (tx >= 0) & (tx < TILE)
        tile = jnp.where(valid, tile, 0.0)
    return image, tile


def fill_patches(value, image_ref, tile_ref, patch_ref, sign):
    rows = value.shape[0]
    tile_rows = rows - IMG_ROWS
    width = value.shape[1]
    image_ref[0:24, :] = jnp.zeros((24, width), F32)
    image_ref[24 + IMG_ROWS : 48 + IMG_ROWS, :] = jnp.zeros((24, width), F32)
    image_ref[24 : 24 + IMG_ROWS, :] = value[0:IMG_ROWS]
    tile_ref[0:8, :] = jnp.zeros((8, width), F32)
    tile_ref[8 + tile_rows : 16 + tile_rows, :] = jnp.zeros((8, width), F32)
    tile_ref[8 : 8 + tile_rows, :] = value[IMG_ROWS:]
    for tap in range(9):
        dy, dx = tap // 3 - 1, tap % 3 - 1
        image, tile = shifted(image_ref, tile_ref, sign * dy, sign * dx, tile_rows)
        patch_ref[tap, 0:IMG_ROWS, :] = image.astype(BF)
        patch_ref[tap, IMG_ROWS:rows, :] = tile.astype(BF)


def dot(a, b):
    return jnp.dot(a, b, preferred_element_type=F32)


def dot_nt(a, b):
    return lax.dot_general(a, b, (((1,), (1,)), ((), ())), preferred_element_type=F32)


def full(shape):
    zeros = (0,) * len(shape)
    return pl.BlockSpec(shape, lambda k: zeros)


def cols(rows):
    return pl.BlockSpec((rows, CH), lambda k: (0, k))


def smem():
    return pl.BlockSpec(memory_space=pltpu.SMEM)


def call(body, steps, in_specs, out_specs, out_shape, scratch=(), name=None, flops=0, transcendentals=0):
    return pl.pallas_call(
        body,
        grid=(steps,),
        in_specs=in_specs,
        out_specs=out_specs,
        out_shape=out_shape,
        scratch_shapes=list(scratch),
        compiler_params=pltpu.CompilerParams(
            vmem_limit_bytes=VMEM_LIMIT, dimension_semantics=("arbitrary",)
        ),
        cost_estimate=pl.CostEstimate(flops=0, bytes_accessed=0, transcendentals=0),
        name=name,
    )


def sds(shape, dtype=F32):
    return jax.ShapeDtypeStruct(shape, dtype)


def near(shape, dtype=F32):
    return pltpu.VMEM(shape, dtype)


def far(shape, dtype=F32):
    return pltpu.HBM(shape, dtype)


def away(value):
    return pltpu.with_memory_space_constraint(value, pltpu.HBM)


def stay(value):
    return pltpu.with_memory_space_constraint(value, pltpu.VMEM)


def mid_rows(table_ref, block, place):
    at = 2 * block + place
    return table_ref.at[at : at + 1], table_ref.at[2 * BLOCKS + at : 2 * BLOCKS + at + 1]


def out_rows(table_ref, block):
    return table_ref.at[block : block + 1], table_ref.at[BLOCKS + block : BLOCKS + block + 1]


def rounded(value):
    return value.astype(BF).astype(F32)


def payload(width, kinds=3):
    return (kinds, 2 * width // 128, 128)


def reduce_first(x, w_reduce, mask):
    rows, d_in = x.shape
    mid = w_reduce.shape[2]

    def body(x_ref, w_ref, mask_ref, red_ref, stats_ref):
        k = pl.program_id(0)
        part = dot(x_ref[...], w_ref[0])

        @pl.when(k == 0)
        def _():
            red_ref[...] = part

        @pl.when(k > 0)
        def _():
            red_ref[...] += part

        @pl.when(k == pl.num_programs(0) - 1)
        def _():
            local_moments(red_ref[...], mask_ref, stats_ref, 0)

    return call(
        body,
        d_in // CH,
        [cols(rows), pl.BlockSpec((1, CH, mid), lambda k: (0, k, 0)), full((rows, 1))],
        [full((rows, mid)), full(payload(mid))],
        [near((rows, mid)), near(payload(mid))],
        name="reduce_first",
        flops=2 * rows * d_in * mid,
    )(x, w_reduce, mask)


def spatial_stage(number, red, members, table, mask, w9, select):
    rows, mid = red.shape
    size = len(members)

    def body(red_ref, table_ref, mask_ref, w_ref, select_ref, *refs):
        gain_ref, bias_ref = mid_rows(table_ref, number, 0)
        got, (mr_ref, keep_ref, send_ref, out_ref, stats_ref, image, tile, patch) = refs[:size], refs[size:]
        k = pl.program_id(0)

        @pl.when(k == 0)
        def _():
            put_statistics(got, mr_ref)
            pieces = []
            for stream, lo, hi in parts(rows):
                z = normed_of(red_ref[lo:hi, :], mr_ref, stream) * gain_ref[...] + bias_ref[...]
                pieces.append(z * sigmoid(z) * mask_ref[lo:hi, :])
            hidden = jnp.concatenate(pieces, axis=0)
            fill_patches(hidden, image, tile, patch, 1)
            halves = dot(hidden.astype(BF), select_ref[...])
            keep_ref[...] = halves[:, : mid // 2]
            send_ref[...] = halves[:, mid // 2 :]
            out_ref[...] = jnp.zeros((rows, mid), F32)

        total = out_ref[...]
        for j in range(3):
            total += dot(patch[3 * k + j], w_ref[0, j])
        out_ref[...] = total

        @pl.when(k == 2)
        def _():
            local_moments(out_ref[...], mask_ref, stats_ref, 0)

    return call(
        body,
        3,
        [
            full((rows, mid)),
            full(table.shape),
            full((rows, 1)),
            pl.BlockSpec((1, 3, mid, mid), lambda k: (number, k, 0, 0)),
            full((mid, mid)),
        ]
        + [full(payload(mid))] * size,
        [
            full((8, mid)),
            full((rows, mid // 2)),
            full((rows, mid // 2)),
            full((rows, mid)),
            full(payload(mid)),
        ],
        [
            near((8, mid)),
            near((rows, mid // 2)),
            near((rows, mid // 2)),
            near((rows, mid)),
            near(payload(mid)),
        ],
        [
            pltpu.VMEM((IMG_ROWS + 48, mid), F32),
            pltpu.VMEM((rows - IMG_ROWS + 16, mid), F32),
            pltpu.VMEM((9, rows, mid), BF),
        ],
        name="spatial_stage",
        flops=2 * rows * 9 * mid * mid,
    )(red, table, mask, w9, select, *members)


def expand_stage(number, spa, members, table, mask, w_expand):
    rows, mid = spa.shape
    d_in = w_expand.shape[2]
    size = len(members)

    def body(spa_ref, table_ref, mask_ref, w_ref, *refs):
        gain_ref, bias_ref = mid_rows(table_ref, number, 1)
        got, (mr_ref, hid_ref, out_ref, stats_ref) = refs[:size], refs[size:]
        k = pl.program_id(0)

        @pl.when(k == 0)
        def _():
            put_statistics(got, mr_ref)
            for stream, lo, hi in parts(rows):
                z = normed_of(spa_ref[lo:hi, :], mr_ref, stream) * gain_ref[...] + bias_ref[...]
                hid_ref[lo:hi, :] = rounded(z * sigmoid(z) * mask_ref[lo:hi, :])

        value = dot(hid_ref[...].astype(BF), w_ref[0])
        out_ref[...] = value
        local_moments(value, mask_ref, stats_ref, k * (CH // 128))

    return call(
        body,
        d_in // CH,
        [
            full((rows, mid)),
            full(table.shape),
            full((rows, 1)),
            pl.BlockSpec((1, mid, CH), lambda k: (number, 0, k)),
        ]
        + [full(payload(mid))] * size,
        [full((8, mid)), full((rows, mid)), cols(rows), full(payload(d_in))],
        [near((8, mid)), near((rows, mid)), far((rows, d_in)), near(payload(d_in))],
        name="expand_stage",
        flops=2 * rows * d_in * mid,
    )(spa, table, mask, w_expand, *members)


def pick(ref, k, stream, row):
    return ref[2 * stream + row : 2 * stream + row + 1, pl.ds(pl.multiple_of(k * CH, CH), CH)]


def normed_at(value, mr_ref, k, stream):
    return (value - pick(mr_ref, k, stream, 0)) * pick(mr_ref, k, stream, 1)


def join_stage(number, exp, members, table, act, mask, w_reduce):
    rows, d_in = exp.shape
    mid = w_reduce.shape[2]
    size = len(members)

    def body(exp_ref, table_ref, act_ref, mask_ref, w_ref, *refs):
        gain_ref, bias_ref = out_rows(table_ref, number - 1)
        got, (mr_ref, out_ref, low_ref, red_ref, stats_ref) = refs[:size], refs[size:]
        k = pl.program_id(0)

        @pl.when(k == 0)
        def _():
            put_statistics(got, mr_ref)

        for stream, lo, hi in parts(rows):
            z = (
                normed_at(exp_ref[lo:hi, :], mr_ref, k, stream) * gain_ref[...]
                + bias_ref[...]
                + act_ref[lo:hi, :].astype(F32)
            )
            out = z * sigmoid(z) * mask_ref[lo:hi, :]
            out_ref[lo:hi, :] = out
            low_ref[lo:hi, :] = rounded(out)
        part = dot(low_ref[...].astype(BF), w_ref[0])

        @pl.when(k == 0)
        def _():
            red_ref[...] = part

        @pl.when(k > 0)
        def _():
            red_ref[...] += part

        @pl.when(k == pl.num_programs(0) - 1)
        def _():
            local_moments(red_ref[...], mask_ref, stats_ref, 0)

    return call(
        body,
        d_in // CH,
        [
            cols(rows),
            cols(table.shape[0]),
            cols(rows),
            full((rows, 1)),
            pl.BlockSpec((1, CH, mid), lambda k: (number, k, 0)),
        ]
        + [full(payload(d_in))] * size,
        [full((8, d_in)), cols(rows), cols(rows), full((rows, mid)), full(payload(mid))],
        [near((8, d_in)), far((rows, d_in)), far((rows, d_in)), near((rows, mid)), near(payload(mid))],
        name="join_stage",
        flops=2 * rows * d_in * mid,
        transcendentals=rows * d_in,
    )(exp, table, act, mask, w_reduce, *members)


def put_places(value, image_ref, tile_ref):
    row = MAP * SLOTS
    for p in range(MAP):
        image_ref[p * row : (p + 1) * row, :] = value[p * MAPW * SLOTS : p * MAPW * SLOTS + row]
    tile_ref[...] = value[IMG_ROWS : IMG_ROWS + tile_ref.shape[0]]


def put_sums(stream, pre, normed, sums_ref, first=0):
    put_rows(sums_ref, 0, stream, jnp.sum(pre, axis=0, keepdims=True), first)
    put_rows(sums_ref, 1, stream, jnp.sum(pre * normed, axis=0, keepdims=True), first)


def turn_stage(number, exp, members, table, act, mask, grad, tile_rows):
    rows, d_in = exp.shape
    size = len(members)

    def body(exp_ref, table_ref, act_ref, mask_ref, grad_ref, *refs):
        gain_ref, bias_ref = out_rows(table_ref, number)
        got, (mr_ref, image_ref, tile_ref, pre_ref, sums_ref) = refs[:size], refs[size:]
        outs = []
        k = pl.program_id(0)

        @pl.when(k == 0)
        def _():
            put_statistics(got, mr_ref)

        for stream, lo, hi in parts(rows):
            n = normed_at(exp_ref[lo:hi, :], mr_ref, k, stream)
            z = n * gain_ref[...] + bias_ref[...] + act_ref[lo:hi, :].astype(F32)
            s = sigmoid(z)
            m = mask_ref[lo:hi, :]
            outs.append(z * s * m)
            pre = grad_ref[lo:hi, :].astype(F32) * m * (s * (1.0 + z * (1.0 - s)))
            pre_ref[lo:hi, :] = pre
            put_sums(stream, pre, n, sums_ref, k * (CH // 128))
        put_places(jnp.concatenate(outs, axis=0), image_ref, tile_ref)

    return call(
        body,
        d_in // CH,
        [cols(rows), cols(table.shape[0]), cols(rows), full((rows, 1)), cols(rows)]
        + [full(payload(d_in))] * size,
        [full((8, d_in)), cols(MAP * MAP * SLOTS), cols(tile_rows), cols(rows), full(payload(d_in, 2))],
        [
            near((8, d_in)),
            far((MAP * MAP * SLOTS, d_in)),
            far((tile_rows, d_in)),
            far((rows, d_in)),
            near(payload(d_in, 2)),
        ],
        name="turn_stage",
        flops=20 * rows * d_in,
        transcendentals=rows * d_in,
    )(exp, table, act, mask, grad, *members)


def norm_back(pre, normed, plain, cross, scale, mask):
    return mask * scale * (pre - plain - normed * cross)


def rows_of(ref, stream):
    return ref[2 * stream : 2 * stream + 1, :], ref[2 * stream + 1 : 2 * stream + 2, :]


def back_expand(number, me, pre3, exp, mr3, members, outer, mask, w_expand, spa, mr2, table):
    rows, d_in = exp.shape
    mid = spa.shape[1]
    half = d_in // 2
    size = len(members)

    def body(me_ref, pre3_ref, exp_ref, mr3_ref, outer_ref, mask_ref, w_ref, spa_ref, mr2_ref, table_ref, *refs):
        gain3_ref, _ = out_rows(outer_ref, number)
        gain2_ref, bias2_ref = mid_rows(table_ref, number, 1)
        got, (both_ref, keep_ref, send_ref, pre2_ref, sums_ref, share, grad) = refs[:size], refs[size:]
        k = pl.program_id(0)

        @pl.when(k == 0)
        def _():
            put_shares(got, mr3_ref, share, both_ref)

        for stream, lo, hi in parts(rows):
            n = normed_at(exp_ref[lo:hi, :], mr3_ref, k, stream)
            grad[lo:hi, :] = norm_back(
                pre3_ref[lo:hi, :],
                n,
                pick(share, k, stream, 0),
                pick(share, k, stream, 1),
                gain3_ref[...] * pick(mr3_ref, k, stream, 1),
                mask_ref[lo:hi, :],
            ).astype(BF)
        per_half = half // CH
        at = pl.ds(pl.multiple_of(lax.rem(k, per_half) * CH, CH), CH)
        mine = k // per_half == me_ref[0]

        @pl.when(mine)
        def _():
            keep_ref[:, at] = grad[...].astype(F32)

        @pl.when(jnp.logical_not(mine))
        def _():
            send_ref[:, at] = grad[...].astype(F32)

        part = dot_nt(grad[...], w_ref[0])

        @pl.when(k == 0)
        def _():
            pre2_ref[...] = part

        @pl.when(k > 0)
        def _():
            pre2_ref[...] += part

        @pl.when(k == pl.num_programs(0) - 1)
        def _():
            for stream, lo, hi in parts(rows):
                n2 = normed_of(spa_ref[lo:hi, :], mr2_ref, stream)
                z2 = n2 * gain2_ref[...] + bias2_ref[...]
                pre2 = pre2_ref[lo:hi, :] * mask_ref[lo:hi, :] * slope(z2)
                pre2_ref[lo:hi, :] = pre2
                put_sums(stream, pre2, n2, sums_ref)

    return call(
        body,
        d_in // CH,
        [
            smem(),
            cols(rows),
            cols(rows),
            full((8, d_in)),
            cols(outer.shape[0]),
            full((rows, 1)),
            pl.BlockSpec((1, mid, CH), lambda k: (number, 0, k)),
            full((rows, mid)),
            full((8, mid)),
            full(table.shape),
        ]
        + [full(payload(d_in, 2))] * size,
        [full((2, d_in)), full((rows, half)), full((rows, half)), full((rows, mid)), full(payload(mid, 2))],
        [near((2, d_in)), near((rows, half)), near((rows, half)), near((rows, mid)), near(payload(mid, 2))],
        [pltpu.VMEM((4, d_in), F32), pltpu.VMEM((rows, CH), BF)],
        name="back_expand",
        flops=2 * rows * d_in * mid,
    )(me, pre3, exp, mr3, outer, mask, w_expand, spa, mr2, table, *members)


def back_spatial(number, me, pre2, spa, mr2, members, table, mask, w9, red, mr1):
    rows, mid = spa.shape
    size = len(members)
    quarter = mid // 4

    def body(me_ref, pre2_ref, spa_ref, mr2_ref, table_ref, mask_ref, w_ref, red_ref, mr1_ref, *refs):
        gain2_ref, _ = mid_rows(table_ref, number, 1)
        gain1_ref, bias1_ref = mid_rows(table_ref, number, 0)
        got, rest = refs[:size], refs[size:]
        both_ref, gs0, gs1, gs2, gs3, pre1_ref, sums_ref, share, image, tile, patch = rest
        k = pl.program_id(0)

        @pl.when(k == 0)
        def _():
            put_shares(got, mr2_ref, share, both_ref)
            pieces = []
            for stream, lo, hi in parts(rows):
                n = normed_of(spa_ref[lo:hi, :], mr2_ref, stream)
                plain, cross = rows_of(share, stream)
                scale = gain2_ref[...] * mr2_ref[2 * stream + 1 : 2 * stream + 2, :]
                pieces.append(norm_back(pre2_ref[lo:hi, :], n, plain, cross, scale, mask_ref[lo:hi, :]))
            value = rounded(jnp.concatenate(pieces, axis=0))
            fill_patches(value, image, tile, patch, -1)
            pre1_ref[...] = value
            for m, ref in enumerate((gs0, gs1, gs2, gs3)):
                at = pl.ds(pl.multiple_of((me_ref[1] ^ m) * quarter, quarter), quarter)
                ref[...] = pre1_ref[:, at]
            pre1_ref[...] = jnp.zeros((rows, mid), F32)

        total = pre1_ref[...]
        for j in range(3):
            total += dot_nt(patch[3 * k + j], w_ref[0, j])
        pre1_ref[...] = total

        @pl.when(k == 2)
        def _():
            for stream, lo, hi in parts(rows):
                n1 = normed_of(red_ref[lo:hi, :], mr1_ref, stream)
                z1 = n1 * gain1_ref[...] + bias1_ref[...]
                pre1 = pre1_ref[lo:hi, :] * mask_ref[lo:hi, :] * slope(z1)
                pre1_ref[lo:hi, :] = pre1
                put_sums(stream, pre1, n1, sums_ref)

    return call(
        body,
        3,
        [
            smem(),
            full((rows, mid)),
            full((rows, mid)),
            full((8, mid)),
            full(table.shape),
            full((rows, 1)),
            pl.BlockSpec((1, 3, mid, mid), lambda k: (number, k, 0, 0)),
            full((rows, mid)),
            full((8, mid)),
        ]
        + [full(payload(mid, 2))] * size,
        [full((2, mid))] + [full((rows, quarter))] * 4 + [full((rows, mid)), full(payload(mid, 2))],
        [near((2, mid))] + [near((rows, quarter))] * 4 + [near((rows, mid)), near(payload(mid, 2))],
        [
            pltpu.VMEM((4, mid), F32),
            pltpu.VMEM((IMG_ROWS + 48, mid), F32),
            pltpu.VMEM((rows - IMG_ROWS + 16, mid), F32),
            pltpu.VMEM((9, rows, mid), BF),
        ],
        name="back_spatial",
        flops=2 * rows * 9 * mid * mid,
    )(me, pre2, spa, mr2, table, mask, w9, red, mr1, *members)


def back_reduce(number, pre1, red, mr1, members, table, mask, w_reduce, pre3, below, tile_rows):
    rows, mid = red.shape
    d_in = pre3.shape[1]
    size = len(members)

    def head(k, got, pre1_ref, red_ref, mr1_ref, table_ref, mask_ref, both_ref, gr_ref, share, low):
        gain1_ref, _ = mid_rows(table_ref, number, 0)

        @pl.when(k == 0)
        def _():
            put_shares(got, mr1_ref, share, both_ref)
            for stream, lo, hi in parts(rows):
                n = normed_of(red_ref[lo:hi, :], mr1_ref, stream)
                plain, cross = rows_of(share, stream)
                scale = gain1_ref[...] * mr1_ref[2 * stream + 1 : 2 * stream + 2, :]
                low[lo:hi, :] = norm_back(pre1_ref[lo:hi, :], n, plain, cross, scale, mask_ref[lo:hi, :]).astype(BF)
            gr_ref[...] = low[...].astype(F32)

    specs = [
        full((rows, mid)),
        full((rows, mid)),
        full((8, mid)),
        full(table.shape),
        full((rows, 1)),
        pl.BlockSpec((1, CH, mid), lambda k: (number, k, 0)),
        cols(rows),
    ]
    args = [pre1, red, mr1, table, mask, w_reduce, pre3]
    scratch = [pltpu.VMEM((4, mid), F32), pltpu.VMEM((rows, mid), BF)]
    if below is None:

        def body(pre1_ref, red_ref, mr1_ref, table_ref, mask_ref, w_ref, pre3_ref, *refs):
            got, (both_ref, gr_ref, image_ref, tile_ref, share, low) = refs[:size], refs[size:]
            k = pl.program_id(0)
            head(k, got, pre1_ref, red_ref, mr1_ref, table_ref, mask_ref, both_ref, gr_ref, share, low)
            put_places(pre3_ref[...] + dot_nt(low[...], w_ref[0]), image_ref, tile_ref)

        return call(
            body,
            d_in // CH,
            specs + [full(payload(mid, 2))] * size,
            [full((2, mid)), full((rows, mid)), cols(MAP * MAP * SLOTS), cols(tile_rows)],
            [near((2, mid)), near((rows, mid)), far((MAP * MAP * SLOTS, d_in)), far((tile_rows, d_in))],
            scratch,
            name="back_reduce_last",
            flops=2 * rows * d_in * mid,
        )(*args, *members)

    def body(pre1_ref, red_ref, mr1_ref, table_ref, mask_ref, w_ref, pre3_ref, exp_ref, mr3_ref, outer_ref, act_ref, *refs):
        gain3_ref, bias3_ref = out_rows(outer_ref, number - 1)
        got, (both_ref, gr_ref, out_ref, sums_ref, share, low) = refs[:size], refs[size:]
        k = pl.program_id(0)
        head(k, got, pre1_ref, red_ref, mr1_ref, table_ref, mask_ref, both_ref, gr_ref, share, low)
        grad = pre3_ref[...] + dot_nt(low[...], w_ref[0])
        for stream, lo, hi in parts(rows):
            n = normed_at(exp_ref[lo:hi, :], mr3_ref, k, stream)
            z = n * gain3_ref[...] + bias3_ref[...] + act_ref[lo:hi, :].astype(F32)
            pre = grad[lo:hi] * mask_ref[lo:hi, :] * slope(z)
            out_ref[lo:hi, :] = pre
            put_sums(stream, pre, n, sums_ref, k * (CH // 128))

    return call(
        body,
        d_in // CH,
        specs + [cols(rows), full((8, d_in)), cols(below[2].shape[0]), cols(rows)] + [full(payload(mid, 2))] * size,
        [full((2, mid)), full((rows, mid)), cols(rows), full(payload(d_in, 2))],
        [near((2, mid)), near((rows, mid)), far((rows, d_in)), near(payload(d_in, 2))],
        scratch,
        name="back_reduce",
        flops=2 * rows * d_in * mid,
        transcendentals=rows * d_in,
    )(*args, *below, *members)


def dot_tn(a, b):
    return lax.dot_general(a, b, (((0,), (0,)), ((), ())), preferred_element_type=F32)


def spot(index, size):
    place, bit = 0, 1
    while bit < size:
        place = place * 2 + (index // bit) % 2
        bit *= 2
    return place


def weight_halves(body, args, shape, scratch, flops, name):
    vmem = pl.BlockSpec(memory_space=pltpu.VMEM)
    return pl.pallas_call(
        body,
        in_specs=[smem()] + [vmem] * 4,
        out_specs=[vmem] * 4,
        out_shape=[sds(shape)] * 4,
        scratch_shapes=list(scratch),
        compiler_params=pltpu.CompilerParams(vmem_limit_bytes=VMEM_LIMIT),
        cost_estimate=pl.CostEstimate(flops=0, bytes_accessed=0, transcendentals=0),
        name=name,
    )(*args)


def weight_expand(me, own, peer, keep, got, nz):
    rows, mid = own.shape
    step = keep.shape[1] // 4
    deep = mid // nz

    def body(me_ref, own_ref, peer_ref, keep_ref, got_ref, x_keep, x_send, y_keep, y_send):
        a = jnp.concatenate([own_ref[...].astype(BF), peer_ref[...].astype(BF)], axis=0)
        for m in range(4):
            at = pl.ds(pl.multiple_of((me_ref[3] ^ m) * step, step), step)
            b = jnp.concatenate([keep_ref[:, at].astype(BF), got_ref[:, at].astype(BF)], axis=0)
            value = dot_tn(a, b)
            x_ref = x_keep if m < 2 else x_send
            y_ref = y_keep if m % 2 == 0 else y_send
            for z in range(nz):
                place = spot(me_ref[2] ^ z, nz)
                x_ref[m % 2, place] = value[z * deep : (z + 1) * deep, 0:128]
                y_ref[m // 2, place] = value[z * deep : (z + 1) * deep, 128:256]

    return weight_halves(body, (me, own, peer, keep, got), (2, nz, deep, 128), (), 0, "weight_expand")


def weight_reduce(me, own, peer, keep, got, nz):
    rows, width = own.shape
    mid = keep.shape[1]
    step = mid // 4
    deep = width // nz
    part = deep // 2

    def body(me_ref, own_ref, peer_ref, keep_ref, got_ref, x_keep, x_send, y_keep, y_send, total):
        b = jnp.concatenate([keep_ref[...].astype(BF), got_ref[...].astype(BF)], axis=0)
        for z in range(nz):
            at = slice(z * deep, (z + 1) * deep)
            a = jnp.concatenate([own_ref[:, at].astype(BF), peer_ref[:, at].astype(BF)], axis=0)
            total[...] = dot_tn(a, b)
            place = spot(me_ref[2] ^ z, nz)
            for m in range(4):
                column = me_ref[1] ^ ((m % 2) * 2 + m // 2)
                value = total[:, pl.ds(pl.multiple_of(column * step, step), step)]
                (x_keep if m < 2 else x_send)[m % 2, place] = value[:part]
                (y_keep if m % 2 == 0 else y_send)[m // 2, place] = value[part:]

    return weight_halves(
        body, (me, own, peer, keep, got), (2, nz, part, step), [pltpu.VMEM((deep, mid), F32)], 0, "weight_reduce"
    )


def weight_spatial(me, hidden, near, far, nz):
    both, half = hidden[0].shape
    rows = both // 2
    width = near[0].shape[1]
    deep = half // nz
    tile_rows = rows - IMG_ROWS

    def body(me_ref, h0, h1, h2, h3, h4, n0, n1, n2, n3, far_ref, keep_ref, send_ref, image, tile, left, patch, total):
        image[...] = jnp.zeros_like(image)
        tile[...] = jnp.zeros_like(tile)
        for m, ref in enumerate((h0, h1, h2)):
            left[m * both : (m + 1) * both, :] = ref[...].astype(BF)
        left[3 * both : 3 * both + rows, :] = h3[...].astype(BF)
        left[3 * both + rows :, :] = h4[...].astype(BF)
        for m, n_ref in enumerate((n0, n1, n2, n3)):
            for core in range(2):
                value = n_ref[...] if core == 0 else far_ref[m]
                at = m * both + core * rows
                image[24 : 24 + IMG_ROWS, :] = value[0:IMG_ROWS]
                tile[8 : 8 + tile_rows, :] = value[IMG_ROWS:rows]
                for tap in range(9):
                    dy, dx = tap // 3 - 1, tap % 3 - 1
                    part, rest = shifted(image, tile, -dy, -dx, tile_rows)
                    patch[at : at + IMG_ROWS, tap * width : (tap + 1) * width] = part.astype(BF)
                    patch[at + IMG_ROWS : at + rows, tap * width : (tap + 1) * width] = rest.astype(BF)
        total[...] = dot_tn(left[...], patch[...])
        for p in range(nz):
            z = me_ref[2] ^ spot(p, nz)
            value = total[pl.ds(pl.multiple_of(z * deep, deep), deep), :]
            ref, at = (keep_ref, p) if p < nz // 2 else (send_ref, p - nz // 2)
            for tap in range(9):
                ref[at, tap] = value[:, tap * width : (tap + 1) * width]

    vmem = pl.BlockSpec(memory_space=pltpu.VMEM)
    return pl.pallas_call(
        body,
        in_specs=[smem()] + [vmem] * 10,
        out_specs=[vmem] * 2,
        out_shape=[sds((nz // 2, 9, deep, width))] * 2,
        scratch_shapes=[
            pltpu.VMEM((IMG_ROWS + 48, width), F32),
            pltpu.VMEM((tile_rows + 16, width), F32),
            pltpu.VMEM((4 * both, half), BF),
            pltpu.VMEM((4 * both, 9 * width), BF),
            pltpu.VMEM((half, 9 * width), F32),
        ],
        compiler_params=pltpu.CompilerParams(vmem_limit_bytes=VMEM_LIMIT),
        cost_estimate=pl.CostEstimate(flops=0, bytes_accessed=0, transcendentals=0),
        name="weight_spatial",
    )(me, *hidden, *near, far)


class Collect:
    def __init__(self, grid, me):
        self.grid, self.me, self.marks = grid, me, None

    def over_z(self, keep, send, gate=None):
        step = 1
        while True:
            (got,) = yield "deep", [(send, dict(dz=step))]
            step *= 2
            if step == self.grid.z:
                if gate:
                    got, _ = lax.optimization_barrier((got, gate[2]))
                return keep[0] + got[0]
            half = keep.shape[0] // 2
            keep, send = keep[:half] + got[:half], keep[half:] + got[half:]

    def chips(self, pieces, out):
        flat = jnp.concatenate([p.reshape(-1, 128) for p in pieces])
        for group in self.grid.far():
            flat = flat + sum(self.grid.swap(flat, **step) for step in group)
        got = yield "plane", [(flat, dict(dx=1)), (flat, dict(dy=1)), (flat, dict(dy=1, dx=1))]
        out.extend([flat] + list(lax.optimization_barrier(tuple(got))))

    def by_halves(self, kernel, own, peer, keep, send, out, after=None, gate=None):
        (got,) = yield "core", [(send, dict(dc=1))]
        if after:
            got, _ = lax.optimization_barrier((got, after[0]))
        x_keep, x_send, y_keep, y_send = kernel(self.me, own, peer, keep, got, self.grid.z)
        self.begun = x_keep
        got = yield "plane", [(x_send, dict(dx=1)), (y_send, dict(dy=1))]
        got = lax.optimization_barrier(tuple(got))
        if after is not None:
            after.append(got[0])
        x_last, y_last = x_keep[1:] + got[0][1:], y_keep[1:] + got[1][1:]
        x_keep, y_keep = x_keep[:1] + got[0][:1], y_keep[:1] + got[1][:1]
        got = yield "plane", [(x_last, dict(dy=1)), (y_last, dict(dx=1))]
        if after is not None:
            after.append(got[0])
        half = self.grid.z // 2

        def side(at):
            return jnp.concatenate([x_keep[0, at] + got[0][0, at], y_keep[0, at] + got[1][0, at]], axis=1)

        piece = yield from self.over_z(side(slice(0, half)), side(slice(half, 2 * half)), gate)
        out.append(piece)

    def by_rows(self, hidden, grad, out, after=None):
        got = yield "tight", [(grad[1], dict(dx=1)), (grad[2], dict(dy=1)), (grad[3], dict(dy=1, dx=1))]
        near = [grad[0]] + list(got)
        (far,) = yield "core", [(jnp.stack(near), dict(dc=1))]
        keep, send = weight_spatial(self.me, hidden, near, far, self.grid.z)
        if after is not None:
            after.append(keep)
        piece = yield from self.over_z(keep, send, after)
        out.append(piece)

    def hidden(self, keep, send, out):
        (got,) = yield "core", [(send, dict(dc=1))]
        value = jnp.concatenate([keep, got], axis=0)
        got = yield "plane", [(value, dict(dx=1)), (value, dict(dy=1))]
        rows = keep.shape[0]
        last = yield "tight", [(got[0][:rows], dict(dy=1)), (got[1][rows:], dict(dx=1))]
        out.extend([value, got[0], got[1], last[0], last[1]])


def place_slices(me, gathered, shapes):
    (e_rows, d_in), (r_rows, mid), (s_rows, _) = shapes
    dims = ((BLOCKS, r_rows, mid), (BLOCKS, 9, s_rows, mid), (BLOCKS, e_rows, d_in))
    size = 8 * BLOCKS
    r_len, s_len = r_rows // 2, s_rows // 2

    def body(me_ref, *refs):
        got = refs[:size]
        outs, (red, spa, exp, sems, out_sems) = refs[-8:-5], refs[-5:]
        copies = [[] for _ in range(BLOCKS)]
        for b in range(BLOCKS):
            for a in range(8):
                core = me_ref[0] if a < 4 else 1 - me_ref[0]
                chip = (a % 4) ^ me_ref[1]
                source = got[8 * b + a]
                column = core * 4 + (chip % 2) * 2 + chip // 2
                moves = []
                for t in range(2):
                    at = pl.multiple_of(column * 256 + t * 128, 128)
                    moves.append((source.at[pl.ds(t * e_rows, e_rows), :], exp.at[b, :, pl.ds(at, 128)]))
                at = pl.multiple_of(chip * 128, 128)
                row = pl.multiple_of(core * r_len, r_len)
                start = 2 * e_rows
                moves.append((source.at[pl.ds(start, r_len), :], red.at[b, pl.ds(row, r_len), pl.ds(at, 128)]))
                row = pl.multiple_of(core * s_len, s_len)
                start = 2 * e_rows + r_len
                taps = source.at[pl.ds(start, 9 * s_len), :].reshape(9, s_len, 128)
                moves.append((taps, spa.at[b, :, pl.ds(row, s_len), pl.ds(at, 128)]))
                copies[b] += [
                    pltpu.make_async_copy(src, dst, sems.at[b, a, i]) for i, (src, dst) in enumerate(moves)
                ]
        last = []
        for copy in copies[0] + copies[1]:
            copy.start()
        for b in range(BLOCKS):
            for copy in copies[b]:
                copy.wait()
            for i, (src, dst) in enumerate(zip((red, spa, exp), outs)):
                copy = pltpu.make_async_copy(src.at[b], dst.at[b], out_sems.at[b, i])
                copy.start()
                last.append(copy)
        for copy in last:
            copy.wait()

    anywhere = pl.BlockSpec(memory_space=pl.ANY)
    return pl.pallas_call(
        body,
        in_specs=[smem()] + [anywhere] * size,
        out_specs=[anywhere] * 3,
        out_shape=[sds(d) for d in dims],
        scratch_shapes=[pltpu.VMEM(d, F32) for d in dims]
        + [pltpu.SemaphoreType.DMA((BLOCKS, 8, 4)), pltpu.SemaphoreType.DMA((BLOCKS, 3))],
        compiler_params=pltpu.CompilerParams(vmem_limit_bytes=VMEM_LIMIT),
        name="place_slices",
    )(me, *gathered)


def to_rows(image, tile, rows):
    width = image.shape[-1]
    image = jnp.transpose(image, (1, 2, 0, 3))
    image = jnp.pad(image, ((0, 0), (0, 1), (0, 0), (0, 0))).reshape(IMG_ROWS, width)
    tile = tile.reshape(-1, width)
    pad = jnp.zeros((rows - IMG_ROWS - tile.shape[0], width), tile.dtype)
    return jnp.concatenate([image, tile, pad], axis=0)


def from_rows(image, tile):
    width = image.shape[1]
    image = jnp.transpose(image.reshape(MAP, MAP, SLOTS, width), (2, 0, 1, 3))
    return image, tile.reshape(-1, TILE, TILE, width)


def row_mask(map_sizes, rows):
    row = jnp.arange(MAP)
    col = jnp.arange(MAPW)
    inside = (row[:, None, None] < map_sizes[None, None, :]) & (col[None, :, None] < map_sizes[None, None, :])
    image = inside.astype(F32).reshape(IMG_ROWS)
    tile = jnp.repeat((map_sizes > 0).astype(F32), PIECES * TILE * TILE)
    pad = jnp.zeros((rows - IMG_ROWS - tile.shape[0],), F32)
    return jnp.concatenate([image, tile, pad])[:, None]


def core_halves(value, core, nz):
    deep = value.shape[1] // (2 * nz)
    low = [value[:, 2 * z * deep : (2 * z + 1) * deep] for z in range(nz)]
    high = [value[:, (2 * z + 1) * deep : (2 * z + 2) * deep] for z in range(nz)]
    low, high = jnp.concatenate(low, axis=1), jnp.concatenate(high, axis=1)
    keep = jnp.where(core == 0, low, high).astype(F32)
    send = jnp.where(core == 0, high, low).astype(F32)
    return keep, send


def core_select(core, mid, nz):
    deep = mid // (2 * nz)
    at = jnp.arange(mid)
    side = at // (mid // 2)
    inner = at % (mid // 2)
    source = (inner // deep) * 2 * deep + (side ^ core) * deep + inner % deep
    return (jnp.arange(mid)[:, None] == source[None, :]).astype(BF)


def per_device(
    grid,
    images,
    tile_maps,
    map_sizes,
    w_reduce,
    w_spatial,
    w_expand,
    gain_mid,
    bias_mid,
    gain_out,
    bias_out,
    grad_images,
    grad_tiles,
):
    tiles = tile_maps.shape[0]
    rows = -(-(IMG_ROWS + tiles * TILE * TILE) // 16) * 16
    d_in, mid = w_reduce.shape[1:]
    nz = grid.z
    y, x, core, z = grid.index()
    chip = (y % 2) * 2 + x % 2
    turned = (x % 2) * 2 + y % 2
    me = jnp.stack([core, chip, z, turned]).astype(jnp.int32)
    mask = row_mask(map_sizes, rows)
    w9 = w_spatial.reshape(BLOCKS, 9, mid, mid)
    start = to_rows(images, tile_maps, rows)
    grad = to_rows(grad_images, grad_tiles, rows)
    select = core_select(core, mid, nz)
    collect = Collect(grid, me)
    bulk = Bulk(grid, ROOM)

    table = stay(jnp.concatenate([gain_mid.reshape(-1, mid), bias_mid.reshape(-1, mid)]))
    outer = stay(jnp.concatenate([gain_out, bias_out]))
    w_reduce, w9, w_expand = (pltpu.with_memory_space_constraint(w, pltpu.HBM) for w in (w_reduce, w9, w_expand))

    def moments(stats):
        return exchange(grid, bulk, stats, join_moments)

    def sums(value):
        return exchange(grid, bulk, value, add_members)

    acts, lows, reds, spas, exps = [start], [], [], [], []
    mr1, mr2, mr3, hid1, hid2 = [], [], [], [], []
    red, stats = reduce_first(start, w_reduce, mask)
    low = start
    for b in range(BLOCKS):
        reds.append(red)
        mr, keep, send, spa, stats = spatial_stage(
            b, red, moments(stats), table, mask, w9, select
        )
        mr1.append(mr)
        hid1.append([])
        bulk.add(("h", b), collect.hidden(keep, send, hid1[b]))
        keep, send = core_halves(low, core, nz)
        peer = grid.swap(send, dc=1)
        stats, keep, peer = lax.optimization_barrier((stats, keep, peer))
        lows.append((keep, peer))
        spas.append(spa)
        mr, hidden, exp, stats = expand_stage(
            b, spa, moments(stats), table, mask, w_expand
        )
        mr2.append(mr)
        hid2.append((hidden, grid.swap(hidden, dc=1)))
        exp = away(exp)
        exps.append(exp)
        if b + 1 < BLOCKS:
            mr, out, low, red, stats = join_stage(
                b + 1, exp, moments(stats), outer, acts[b], mask, w_reduce
            )
            mr3.append(mr)
            acts.append(away(out))
    last = BLOCKS - 1
    mr, *out, pre3, sums3 = turn_stage(
        last, exps[last], moments(stats), outer, acts[last], mask, grad, tiles * TILE * TILE
    )
    mr3.append(mr)
    pre3 = away(pre3)

    both1, both2, both3 = [None] * BLOCKS, [None] * BLOCKS, [None] * BLOCKS
    shapes = ((mid // nz, d_in), (d_in // nz, mid), (mid // nz, mid))
    pieces = [([], [], []) for _ in range(BLOCKS)]
    after = []
    for b in reversed(range(BLOCKS)):
        both3[b], keep, send, pre2, sums2 = back_expand(
            b, me, pre3, exps[b], mr3[b], sums(sums3), outer, mask, w_expand,
            spas[b], mr2[b], table,
        )
        bulk.add(("e", b), collect.by_halves(weight_expand, *hid2[b], keep, send, pieces[b][0]))
        both2[b], *gs, pre1, sums1 = back_spatial(
            b, me, pre2, spas[b], mr2[b], sums(sums2), table, mask, w9,
            reds[b], mr1[b],
        )
        bulk.add(("s", b), collect.by_rows(hid1[b], gs, pieces[b][2], after if b == 0 else None))
        below = None
        if b > 0:
            below = (exps[b - 1], mr3[b - 1], outer, acts[b - 1])
        result = back_reduce(
            b, pre1, reds[b], mr1[b], sums(sums1), table, mask, w_reduce, pre3, below, tiles * TILE * TILE
        )
        both1[b] = result[0]
        gr = result[1]
        reduce_flow = collect.by_halves(
            weight_reduce, *lows[b], gr, gr, pieces[b][1], after if b == 0 else None, after if b else None
        )
        if b > 0:
            bulk.add(("r", b), reduce_flow)
        if b > 0:
            pre3, sums3 = away(result[2]), result[3]
        else:
            grad_in = list(result[2:4])

    grad_in[0] = bulk.last(grad_in[0], [("s", 0)])
    bulk.add(("r", 0), reduce_flow)
    later = [(n, b) for b in range(1, BLOCKS) for n in "ers"]
    every = later + [("e", 0)]
    bulk.hold(later, collect.begun)
    bulk.resume(later, collect.begun)
    bulk.run([("r", 0)], ("plane",), 1)
    bulk.resume([("e", 0)], after[1])
    bulk.hold([("e", 0)], after[1])
    bulk.run([("r", 0)], ("plane",))
    bulk.run([("s", 0)])
    bulk.run(every, ("deep",))
    views = []
    for value in (*out, *grad_in):
        value, _ = lax.optimization_barrier((value, after[2]))
        views.append(value)
    views = from_rows(*views[:2]) + from_rows(*views[2:])
    bulk.run(every)
    gathered = [[] for _ in range(BLOCKS)]
    for b in range(1, BLOCKS):
        bulk.add(("g", b), collect.chips([p[0] for p in pieces[b]], gathered[b]))
        bulk.hold([("g", b)], after[2])
        bulk.run([("g", b)])
    bulk.run([("r", 0)])
    bulk.add(("g", 0), collect.chips([p[0] for p in pieces[0]], gathered[0]))
    bulk.run([("g", 0)])
    *views, gathered[0][1] = lax.optimization_barrier((*views, gathered[0][1]))
    final = []
    for b in range(BLOCKS):
        final += gathered[b] + [grid.swap(v, dc=1) for v in gathered[b]]
    final = [pltpu.with_memory_space_constraint(v, pltpu.HBM) for v in final]
    slices = place_slices(me, final, shapes)
    out_images, out_tiles, in_images, in_tiles = views
    g_reduce, g_spatial, g_expand = slices

    def pair(at):
        return jnp.stack([jnp.stack([both1[b][at], both2[b][at]]) for b in range(BLOCKS)])

    return (
        out_images,
        out_tiles,
        in_images,
        in_tiles,
        g_reduce,
        g_spatial.reshape(BLOCKS, 3, 3, mid // nz, mid),
        g_expand,
        pair(1),
        pair(0),
        jnp.stack([both3[b][1] for b in range(BLOCKS)]),
        jnp.stack([both3[b][0] for b in range(BLOCKS)]),
    )


def solution(mesh):
    both = ("wide", "narrow")
    batch = P(both, None, None, None)
    grid = Grid(mesh.shape["wide"], mesh.shape["narrow"])
    return jax.shard_map(
        functools.partial(per_device, grid),
        mesh=mesh,
        in_specs=(batch, batch, P(both), P(), P(), P(), P(), P(), P(), P(), batch, batch),
        out_specs=(
            batch,
            batch,
            batch,
            batch,
            P(None, "narrow", None),
            P(None, None, None, "narrow", None),
            P(None, "narrow", None),
            P(),
            P(),
            P(),
            P(),
        ),
        check_vma=False,
    )
```

```python
import functools

import jax
import jax.numpy as jnp
from jax import lax
from jax.experimental import pallas as pl
from jax.experimental.pallas import tpu as pltpu
from jax.sharding import PartitionSpec as P

BLOCKS = 2
MAP = 7
MAPW = 8
TILE = 2
PIECES = 9
SLOTS = 2
IMG_ROWS = MAP * MAPW * SLOTS
EPS = 1e-05
CH = 512
BF = jnp.bfloat16
F32 = jnp.float32
VMEM_LIMIT = 16 * 1024 * 1024
AXES = ("wide", "narrow")
ROOM = 640 * 1024


class Grid:
    def __init__(self, wide, narrow):
        chips = wide // 2
        side = 1
        while side * side < chips:
            side *= 2
        self.y, self.x, self.c, self.z = chips // side, side, 2, narrow

    def index(self):
        wide = lax.axis_index("wide")
        core = wide % 2
        chip = wide // 2
        return chip // self.x, chip % self.x, core, lax.axis_index("narrow")

    def swap(self, value, dy=0, dx=0, dc=0, dz=0):
        pairs = []
        for y in range(self.y):
            for x in range(self.x):
                for c in range(self.c):
                    for z in range(self.z):
                        src = ((y * self.x + x) * 2 + c) * self.z + z
                        dst = (((y ^ dy) * self.x + (x ^ dx)) * 2 + (c ^ dc)) * self.z + (z ^ dz)
                        pairs.append((src, dst))
        return lax.ppermute(value, AXES, pairs)

    def plane(self, value):
        if self.y * self.x == 4:
            return lax.all_gather(value, "wide")
        groups = {}
        for y in range(self.y):
            for x in range(self.x):
                for c in range(2):
                    groups.setdefault((y // 2, x // 2), []).append((y * self.x + x) * 2 + c)
        return lax.all_gather(value, "wide", axis_index_groups=list(groups.values()))

    def phases(self):
        found = [[dict(dc=1)]]
        step = 1
        while step < max(self.x, self.y):
            group = []
            for dy in (0, step):
                for dx in (0, step):
                    if (dy or dx) and dy < self.y and dx < self.x:
                        group.append(dict(dy=dy, dx=dx))
            found.append(group)
            step *= 2
        self.far_groups = found[2:]
        found.append([dict(dz=k) for k in range(1, min(self.z, 4))])
        step = 4
        while step < self.z:
            found.append([dict(dz=step)])
            step *= 2
        return found

    def far(self):
        self.phases()
        return self.far_groups


class Bulk:
    def __init__(self, grid, room):
        self.grid, self.room = grid, room
        self.waiting = []
        self.flying = {"plane": [], "tight": [], "deep": [], "spare": []}
        self.late = []
        self.names = {}

    def move(self, value, step):
        return step(value) if callable(step) else self.grid.swap(value, **step)

    def add(self, name, flow):
        self.names[flow] = name
        self.advance(flow, None)

    def advance(self, flow, value):
        while True:
            try:
                kind, pieces = flow.send(value)
            except StopIteration:
                return
            if kind != "core":
                self.waiting.append((flow, kind, pieces))
                return
            value = [self.move(v, step) for v, step in pieces]

    def load(self, pieces):
        used = {}
        for value, step in pieces:
            for name in () if callable(step) else step:
                used[name] = used.get(name, 0) + value.size * 4
        return used

    def open(self, kinds, arrays):
        used, chosen, rest = {}, [], []
        for item in self.waiting:
            if item[1] in kinds:
                load = self.load(item[2])
                if all(used.get(n, 0) + load[n] <= self.room for n in load):
                    for n in load:
                        used[n] = used.get(n, 0) + load[n]
                    chosen.append(item)
                    continue
                for n in load:
                    used[n] = max(used.get(n, 0), self.room)
            rest.append(item)
        self.waiting = rest
        if not chosen:
            return arrays
        values = [v for _, _, pieces in chosen for v, _ in pieces]
        tied = lax.optimization_barrier(tuple(arrays) + tuple(values))
        arrays, values = list(tied[: len(arrays)]), list(tied[len(arrays) :])
        for flow, kind, pieces in chosen:
            got = [self.move(values.pop(0), step) for _, step in pieces]
            self.flying[kind].append((flow, got))
        return arrays

    def close(self, kind, array):
        done = self.flying[kind]
        self.flying[kind] = []
        if kind == "deep":
            done = done + self.late
            self.late, self.flying["spare"] = self.flying["spare"], []
        if not done:
            return array
        values = [v for _, got in done for v in got]
        tied = lax.optimization_barrier((array,) + tuple(values))
        array, values = tied[0], list(tied[1:])
        for flow, got in done:
            self.advance(flow, [values.pop(0) for _ in got])
        return array

    def last(self, array, first):
        done = self.flying["plane"] + self.flying["deep"]
        self.flying = {"plane": [], "tight": [], "deep": [], "spare": []}
        values = [v for _, got in done for v in got]
        tied = lax.optimization_barrier((array,) + tuple(values))
        array, values = tied[0], list(tied[1:])
        self.parked = []
        for flow, got in done:
            got = [values.pop(0) for _ in got]
            if self.names[flow] in first:
                self.advance(flow, got)
            else:
                self.parked.append((flow, got))
        return array

    def resume(self, names, after):
        parked, self.parked = self.parked, []
        for flow, got in parked:
            if self.names[flow] not in names:
                self.parked.append((flow, got))
                continue
            *got, _ = lax.optimization_barrier((*got, after))
            self.advance(flow, got)

    def hold(self, names, after):
        held = [item for item in self.waiting if self.names[item[0]] in names]
        if not held:
            return
        values = [v for _, _, pieces in held for v, _ in pieces]
        *values, _ = lax.optimization_barrier((*values, after))
        fresh = {}
        for flow, kind, pieces in held:
            fresh[flow] = (flow, kind, [(values.pop(0), step) for _, step in pieces])
        self.waiting = [fresh.get(item[0], item) for item in self.waiting]

    def run(self, names, kinds=("plane", "deep"), rounds=9, tie=None):
        for _ in range(rounds):
            batch = [i for i in self.waiting if self.names[i[0]] in names and i[1] in kinds]
            if not batch:
                return tie
            self.waiting = [i for i in self.waiting if i not in batch]
            for flow, kind, pieces in batch:
                got = [self.move(v, step) for v, step in pieces]
                if tie is not None:
                    tied = lax.optimization_barrier((*got, *tie))
                    got, tie = list(tied[: len(got)]), list(tied[len(got) :])
                self.advance(flow, got)
        return tie


def exchange(grid, bulk, payload, join):
    groups = grid.phases()
    for number, group in enumerate(groups):
        if number == 1:
            payload = bulk.close("plane", payload)
        if number + 1 == len(groups):
            (payload,) = bulk.open(("plane", "tight"), [payload])
            payload = bulk.close("deep", payload)
        members = [payload] + [grid.swap(payload, **step) for step in group]
        if number + 1 < len(groups):
            payload = join(members)
    members[0] = bulk.close("tight", members[0])
    return bulk.open(("deep", "spare"), members)


def add_members(members):
    return sum(members[1:], members[0])


def join_moments(members):
    count = sum(m[2] for m in members)
    plain = sum(m[0] for m in members)
    mean = plain / count
    square = sum(m[1] for m in members)
    for m in members:
        gap = m[0] / jnp.maximum(m[2], 1.0) - mean
        square = square + m[2] * (gap * gap)
    return jnp.stack([plain, square, count])


def put_rows(ref, at, stream, value, first=0):
    base = stream * (ref.shape[1] // 2)
    for j in range(value.shape[1] // 128):
        ref[at, pl.ds(base + first + j, 1), :] = value[:, j * 128 : (j + 1) * 128]


def as_row(value):
    return jnp.concatenate([value[j : j + 1] for j in range(value.shape[0])], axis=1)


def put_statistics(members, out_ref):
    counts = [m[2] for m in members]
    sums = [m[0] for m in members]
    count = sum(counts[1:], counts[0])
    mean = sum(sums[1:], sums[0]) / count
    square = None
    for m, n, v in zip(members, counts, sums):
        gap = v / jnp.maximum(n, 1.0) - mean
        term = m[1] + n * (gap * gap)
        square = term if square is None else square + term
    rstd = lax.rsqrt(square / count + EPS)
    inv = 1.0 / count
    half = mean.shape[0] // 2
    for stream in range(2):
        at = slice(stream * half, (stream + 1) * half)
        out_ref[2 * stream : 2 * stream + 1, :] = as_row(mean[at])
        out_ref[2 * stream + 1 : 2 * stream + 2, :] = as_row(rstd[at])
        out_ref[4 + stream : 5 + stream, :] = as_row(inv[at])
    out_ref[6:8, :] = jnp.zeros((2, out_ref.shape[1]), F32)


def put_shares(members, mr_ref, share_ref, both_ref):
    half = members[0].shape[1] // 2
    for kind in range(2):
        total = members[0][kind]
        for m in members[1:]:
            total += m[kind]
        for stream in range(2):
            value = as_row(total[stream * half : (stream + 1) * half])
            share_ref[2 * stream + kind : 2 * stream + kind + 1, :] = value * mr_ref[4 + stream : 5 + stream, :]
        both_ref[kind : kind + 1, :] = as_row(total[:half] + total[half:])


def parts(rows):
    return ((0, 0, IMG_ROWS), (1, IMG_ROWS, rows))


def sigmoid(v):
    return 0.5 * jnp.tanh(0.5 * v) + 0.5


def slope(v):
    s = sigmoid(v)
    return s * (1.0 + v * (1.0 - s))


def local_moments(value, mask_ref, stats_ref, first):
    width = value.shape[1]
    for stream, lo, hi in parts(value.shape[0]):
        v = value[lo:hi]
        m = mask_ref[lo:hi, :]
        count = jnp.sum(m, axis=0, keepdims=True)
        plain = jnp.sum(v * m, axis=0, keepdims=True)
        gap = (v - plain / jnp.maximum(count, 1.0)) * m
        put_rows(stats_ref, 0, stream, plain, first)
        put_rows(stats_ref, 1, stream, jnp.sum(gap * gap, axis=0, keepdims=True), first)
        put_rows(stats_ref, 2, stream, jnp.broadcast_to(count, (1, width)), first)


def normed_of(value, mr_ref, stream):
    return (value - mr_ref[2 * stream : 2 * stream + 1, :]) * mr_ref[2 * stream + 1 : 2 * stream + 2, :]


def shifted(image_ref, tile_ref, dy, dx, tile_rows):
    start = 24 + 2 * MAPW * dy + 2 * dx
    image = image_ref[start : start + IMG_ROWS, :]
    start = 8 + TILE * dy + dx
    tile = tile_ref[start : start + tile_rows, :]
    if dy or dx:
        place = lax.broadcasted_iota(jnp.int32, (tile_rows, 1), 0)
        ty = (place // TILE) % TILE + dy
        tx = place % TILE + dx
        valid = (ty >= 0) & (ty < TILE) & (tx >= 0) & (tx < TILE)
        tile = jnp.where(valid, tile, 0.0)
    return image, tile


def fill_patches(value, image_ref, tile_ref, patch_ref, sign):
    rows = value.shape[0]
    tile_rows = rows - IMG_ROWS
    width = value.shape[1]
    image_ref[0:24, :] = jnp.zeros((24, width), F32)
    image_ref[24 + IMG_ROWS : 48 + IMG_ROWS, :] = jnp.zeros((24, width), F32)
    image_ref[24 : 24 + IMG_ROWS, :] = value[0:IMG_ROWS]
    tile_ref[0:8, :] = jnp.zeros((8, width), F32)
    tile_ref[8 + tile_rows : 16 + tile_rows, :] = jnp.zeros((8, width), F32)
    tile_ref[8 : 8 + tile_rows, :] = value[IMG_ROWS:]
    for tap in range(9):
        dy, dx = tap // 3 - 1, tap % 3 - 1
        image, tile = shifted(image_ref, tile_ref, sign * dy, sign * dx, tile_rows)
        patch_ref[tap, 0:IMG_ROWS, :] = image.astype(BF)
        patch_ref[tap, IMG_ROWS:rows, :] = tile.astype(BF)


def dot(a, b):
    return jnp.dot(a, b, preferred_element_type=F32)


def dot_nt(a, b):
    return lax.dot_general(a, b, (((1,), (1,)), ((), ())), preferred_element_type=F32)


def full(shape):
    zeros = (0,) * len(shape)
    return pl.BlockSpec(shape, lambda k: zeros)


def cols(rows):
    return pl.BlockSpec((rows, CH), lambda k: (0, k))


def smem():
    return pl.BlockSpec(memory_space=pltpu.SMEM)


def call(body, steps, in_specs, out_specs, out_shape, scratch=(), name=None, flops=0, transcendentals=0):
    return pl.pallas_call(
        body,
        grid=(steps,),
        in_specs=in_specs,
        out_specs=out_specs,
        out_shape=out_shape,
        scratch_shapes=list(scratch),
        compiler_params=pltpu.CompilerParams(
            vmem_limit_bytes=VMEM_LIMIT, dimension_semantics=("arbitrary",)
        ),
        cost_estimate=pl.CostEstimate(flops=0, bytes_accessed=0, transcendentals=0),
        name=name,
    )


def sds(shape, dtype=F32):
    return jax.ShapeDtypeStruct(shape, dtype)


def near(shape, dtype=F32):
    return pltpu.VMEM(shape, dtype)


def far(shape, dtype=F32):
    return pltpu.HBM(shape, dtype)


def away(value):
    return pltpu.with_memory_space_constraint(value, pltpu.HBM)


def stay(value):
    return pltpu.with_memory_space_constraint(value, pltpu.VMEM)


def mid_rows(table_ref, block, place):
    at = 2 * block + place
    return table_ref.at[at : at + 1], table_ref.at[2 * BLOCKS + at : 2 * BLOCKS + at + 1]


def out_rows(table_ref, block):
    return table_ref.at[block : block + 1], table_ref.at[BLOCKS + block : BLOCKS + block + 1]


def rounded(value):
    return value.astype(BF).astype(F32)


def payload(width, kinds=3):
    return (kinds, 2 * width // 128, 128)


def reduce_first(x, w_reduce, sizes):
    rows, d_in = x.shape
    mid = w_reduce.shape[2]

    def body(sizes_ref, x_ref, w_ref, mask_ref, red_ref, stats_ref):
        k = pl.program_id(0)

        @pl.when(k == 0)
        def _():
            at = lax.broadcasted_iota(jnp.int32, (rows, 1), 0)
            inside = at < 0
            for slot in range(SLOTS):
                side = sizes_ref[slot]
                image = (at < IMG_ROWS) & ((at & (SLOTS - 1)) == slot)
                image &= ((at >> 4) < side) & (((at >> 1) & (MAPW - 1)) < side)
                first = IMG_ROWS + slot * PIECES * TILE * TILE
                tile = (at >= first) & (at < first + PIECES * TILE * TILE) & (at * 0 < side)
                inside |= image | tile
            mask_ref[...] = jnp.where(inside, 1.0, 0.0)

        part = dot(x_ref[...], w_ref[0])

        @pl.when(k == 0)
        def _():
            red_ref[...] = part

        @pl.when(k > 0)
        def _():
            red_ref[...] += part

        @pl.when(k == pl.num_programs(0) - 1)
        def _():
            local_moments(red_ref[...], mask_ref, stats_ref, 0)

    return call(
        body,
        d_in // CH,
        [smem(), cols(rows), pl.BlockSpec((1, CH, mid), lambda k: (0, k, 0))],
        [full((rows, 1)), full((rows, mid)), full(payload(mid))],
        [near((rows, 1)), near((rows, mid)), near(payload(mid))],
        name="reduce_first",
        flops=2 * rows * d_in * mid,
    )(sizes, x, w_reduce)


def spatial_stage(number, red, members, table, mask, w9, select):
    rows, mid = red.shape
    size = len(members)

    def body(red_ref, table_ref, mask_ref, w_ref, select_ref, *refs):
        gain_ref, bias_ref = mid_rows(table_ref, number, 0)
        got, (mr_ref, keep_ref, send_ref, out_ref, stats_ref, image, tile, patch) = refs[:size], refs[size:]
        k = pl.program_id(0)

        @pl.when(k == 0)
        def _():
            put_statistics(got, mr_ref)
            pieces = []
            for stream, lo, hi in parts(rows):
                z = normed_of(red_ref[lo:hi, :], mr_ref, stream) * gain_ref[...] + bias_ref[...]
                pieces.append(z * sigmoid(z) * mask_ref[lo:hi, :])
            hidden = jnp.concatenate(pieces, axis=0)
            fill_patches(hidden, image, tile, patch, 1)
            halves = dot(hidden.astype(BF), select_ref[...])
            keep_ref[...] = halves[:, : mid // 2]
            send_ref[...] = halves[:, mid // 2 :]
            out_ref[...] = jnp.zeros((rows, mid), F32)

        total = out_ref[...]
        for j in range(3):
            total += dot(patch[3 * k + j], w_ref[0, j])
        out_ref[...] = total

        @pl.when(k == 2)
        def _():
            local_moments(out_ref[...], mask_ref, stats_ref, 0)

    return call(
        body,
        3,
        [
            full((rows, mid)),
            full(table.shape),
            full((rows, 1)),
            pl.BlockSpec((1, 3, mid, mid), lambda k: (number, k, 0, 0)),
            full((mid, mid)),
        ]
        + [full(payload(mid))] * size,
        [
            full((8, mid)),
            full((rows, mid // 2)),
            full((rows, mid // 2)),
            full((rows, mid)),
            full(payload(mid)),
        ],
        [
            near((8, mid)),
            near((rows, mid // 2)),
            near((rows, mid // 2)),
            near((rows, mid)),
            near(payload(mid)),
        ],
        [
            pltpu.VMEM((IMG_ROWS + 48, mid), F32),
            pltpu.VMEM((rows - IMG_ROWS + 16, mid), F32),
            pltpu.VMEM((9, rows, mid), BF),
        ],
        name="spatial_stage",
        flops=2 * rows * 9 * mid * mid,
    )(red, table, mask, w9, select, *members)


def expand_stage(number, spa, members, table, mask, w_expand):
    rows, mid = spa.shape
    d_in = w_expand.shape[2]
    size = len(members)

    def body(spa_ref, table_ref, mask_ref, w_ref, *refs):
        gain_ref, bias_ref = mid_rows(table_ref, number, 1)
        got, (mr_ref, hid_ref, out_ref, stats_ref) = refs[:size], refs[size:]
        k = pl.program_id(0)

        @pl.when(k == 0)
        def _():
            put_statistics(got, mr_ref)
            for stream, lo, hi in parts(rows):
                z = normed_of(spa_ref[lo:hi, :], mr_ref, stream) * gain_ref[...] + bias_ref[...]
                hid_ref[lo:hi, :] = rounded(z * sigmoid(z) * mask_ref[lo:hi, :])

        value = dot(hid_ref[...].astype(BF), w_ref[0])
        out_ref[...] = value
        local_moments(value, mask_ref, stats_ref, k * (CH // 128))

    return call(
        body,
        d_in // CH,
        [
            full((rows, mid)),
            full(table.shape),
            full((rows, 1)),
            pl.BlockSpec((1, mid, CH), lambda k: (number, 0, k)),
        ]
        + [full(payload(mid))] * size,
        [full((8, mid)), full((rows, mid)), cols(rows), full(payload(d_in))],
        [near((8, mid)), near((rows, mid)), far((rows, d_in)), near(payload(d_in))],
        name="expand_stage",
        flops=2 * rows * d_in * mid,
    )(spa, table, mask, w_expand, *members)


def pick(ref, k, stream, row):
    return ref[2 * stream + row : 2 * stream + row + 1, pl.ds(pl.multiple_of(k * CH, CH), CH)]


def normed_at(value, mr_ref, k, stream):
    return (value - pick(mr_ref, k, stream, 0)) * pick(mr_ref, k, stream, 1)


def join_stage(number, exp, members, table, act, mask, w_reduce):
    rows, d_in = exp.shape
    mid = w_reduce.shape[2]
    size = len(members)

    def body(exp_ref, table_ref, act_ref, mask_ref, w_ref, *refs):
        gain_ref, bias_ref = out_rows(table_ref, number - 1)
        got, (mr_ref, out_ref, low_ref, red_ref, stats_ref) = refs[:size], refs[size:]
        k = pl.program_id(0)

        @pl.when(k == 0)
        def _():
            put_statistics(got, mr_ref)

        for stream, lo, hi in parts(rows):
            z = (
                normed_at(exp_ref[lo:hi, :], mr_ref, k, stream) * gain_ref[...]
                + bias_ref[...]
                + act_ref[lo:hi, :].astype(F32)
            )
            out = z * sigmoid(z) * mask_ref[lo:hi, :]
            out_ref[lo:hi, :] = out
            low_ref[lo:hi, :] = rounded(out)
        part = dot(low_ref[...].astype(BF), w_ref[0])

        @pl.when(k == 0)
        def _():
            red_ref[...] = part

        @pl.when(k > 0)
        def _():
            red_ref[...] += part

        @pl.when(k == pl.num_programs(0) - 1)
        def _():
            local_moments(red_ref[...], mask_ref, stats_ref, 0)

    return call(
        body,
        d_in // CH,
        [
            cols(rows),
            cols(table.shape[0]),
            cols(rows),
            full((rows, 1)),
            pl.BlockSpec((1, CH, mid), lambda k: (number, k, 0)),
        ]
        + [full(payload(d_in))] * size,
        [full((8, d_in)), cols(rows), cols(rows), full((rows, mid)), full(payload(mid))],
        [near((8, d_in)), far((rows, d_in)), far((rows, d_in)), near((rows, mid)), near(payload(mid))],
        name="join_stage",
        flops=2 * rows * d_in * mid,
        transcendentals=rows * d_in,
    )(exp, table, act, mask, w_reduce, *members)


def put_places(value, image_ref, tile_ref):
    row = MAP * SLOTS
    for p in range(MAP):
        image_ref[p * row : (p + 1) * row, :] = value[p * MAPW * SLOTS : p * MAPW * SLOTS + row]
    tile_ref[...] = value[IMG_ROWS : IMG_ROWS + tile_ref.shape[0]]


def put_sums(stream, pre, normed, sums_ref, first=0):
    put_rows(sums_ref, 0, stream, jnp.sum(pre, axis=0, keepdims=True), first)
    put_rows(sums_ref, 1, stream, jnp.sum(pre * normed, axis=0, keepdims=True), first)


def turn_stage(number, exp, members, table, act, mask, grad, tile_rows):
    rows, d_in = exp.shape
    size = len(members)

    def body(exp_ref, table_ref, act_ref, mask_ref, grad_ref, *refs):
        gain_ref, bias_ref = out_rows(table_ref, number)
        got, (mr_ref, image_ref, tile_ref, pre_ref, sums_ref) = refs[:size], refs[size:]
        outs = []
        k = pl.program_id(0)

        @pl.when(k == 0)
        def _():
            put_statistics(got, mr_ref)

        for stream, lo, hi in parts(rows):
            n = normed_at(exp_ref[lo:hi, :], mr_ref, k, stream)
            z = n * gain_ref[...] + bias_ref[...] + act_ref[lo:hi, :].astype(F32)
            s = sigmoid(z)
            m = mask_ref[lo:hi, :]
            outs.append(z * s * m)
            pre = grad_ref[lo:hi, :].astype(F32) * m * (s * (1.0 + z * (1.0 - s)))
            pre_ref[lo:hi, :] = pre
            put_sums(stream, pre, n, sums_ref, k * (CH // 128))
        put_places(jnp.concatenate(outs, axis=0), image_ref, tile_ref)

    return call(
        body,
        d_in // CH,
        [cols(rows), cols(table.shape[0]), cols(rows), full((rows, 1)), cols(rows)]
        + [full(payload(d_in))] * size,
        [full((8, d_in)), cols(MAP * MAP * SLOTS), cols(tile_rows), cols(rows), full(payload(d_in, 2))],
        [
            near((8, d_in)),
            far((MAP * MAP * SLOTS, d_in)),
            far((tile_rows, d_in)),
            far((rows, d_in)),
            near(payload(d_in, 2)),
        ],
        name="turn_stage",
        flops=20 * rows * d_in,
        transcendentals=rows * d_in,
    )(exp, table, act, mask, grad, *members)


def norm_back(pre, normed, plain, cross, scale, mask):
    return mask * scale * (pre - plain - normed * cross)


def rows_of(ref, stream):
    return ref[2 * stream : 2 * stream + 1, :], ref[2 * stream + 1 : 2 * stream + 2, :]


def back_expand(number, me, pre3, exp, mr3, members, outer, mask, w_expand, spa, mr2, table):
    rows, d_in = exp.shape
    mid = spa.shape[1]
    half = d_in // 2
    size = len(members)

    def body(me_ref, pre3_ref, exp_ref, mr3_ref, outer_ref, mask_ref, w_ref, spa_ref, mr2_ref, table_ref, *refs):
        gain3_ref, _ = out_rows(outer_ref, number)
        gain2_ref, bias2_ref = mid_rows(table_ref, number, 1)
        got, (both_ref, keep_ref, send_ref, pre2_ref, sums_ref, share, grad) = refs[:size], refs[size:]
        k = pl.program_id(0)

        @pl.when(k == 0)
        def _():
            put_shares(got, mr3_ref, share, both_ref)

        for stream, lo, hi in parts(rows):
            n = normed_at(exp_ref[lo:hi, :], mr3_ref, k, stream)
            grad[lo:hi, :] = norm_back(
                pre3_ref[lo:hi, :],
                n,
                pick(share, k, stream, 0),
                pick(share, k, stream, 1),
                gain3_ref[...] * pick(mr3_ref, k, stream, 1),
                mask_ref[lo:hi, :],
            ).astype(BF)
        per_half = half // CH
        at = pl.ds(pl.multiple_of(lax.rem(k, per_half) * CH, CH), CH)
        mine = k // per_half == me_ref[0]

        @pl.when(mine)
        def _():
            keep_ref[:, at] = grad[...].astype(F32)

        @pl.when(jnp.logical_not(mine))
        def _():
            send_ref[:, at] = grad[...].astype(F32)

        part = dot_nt(grad[...], w_ref[0])

        @pl.when(k == 0)
        def _():
            pre2_ref[...] = part

        @pl.when(k > 0)
        def _():
            pre2_ref[...] += part

        @pl.when(k == pl.num_programs(0) - 1)
        def _():
            for stream, lo, hi in parts(rows):
                n2 = normed_of(spa_ref[lo:hi, :], mr2_ref, stream)
                z2 = n2 * gain2_ref[...] + bias2_ref[...]
                pre2 = pre2_ref[lo:hi, :] * mask_ref[lo:hi, :] * slope(z2)
                pre2_ref[lo:hi, :] = pre2
                put_sums(stream, pre2, n2, sums_ref)

    return call(
        body,
        d_in // CH,
        [
            smem(),
            cols(rows),
            cols(rows),
            full((8, d_in)),
            cols(outer.shape[0]),
            full((rows, 1)),
            pl.BlockSpec((1, mid, CH), lambda k: (number, 0, k)),
            full((rows, mid)),
            full((8, mid)),
            full(table.shape),
        ]
        + [full(payload(d_in, 2))] * size,
        [full((2, d_in)), full((rows, half)), full((rows, half)), full((rows, mid)), full(payload(mid, 2))],
        [near((2, d_in)), near((rows, half)), near((rows, half)), near((rows, mid)), near(payload(mid, 2))],
        [pltpu.VMEM((4, d_in), F32), pltpu.VMEM((rows, CH), BF)],
        name="back_expand",
        flops=2 * rows * d_in * mid,
    )(me, pre3, exp, mr3, outer, mask, w_expand, spa, mr2, table, *members)


def back_spatial(number, me, pre2, spa, mr2, members, table, mask, w9, red, mr1):
    rows, mid = spa.shape
    size = len(members)
    quarter = mid // 4

    def body(me_ref, pre2_ref, spa_ref, mr2_ref, table_ref, mask_ref, w_ref, red_ref, mr1_ref, *refs):
        gain2_ref, _ = mid_rows(table_ref, number, 1)
        gain1_ref, bias1_ref = mid_rows(table_ref, number, 0)
        got, rest = refs[:size], refs[size:]
        both_ref, gs0, gs1, gs2, gs3, pre1_ref, sums_ref, share, image, tile, patch = rest
        k = pl.program_id(0)

        @pl.when(k == 0)
        def _():
            put_shares(got, mr2_ref, share, both_ref)
            pieces = []
            for stream, lo, hi in parts(rows):
                n = normed_of(spa_ref[lo:hi, :], mr2_ref, stream)
                plain, cross = rows_of(share, stream)
                scale = gain2_ref[...] * mr2_ref[2 * stream + 1 : 2 * stream + 2, :]
                pieces.append(norm_back(pre2_ref[lo:hi, :], n, plain, cross, scale, mask_ref[lo:hi, :]))
            value = rounded(jnp.concatenate(pieces, axis=0))
            fill_patches(value, image, tile, patch, -1)
            pre1_ref[...] = value
            for m, ref in enumerate((gs0, gs1, gs2, gs3)):
                at = pl.ds(pl.multiple_of((me_ref[1] ^ m) * quarter, quarter), quarter)
                ref[...] = pre1_ref[:, at]
            pre1_ref[...] = jnp.zeros((rows, mid), F32)

        total = pre1_ref[...]
        for j in range(3):
            total += dot_nt(patch[3 * k + j], w_ref[0, j])
        pre1_ref[...] = total

        @pl.when(k == 2)
        def _():
            for stream, lo, hi in parts(rows):
                n1 = normed_of(red_ref[lo:hi, :], mr1_ref, stream)
                z1 = n1 * gain1_ref[...] + bias1_ref[...]
                pre1 = pre1_ref[lo:hi, :] * mask_ref[lo:hi, :] * slope(z1)
                pre1_ref[lo:hi, :] = pre1
                put_sums(stream, pre1, n1, sums_ref)

    return call(
        body,
        3,
        [
            smem(),
            full((rows, mid)),
            full((rows, mid)),
            full((8, mid)),
            full(table.shape),
            full((rows, 1)),
            pl.BlockSpec((1, 3, mid, mid), lambda k: (number, k, 0, 0)),
            full((rows, mid)),
            full((8, mid)),
        ]
        + [full(payload(mid, 2))] * size,
        [full((2, mid))] + [full((rows, quarter))] * 4 + [full((rows, mid)), full(payload(mid, 2))],
        [near((2, mid))] + [near((rows, quarter))] * 4 + [near((rows, mid)), near(payload(mid, 2))],
        [
            pltpu.VMEM((4, mid), F32),
            pltpu.VMEM((IMG_ROWS + 48, mid), F32),
            pltpu.VMEM((rows - IMG_ROWS + 16, mid), F32),
            pltpu.VMEM((9, rows, mid), BF),
        ],
        name="back_spatial",
        flops=2 * rows * 9 * mid * mid,
    )(me, pre2, spa, mr2, table, mask, w9, red, mr1, *members)


def back_reduce(number, pre1, red, mr1, members, table, mask, w_reduce, pre3, below, tile_rows):
    rows, mid = red.shape
    d_in = pre3.shape[1]
    size = len(members)

    def head(k, got, pre1_ref, red_ref, mr1_ref, table_ref, mask_ref, both_ref, gr_ref, share, low):
        gain1_ref, _ = mid_rows(table_ref, number, 0)

        @pl.when(k == 0)
        def _():
            put_shares(got, mr1_ref, share, both_ref)
            for stream, lo, hi in parts(rows):
                n = normed_of(red_ref[lo:hi, :], mr1_ref, stream)
                plain, cross = rows_of(share, stream)
                scale = gain1_ref[...] * mr1_ref[2 * stream + 1 : 2 * stream + 2, :]
                low[lo:hi, :] = norm_back(pre1_ref[lo:hi, :], n, plain, cross, scale, mask_ref[lo:hi, :]).astype(BF)
            gr_ref[...] = low[...].astype(F32)

    specs = [
        full((rows, mid)),
        full((rows, mid)),
        full((8, mid)),
        full(table.shape),
        full((rows, 1)),
        pl.BlockSpec((1, CH, mid), lambda k: (number, k, 0)),
        cols(rows),
    ]
    args = [pre1, red, mr1, table, mask, w_reduce, pre3]
    scratch = [pltpu.VMEM((4, mid), F32), pltpu.VMEM((rows, mid), BF)]
    if below is None:

        def body(pre1_ref, red_ref, mr1_ref, table_ref, mask_ref, w_ref, pre3_ref, *refs):
            got, (both_ref, gr_ref, image_ref, tile_ref, share, low) = refs[:size], refs[size:]
            k = pl.program_id(0)
            head(k, got, pre1_ref, red_ref, mr1_ref, table_ref, mask_ref, both_ref, gr_ref, share, low)
            put_places(pre3_ref[...] + dot_nt(low[...], w_ref[0]), image_ref, tile_ref)

        return call(
            body,
            d_in // CH,
            specs + [full(payload(mid, 2))] * size,
            [full((2, mid)), full((rows, mid)), cols(MAP * MAP * SLOTS), cols(tile_rows)],
            [near((2, mid)), near((rows, mid)), far((MAP * MAP * SLOTS, d_in)), far((tile_rows, d_in))],
            scratch,
            name="back_reduce_last",
            flops=2 * rows * d_in * mid,
        )(*args, *members)

    def body(pre1_ref, red_ref, mr1_ref, table_ref, mask_ref, w_ref, pre3_ref, exp_ref, mr3_ref, outer_ref, act_ref, *refs):
        gain3_ref, bias3_ref = out_rows(outer_ref, number - 1)
        got, (both_ref, gr_ref, out_ref, sums_ref, share, low) = refs[:size], refs[size:]
        k = pl.program_id(0)
        head(k, got, pre1_ref, red_ref, mr1_ref, table_ref, mask_ref, both_ref, gr_ref, share, low)
        grad = pre3_ref[...] + dot_nt(low[...], w_ref[0])
        for stream, lo, hi in parts(rows):
            n = normed_at(exp_ref[lo:hi, :], mr3_ref, k, stream)
            z = n * gain3_ref[...] + bias3_ref[...] + act_ref[lo:hi, :].astype(F32)
            pre = grad[lo:hi] * mask_ref[lo:hi, :] * slope(z)
            out_ref[lo:hi, :] = pre
            put_sums(stream, pre, n, sums_ref, k * (CH // 128))

    return call(
        body,
        d_in // CH,
        specs + [cols(rows), full((8, d_in)), cols(below[2].shape[0]), cols(rows)] + [full(payload(mid, 2))] * size,
        [full((2, mid)), full((rows, mid)), cols(rows), full(payload(d_in, 2))],
        [near((2, mid)), near((rows, mid)), far((rows, d_in)), near(payload(d_in, 2))],
        scratch,
        name="back_reduce",
        flops=2 * rows * d_in * mid,
        transcendentals=rows * d_in,
    )(*args, *below, *members)


def dot_tn(a, b):
    return lax.dot_general(a, b, (((0,), (0,)), ((), ())), preferred_element_type=F32)


def spot(index, size):
    place, bit = 0, 1
    while bit < size:
        place = place * 2 + (index // bit) % 2
        bit *= 2
    return place


def weight_halves(body, args, shape, scratch, flops, name):
    vmem = pl.BlockSpec(memory_space=pltpu.VMEM)
    return pl.pallas_call(
        body,
        in_specs=[smem()] + [vmem] * 4,
        out_specs=[vmem] * 4,
        out_shape=[sds(shape)] * 4,
        scratch_shapes=list(scratch),
        compiler_params=pltpu.CompilerParams(vmem_limit_bytes=VMEM_LIMIT),
        cost_estimate=pl.CostEstimate(flops=0, bytes_accessed=0, transcendentals=0),
        name=name,
    )(*args)


def weight_expand(me, own, peer, keep, got, nz):
    rows, mid = own.shape
    step = keep.shape[1] // 4
    deep = mid // nz

    def body(me_ref, own_ref, peer_ref, keep_ref, got_ref, x_keep, x_send, y_keep, y_send):
        a = jnp.concatenate([own_ref[...].astype(BF), peer_ref[...].astype(BF)], axis=0)
        for m in range(4):
            at = pl.ds(pl.multiple_of((me_ref[3] ^ m) * step, step), step)
            b = jnp.concatenate([keep_ref[:, at].astype(BF), got_ref[:, at].astype(BF)], axis=0)
            value = dot_tn(a, b)
            x_ref = x_keep if m < 2 else x_send
            y_ref = y_keep if m % 2 == 0 else y_send
            for z in range(nz):
                place = spot(me_ref[2] ^ z, nz)
                x_ref[m % 2, place] = value[z * deep : (z + 1) * deep, 0:128]
                y_ref[m // 2, place] = value[z * deep : (z + 1) * deep, 128:256]

    return weight_halves(body, (me, own, peer, keep, got), (2, nz, deep, 128), (), 0, "weight_expand")


def weight_reduce(me, own, peer, keep, got, nz):
    rows, width = own.shape
    mid = keep.shape[1]
    step = mid // 4
    deep = width // nz
    part = deep // 2

    def body(me_ref, own_ref, peer_ref, keep_ref, got_ref, x_keep, x_send, y_keep, y_send, total):
        b = jnp.concatenate([keep_ref[...].astype(BF), got_ref[...].astype(BF)], axis=0)
        for z in range(nz):
            at = slice(z * deep, (z + 1) * deep)
            a = jnp.concatenate([own_ref[:, at].astype(BF), peer_ref[:, at].astype(BF)], axis=0)
            total[...] = dot_tn(a, b)
            place = spot(me_ref[2] ^ z, nz)
            for m in range(4):
                column = me_ref[1] ^ ((m % 2) * 2 + m // 2)
                value = total[:, pl.ds(pl.multiple_of(column * step, step), step)]
                (x_keep if m < 2 else x_send)[m % 2, place] = value[:part]
                (y_keep if m % 2 == 0 else y_send)[m // 2, place] = value[part:]

    return weight_halves(
        body, (me, own, peer, keep, got), (2, nz, part, step), [pltpu.VMEM((deep, mid), F32)], 0, "weight_reduce"
    )


def weight_spatial(me, hidden, near, far, nz):
    both, half = hidden[0].shape
    rows = both // 2
    width = near[0].shape[1]
    deep = half // nz
    tile_rows = rows - IMG_ROWS

    def body(me_ref, h0, h1, h2, h3, h4, n0, n1, n2, n3, far_ref, keep_ref, send_ref, image, tile, left, patch, total):
        image[...] = jnp.zeros_like(image)
        tile[...] = jnp.zeros_like(tile)
        for m, ref in enumerate((h0, h1, h2)):
            left[m * both : (m + 1) * both, :] = ref[...].astype(BF)
        left[3 * both : 3 * both + rows, :] = h3[...].astype(BF)
        left[3 * both + rows :, :] = h4[...].astype(BF)
        for m, n_ref in enumerate((n0, n1, n2, n3)):
            for core in range(2):
                value = n_ref[...] if core == 0 else far_ref[m]
                at = m * both + core * rows
                image[24 : 24 + IMG_ROWS, :] = value[0:IMG_ROWS]
                tile[8 : 8 + tile_rows, :] = value[IMG_ROWS:rows]
                for tap in range(9):
                    dy, dx = tap // 3 - 1, tap % 3 - 1
                    part, rest = shifted(image, tile, -dy, -dx, tile_rows)
                    patch[at : at + IMG_ROWS, tap * width : (tap + 1) * width] = part.astype(BF)
                    patch[at + IMG_ROWS : at + rows, tap * width : (tap + 1) * width] = rest.astype(BF)
        total[...] = dot_tn(left[...], patch[...])
        for p in range(nz):
            z = me_ref[2] ^ spot(p, nz)
            value = total[pl.ds(pl.multiple_of(z * deep, deep), deep), :]
            ref, at = (keep_ref, p) if p < nz // 2 else (send_ref, p - nz // 2)
            for tap in range(9):
                ref[at, tap] = value[:, tap * width : (tap + 1) * width]

    vmem = pl.BlockSpec(memory_space=pltpu.VMEM)
    return pl.pallas_call(
        body,
        in_specs=[smem()] + [vmem] * 10,
        out_specs=[vmem] * 2,
        out_shape=[sds((nz // 2, 9, deep, width))] * 2,
        scratch_shapes=[
            pltpu.VMEM((IMG_ROWS + 48, width), F32),
            pltpu.VMEM((tile_rows + 16, width), F32),
            pltpu.VMEM((4 * both, half), BF),
            pltpu.VMEM((4 * both, 9 * width), BF),
            pltpu.VMEM((half, 9 * width), F32),
        ],
        compiler_params=pltpu.CompilerParams(vmem_limit_bytes=VMEM_LIMIT),
        cost_estimate=pl.CostEstimate(flops=0, bytes_accessed=0, transcendentals=0),
        name="weight_spatial",
    )(me, *hidden, *near, far)


class Collect:
    def __init__(self, grid, me):
        self.grid, self.me, self.marks = grid, me, None

    def over_z(self, keep, send, gate=None):
        step = 1
        while True:
            (got,) = yield "deep", [(send, dict(dz=step))]
            step *= 2
            if step == self.grid.z:
                if gate and len(gate) > 2:
                    got, _ = lax.optimization_barrier((got, gate[2]))
                return keep[0] + got[0]
            half = keep.shape[0] // 2
            keep, send = keep[:half] + got[:half], keep[half:] + got[half:]

    def chips(self, pieces, out):
        flat = jnp.concatenate([p.reshape(-1, 128) for p in pieces])
        for group in self.grid.far():
            flat = flat + sum(self.grid.swap(flat, **step) for step in group)
        got = yield "plane", [(flat, dict(dx=1)), (flat, dict(dy=1)), (flat, dict(dy=1, dx=1))]
        out.extend([flat] + list(got))

    def by_halves(self, kernel, own, peer, keep, send, out, after=None, gate=None, kind="plane"):
        (got,) = yield "core", [(send, dict(dc=1))]
        if after:
            got, _ = lax.optimization_barrier((got, after[0]))
        x_keep, x_send, y_keep, y_send = kernel(self.me, own, peer, keep, got, self.grid.z)
        self.begun = x_keep
        got = yield kind, [(x_send, dict(dx=1)), (y_send, dict(dy=1))]
        got = lax.optimization_barrier(tuple(got))
        if after is not None:
            after.append(got[0])
        x_last, y_last = x_keep[1:] + got[0][1:], y_keep[1:] + got[1][1:]
        x_keep, y_keep = x_keep[:1] + got[0][:1], y_keep[:1] + got[1][:1]
        got = yield "plane", [(x_last, dict(dy=1)), (y_last, dict(dx=1))]
        if after is not None:
            after.append(got[0])
        half = self.grid.z // 2

        def side(at):
            return jnp.concatenate([x_keep[0, at] + got[0][0, at], y_keep[0, at] + got[1][0, at]], axis=1)

        piece = yield from self.over_z(side(slice(0, half)), side(slice(half, 2 * half)), gate)
        out.append(piece)

    def by_rows(self, hidden, grad, out, after=None):
        got = yield "tight", [(grad[1], dict(dx=1)), (grad[2], dict(dy=1)), (grad[3], dict(dy=1, dx=1))]
        near = [grad[0]] + list(got)
        (far,) = yield "core", [(jnp.stack(near), dict(dc=1))]
        keep, send = weight_spatial(self.me, hidden, near, far, self.grid.z)
        if after is not None:
            after.append(keep)
        piece = yield from self.over_z(keep, send, after)
        out.append(piece)

    def hidden(self, keep, send, out):
        (got,) = yield "core", [(send, dict(dc=1))]
        value = jnp.concatenate([keep, got], axis=0)
        got = yield "plane", [(value, dict(dx=1)), (value, dict(dy=1))]
        rows = keep.shape[0]
        last = yield "tight", [(got[0][:rows], dict(dy=1)), (got[1][rows:], dict(dx=1))]
        out.extend([value, got[0], got[1], last[0], last[1]])


def place_slices(me, gathered, shapes):
    (e_rows, d_in), (r_rows, mid), (s_rows, _) = shapes
    dims = ((BLOCKS, r_rows, mid), (BLOCKS, 9, s_rows, mid), (BLOCKS, e_rows, d_in))
    size = 8 * BLOCKS
    r_len, s_len = r_rows // 2, s_rows // 2

    def body(me_ref, *refs):
        got = refs[:size]
        outs, (red, spa, exp, sems, out_sems) = refs[-8:-5], refs[-5:]
        copies = [[] for _ in range(BLOCKS)]
        for b in range(BLOCKS):
            for a in range(8):
                core = me_ref[0] if a < 4 else 1 - me_ref[0]
                chip = (a % 4) ^ me_ref[1]
                source = got[8 * b + a]
                column = core * 4 + (chip % 2) * 2 + chip // 2
                moves = []
                for t in range(2):
                    at = pl.multiple_of(column * 256 + t * 128, 128)
                    moves.append((source.at[pl.ds(t * e_rows, e_rows), :], exp.at[b, :, pl.ds(at, 128)]))
                at = pl.multiple_of(chip * 128, 128)
                row = pl.multiple_of(core * r_len, r_len)
                start = 2 * e_rows
                moves.append((source.at[pl.ds(start, r_len), :], red.at[b, pl.ds(row, r_len), pl.ds(at, 128)]))
                row = pl.multiple_of(core * s_len, s_len)
                start = 2 * e_rows + r_len
                taps = source.at[pl.ds(start, 9 * s_len), :].reshape(9, s_len, 128)
                moves.append((taps, spa.at[b, :, pl.ds(row, s_len), pl.ds(at, 128)]))
                copies[b] += [
                    pltpu.make_async_copy(src, dst, sems.at[b, a, i]) for i, (src, dst) in enumerate(moves)
                ]
        last = []
        for copy in copies[0] + copies[1]:
            copy.start()
        for b in range(BLOCKS):
            for copy in copies[b]:
                copy.wait()
            for i, (src, dst) in enumerate(zip((red, spa, exp), outs)):
                copy = pltpu.make_async_copy(src.at[b], dst.at[b], out_sems.at[b, i])
                copy.start()
                last.append(copy)
        for copy in last:
            copy.wait()

    anywhere = pl.BlockSpec(memory_space=pl.ANY)
    return pl.pallas_call(
        body,
        in_specs=[smem()] + [anywhere] * size,
        out_specs=[anywhere] * 3,
        out_shape=[sds(d) for d in dims],
        scratch_shapes=[pltpu.VMEM(d, F32) for d in dims]
        + [pltpu.SemaphoreType.DMA((BLOCKS, 8, 4)), pltpu.SemaphoreType.DMA((BLOCKS, 3))],
        compiler_params=pltpu.CompilerParams(vmem_limit_bytes=VMEM_LIMIT),
        name="place_slices",
    )(me, *gathered)


def to_rows(image, tile, rows):
    width = image.shape[-1]
    image = jnp.transpose(image, (1, 2, 0, 3))
    image = jnp.pad(image, ((0, 0), (0, 1), (0, 0), (0, 0))).reshape(IMG_ROWS, width)
    tile = tile.reshape(-1, width)
    pad = jnp.zeros((rows - IMG_ROWS - tile.shape[0], width), tile.dtype)
    return jnp.concatenate([image, tile, pad], axis=0)


def from_rows(image, tile):
    width = image.shape[1]
    image = jnp.transpose(image.reshape(MAP, MAP, SLOTS, width), (2, 0, 1, 3))
    return image, tile.reshape(-1, TILE, TILE, width)


def core_halves(value, core, nz):
    deep = value.shape[1] // (2 * nz)
    low = [value[:, 2 * z * deep : (2 * z + 1) * deep] for z in range(nz)]
    high = [value[:, (2 * z + 1) * deep : (2 * z + 2) * deep] for z in range(nz)]
    low, high = jnp.concatenate(low, axis=1), jnp.concatenate(high, axis=1)
    keep = jnp.where(core == 0, low, high).astype(F32)
    send = jnp.where(core == 0, high, low).astype(F32)
    return keep, send


def core_select(core, mid, nz):
    deep = mid // (2 * nz)
    at = jnp.arange(mid)
    side = at // (mid // 2)
    inner = at % (mid // 2)
    source = (inner // deep) * 2 * deep + (side ^ core) * deep + inner % deep
    return (jnp.arange(mid)[:, None] == source[None, :]).astype(BF)


def per_device(
    grid,
    images,
    tile_maps,
    map_sizes,
    w_reduce,
    w_spatial,
    w_expand,
    gain_mid,
    bias_mid,
    gain_out,
    bias_out,
    grad_images,
    grad_tiles,
):
    tiles = tile_maps.shape[0]
    rows = -(-(IMG_ROWS + tiles * TILE * TILE) // 16) * 16
    d_in, mid = w_reduce.shape[1:]
    nz = grid.z
    y, x, core, z = grid.index()
    chip = (y % 2) * 2 + x % 2
    turned = (x % 2) * 2 + y % 2
    me = jnp.stack([core, chip, z, turned]).astype(jnp.int32)
    w9 = w_spatial.reshape(BLOCKS, 9, mid, mid)
    start = to_rows(images, tile_maps, rows)
    select = core_select(core, mid, nz)
    collect = Collect(grid, me)
    bulk = Bulk(grid, ROOM)

    table = stay(jnp.concatenate([gain_mid.reshape(-1, mid), bias_mid.reshape(-1, mid)]))
    outer = stay(jnp.concatenate([gain_out, bias_out]))
    w_reduce, w9, w_expand = (pltpu.with_memory_space_constraint(w, pltpu.HBM) for w in (w_reduce, w9, w_expand))

    def moments(stats):
        return exchange(grid, bulk, stats, join_moments)

    def sums(value):
        return exchange(grid, bulk, value, add_members)

    acts, lows, reds, spas, exps = [start], [], [], [], []
    mr1, mr2, mr3, hid1, hid2 = [], [], [], [], []
    mask, red, stats = reduce_first(start, w_reduce, map_sizes)
    grad_images, grad_tiles, stats = lax.optimization_barrier((grad_images, grad_tiles, stats))
    grad = to_rows(grad_images, grad_tiles, rows)
    low = start
    for b in range(BLOCKS):
        reds.append(red)
        mr, keep, send, spa, stats = spatial_stage(
            b, red, moments(stats), table, mask, w9, select
        )
        mr1.append(mr)
        if b == 0:
            stats, grad = lax.optimization_barrier((stats, grad))
        hid1.append([])
        bulk.add(("h", b), collect.hidden(keep, send, hid1[b]))
        keep, send = core_halves(low, core, nz)
        peer = grid.swap(send, dc=1)
        stats, keep, peer = lax.optimization_barrier((stats, keep, peer))
        lows.append((keep, peer))
        spas.append(spa)
        mr, hidden, exp, stats = expand_stage(
            b, spa, moments(stats), table, mask, w_expand
        )
        mr2.append(mr)
        hid2.append((hidden, grid.swap(hidden, dc=1)))
        exp = away(exp)
        exps.append(exp)
        if b + 1 < BLOCKS:
            mr, out, low, red, stats = join_stage(
                b + 1, exp, moments(stats), outer, acts[b], mask, w_reduce
            )
            mr3.append(mr)
            acts.append(away(out))
    last = BLOCKS - 1
    mr, *out, pre3, sums3 = turn_stage(
        last, exps[last], moments(stats), outer, acts[last], mask, grad, tiles * TILE * TILE
    )
    mr3.append(mr)
    pre3 = away(pre3)

    both1, both2, both3 = [None] * BLOCKS, [None] * BLOCKS, [None] * BLOCKS
    shapes = ((mid // nz, d_in), (d_in // nz, mid), (mid // nz, mid))
    pieces = [([], [], []) for _ in range(BLOCKS)]
    after = []
    for b in reversed(range(BLOCKS)):
        both3[b], keep, send, pre2, sums2 = back_expand(
            b, me, pre3, exps[b], mr3[b], sums(sums3), outer, mask, w_expand,
            spas[b], mr2[b], table,
        )
        bulk.add(("e", b), collect.by_halves(weight_expand, *hid2[b], keep, send, pieces[b][0]))
        both2[b], *gs, pre1, sums1 = back_spatial(
            b, me, pre2, spas[b], mr2[b], sums(sums2), table, mask, w9,
            reds[b], mr1[b],
        )
        bulk.add(("s", b), collect.by_rows(hid1[b], gs, pieces[b][2], after if b == 0 else None))
        below = None
        if b > 0:
            below = (exps[b - 1], mr3[b - 1], outer, acts[b - 1])
        result = back_reduce(
            b, pre1, reds[b], mr1[b], sums(sums1), table, mask, w_reduce, pre3, below, tiles * TILE * TILE
        )
        both1[b] = result[0]
        gr = result[1]
        reduce_flow = collect.by_halves(
            weight_reduce, *lows[b], gr, gr, pieces[b][1], after if b == 0 else None, after if b else None
        )
        if b > 0:
            bulk.add(("r", b), reduce_flow)
        if b > 0:
            pre3, sums3 = away(result[2]), result[3]
        else:
            grad_in = list(result[2:4])

    grad_in[0] = bulk.last(grad_in[0], [("s", 0)])
    bulk.add(("r", 0), reduce_flow)
    later = [(n, b) for b in range(1, BLOCKS) for n in "ers"]
    every = later + [("e", 0)]
    bulk.hold(later, collect.begun)
    bulk.resume(later, collect.begun)
    bulk.run([("r", 0)], ("plane",), 1)
    bulk.resume([("e", 0)], after[1])
    bulk.hold([("e", 0)], after[1])
    bulk.run([("r", 0)], ("plane",))
    bulk.run([("s", 0)])
    bulk.run(every, ("deep",))
    views = []
    for value in (*out, *grad_in):
        value, _ = lax.optimization_barrier((value, after[2]))
        views.append(value)
    views = from_rows(*views[:2]) + from_rows(*views[2:])
    bulk.run(every)
    gathered = [[] for _ in range(BLOCKS)]
    for b in range(1, BLOCKS):
        bulk.add(("g", b), collect.chips([p[0] for p in pieces[b]], gathered[b]))
        bulk.hold([("g", b)], after[2])
        bulk.run([("g", b)])
    bulk.run([("r", 0)])
    bulk.add(("g", 0), collect.chips([p[0] for p in pieces[0]], gathered[0]))
    bulk.run([("g", 0)])
    *views, gathered[0][1] = lax.optimization_barrier((*views, gathered[0][1]))
    final = []
    for b in range(BLOCKS):
        final += gathered[b] + [grid.swap(v, dc=1) for v in gathered[b]]
    final = [pltpu.with_memory_space_constraint(v, pltpu.HBM) for v in final]
    slices = place_slices(me, final, shapes)
    out_images, out_tiles, in_images, in_tiles = views
    g_reduce, g_spatial, g_expand = slices

    def pair(at):
        return jnp.stack([jnp.stack([both1[b][at], both2[b][at]]) for b in range(BLOCKS)])

    return (
        out_images,
        out_tiles,
        in_images,
        in_tiles,
        g_reduce,
        g_spatial.reshape(BLOCKS, 3, 3, mid // nz, mid),
        g_expand,
        pair(1),
        pair(0),
        jnp.stack([both3[b][1] for b in range(BLOCKS)]),
        jnp.stack([both3[b][0] for b in range(BLOCKS)]),
    )


def solution(mesh):
    both = ("wide", "narrow")
    batch = P(both, None, None, None)
    grid = Grid(mesh.shape["wide"], mesh.shape["narrow"])
    return jax.shard_map(
        functools.partial(per_device, grid),
        mesh=mesh,
        in_specs=(batch, batch, P(both), P(), P(), P(), P(), P(), P(), P(), batch, batch),
        out_specs=(
            batch,
            batch,
            batch,
            batch,
            P(None, "narrow", None),
            P(None, None, None, "narrow", None),
            P(None, "narrow", None),
            P(),
            P(),
            P(),
            P(),
        ),
        check_vma=False,
    )
```

```python
import functools

import jax
import jax.numpy as jnp
from jax import lax
from jax.experimental import pallas as pl
from jax.experimental.pallas import tpu as pltpu
from jax.sharding import PartitionSpec as P

BLOCKS = 2
MAP = 7
MAPW = 8
TILE = 2
PIECES = 9
SLOTS = 2
IMG_ROWS = MAP * MAPW * SLOTS
EPS = 1e-05
CH = 512
BF = jnp.bfloat16
F32 = jnp.float32
VMEM_LIMIT = 16 * 1024 * 1024
AXES = ("wide", "narrow")
ROOM = 640 * 1024


class Grid:
    def __init__(self, wide, narrow):
        chips = wide // 2
        side = 1
        while side * side < chips:
            side *= 2
        self.y, self.x, self.c, self.z = chips // side, side, 2, narrow

    def index(self):
        wide = lax.axis_index("wide")
        core = wide % 2
        chip = wide // 2
        return chip // self.x, chip % self.x, core, lax.axis_index("narrow")

    def swap(self, value, dy=0, dx=0, dc=0, dz=0):
        pairs = []
        for y in range(self.y):
            for x in range(self.x):
                for c in range(self.c):
                    for z in range(self.z):
                        src = ((y * self.x + x) * 2 + c) * self.z + z
                        dst = (((y ^ dy) * self.x + (x ^ dx)) * 2 + (c ^ dc)) * self.z + (z ^ dz)
                        pairs.append((src, dst))
        return lax.ppermute(value, AXES, pairs)

    def plane(self, value):
        if self.y * self.x == 4:
            return lax.all_gather(value, "wide")
        groups = {}
        for y in range(self.y):
            for x in range(self.x):
                for c in range(2):
                    groups.setdefault((y // 2, x // 2), []).append((y * self.x + x) * 2 + c)
        return lax.all_gather(value, "wide", axis_index_groups=list(groups.values()))

    def phases(self):
        found = [[dict(dc=1)]]
        step = 1
        while step < max(self.x, self.y):
            group = []
            for dy in (0, step):
                for dx in (0, step):
                    if (dy or dx) and dy < self.y and dx < self.x:
                        group.append(dict(dy=dy, dx=dx))
            found.append(group)
            step *= 2
        self.far_groups = found[2:]
        found.append([dict(dz=k) for k in range(1, min(self.z, 4))])
        step = 4
        while step < self.z:
            found.append([dict(dz=step)])
            step *= 2
        return found

    def far(self):
        self.phases()
        return self.far_groups


class Bulk:
    def __init__(self, grid, room):
        self.grid, self.room = grid, room
        self.waiting = []
        self.flying = {"plane": [], "tight": [], "deep": [], "spare": []}
        self.late = []
        self.names = {}

    def move(self, value, step):
        return step(value) if callable(step) else self.grid.swap(value, **step)

    def add(self, name, flow):
        self.names[flow] = name
        self.advance(flow, None)

    def advance(self, flow, value):
        while True:
            try:
                kind, pieces = flow.send(value)
            except StopIteration:
                return
            if kind != "core":
                self.waiting.append((flow, kind, pieces))
                return
            value = [self.move(v, step) for v, step in pieces]

    def load(self, pieces):
        used = {}
        for value, step in pieces:
            for name in () if callable(step) else step:
                used[name] = used.get(name, 0) + value.size * 4
        return used

    def open(self, kinds, arrays):
        used, chosen, rest = {}, [], []
        for item in self.waiting:
            if item[1] in kinds:
                load = self.load(item[2])
                if all(used.get(n, 0) + load[n] <= self.room for n in load):
                    for n in load:
                        used[n] = used.get(n, 0) + load[n]
                    chosen.append(item)
                    continue
                for n in load:
                    used[n] = max(used.get(n, 0), self.room)
            rest.append(item)
        self.waiting = rest
        if not chosen:
            return arrays
        values = [v for _, _, pieces in chosen for v, _ in pieces]
        tied = lax.optimization_barrier(tuple(arrays) + tuple(values))
        arrays, values = list(tied[: len(arrays)]), list(tied[len(arrays) :])
        for flow, kind, pieces in chosen:
            got = [self.move(values.pop(0), step) for _, step in pieces]
            self.flying[kind].append((flow, got))
        return arrays

    def close(self, kind, array):
        done = self.flying[kind]
        self.flying[kind] = []
        if kind == "deep":
            done = done + self.late
            self.late, self.flying["spare"] = self.flying["spare"], []
        if not done:
            return array
        values = [v for _, got in done for v in got]
        tied = lax.optimization_barrier((array,) + tuple(values))
        array, values = tied[0], list(tied[1:])
        for flow, got in done:
            self.advance(flow, [values.pop(0) for _ in got])
        return array

    def last(self, array, first):
        done = self.flying["plane"] + self.flying["deep"]
        self.flying = {"plane": [], "tight": [], "deep": [], "spare": []}
        values = [v for _, got in done for v in got]
        tied = lax.optimization_barrier((array,) + tuple(values))
        array, values = tied[0], list(tied[1:])
        self.parked = []
        for flow, got in done:
            got = [values.pop(0) for _ in got]
            if self.names[flow] in first:
                self.advance(flow, got)
            else:
                self.parked.append((flow, got))
        return array

    def resume(self, names, after):
        parked, self.parked = self.parked, []
        for flow, got in parked:
            if self.names[flow] not in names:
                self.parked.append((flow, got))
                continue
            *got, _ = lax.optimization_barrier((*got, after))
            self.advance(flow, got)

    def hold(self, names, after):
        held = [item for item in self.waiting if self.names[item[0]] in names]
        if not held:
            return
        values = [v for _, _, pieces in held for v, _ in pieces]
        *values, _ = lax.optimization_barrier((*values, after))
        fresh = {}
        for flow, kind, pieces in held:
            fresh[flow] = (flow, kind, [(values.pop(0), step) for _, step in pieces])
        self.waiting = [fresh.get(item[0], item) for item in self.waiting]

    def run(self, names, kinds=("plane", "deep"), rounds=9, tie=None):
        for _ in range(rounds):
            batch = [i for i in self.waiting if self.names[i[0]] in names and i[1] in kinds]
            if not batch:
                return tie
            self.waiting = [i for i in self.waiting if i not in batch]
            for flow, kind, pieces in batch:
                got = [self.move(v, step) for v, step in pieces]
                if tie is not None:
                    tied = lax.optimization_barrier((*got, *tie))
                    got, tie = list(tied[: len(got)]), list(tied[len(got) :])
                self.advance(flow, got)
        return tie


def exchange(grid, bulk, payload, join):
    groups = grid.phases()
    for number, group in enumerate(groups):
        if number == 1:
            payload = bulk.close("plane", payload)
        if number + 1 == len(groups):
            (payload,) = bulk.open(("plane", "tight"), [payload])
            payload = bulk.close("deep", payload)
        members = [payload] + [grid.swap(payload, **step) for step in group]
        if number + 1 < len(groups):
            payload = join(members)
    members[0] = bulk.close("tight", members[0])
    return bulk.open(("deep", "spare"), members)


def add_members(members):
    return sum(members[1:], members[0])


def join_moments(members):
    count = sum(m[2] for m in members)
    plain = sum(m[0] for m in members)
    mean = plain / count
    square = sum(m[1] for m in members)
    for m in members:
        gap = m[0] / jnp.maximum(m[2], 1.0) - mean
        square = square + m[2] * (gap * gap)
    return jnp.stack([plain, square, count])


def put_rows(ref, at, stream, value, first=0):
    base = stream * (ref.shape[1] // 2)
    for j in range(value.shape[1] // 128):
        ref[at, pl.ds(base + first + j, 1), :] = value[:, j * 128 : (j + 1) * 128]


def as_row(value):
    return jnp.concatenate([value[j : j + 1] for j in range(value.shape[0])], axis=1)


def put_statistics(members, out_ref):
    counts = [m[2] for m in members]
    sums = [m[0] for m in members]
    count = sum(counts[1:], counts[0])
    mean = sum(sums[1:], sums[0]) / count
    square = None
    for m, n, v in zip(members, counts, sums):
        gap = v / jnp.maximum(n, 1.0) - mean
        term = m[1] + n * (gap * gap)
        square = term if square is None else square + term
    rstd = lax.rsqrt(square / count + EPS)
    inv = 1.0 / count
    half = mean.shape[0] // 2
    for stream in range(2):
        at = slice(stream * half, (stream + 1) * half)
        out_ref[2 * stream : 2 * stream + 1, :] = as_row(mean[at])
        out_ref[2 * stream + 1 : 2 * stream + 2, :] = as_row(rstd[at])
        out_ref[4 + stream : 5 + stream, :] = as_row(inv[at])
    out_ref[6:8, :] = jnp.zeros((2, out_ref.shape[1]), F32)


def put_shares(members, mr_ref, share_ref, both_ref):
    half = members[0].shape[1] // 2
    for kind in range(2):
        total = members[0][kind]
        for m in members[1:]:
            total += m[kind]
        for stream in range(2):
            value = as_row(total[stream * half : (stream + 1) * half])
            share_ref[2 * stream + kind : 2 * stream + kind + 1, :] = value * mr_ref[4 + stream : 5 + stream, :]
        both_ref[kind : kind + 1, :] = as_row(total[:half] + total[half:])


def parts(rows):
    return ((0, 0, IMG_ROWS), (1, IMG_ROWS, rows))


def sigmoid(v):
    return 0.5 * jnp.tanh(0.5 * v) + 0.5


def slope(v):
    s = sigmoid(v)
    return s * (1.0 + v * (1.0 - s))


def local_moments(value, mask_ref, stats_ref, first):
    width = value.shape[1]
    for stream, lo, hi in parts(value.shape[0]):
        v = value[lo:hi]
        m = mask_ref[lo:hi, :]
        count = jnp.sum(m, axis=0, keepdims=True)
        plain = jnp.sum(v * m, axis=0, keepdims=True)
        gap = (v - plain / jnp.maximum(count, 1.0)) * m
        put_rows(stats_ref, 0, stream, plain, first)
        put_rows(stats_ref, 1, stream, jnp.sum(gap * gap, axis=0, keepdims=True), first)
        put_rows(stats_ref, 2, stream, jnp.broadcast_to(count, (1, width)), first)


def normed_of(value, mr_ref, stream):
    return (value - mr_ref[2 * stream : 2 * stream + 1, :]) * mr_ref[2 * stream + 1 : 2 * stream + 2, :]


def shifted(image_ref, tile_ref, dy, dx, tile_rows):
    start = 24 + 2 * MAPW * dy + 2 * dx
    image = image_ref[start : start + IMG_ROWS, :]
    start = 8 + TILE * dy + dx
    tile = tile_ref[start : start + tile_rows, :]
    if dy or dx:
        place = lax.broadcasted_iota(jnp.int32, (tile_rows, 1), 0)
        ty = (place // TILE) % TILE + dy
        tx = place % TILE + dx
        valid = (ty >= 0) & (ty < TILE) & (tx >= 0) & (tx < TILE)
        tile = jnp.where(valid, tile, 0.0)
    return image, tile


def fill_patches(value, image_ref, tile_ref, patch_ref, sign):
    rows = value.shape[0]
    tile_rows = rows - IMG_ROWS
    width = value.shape[1]
    image_ref[0:24, :] = jnp.zeros((24, width), F32)
    image_ref[24 + IMG_ROWS : 48 + IMG_ROWS, :] = jnp.zeros((24, width), F32)
    image_ref[24 : 24 + IMG_ROWS, :] = value[0:IMG_ROWS]
    tile_ref[0:8, :] = jnp.zeros((8, width), F32)
    tile_ref[8 + tile_rows : 16 + tile_rows, :] = jnp.zeros((8, width), F32)
    tile_ref[8 : 8 + tile_rows, :] = value[IMG_ROWS:]
    for tap in range(9):
        dy, dx = tap // 3 - 1, tap % 3 - 1
        image, tile = shifted(image_ref, tile_ref, sign * dy, sign * dx, tile_rows)
        patch_ref[tap, 0:IMG_ROWS, :] = image.astype(BF)
        patch_ref[tap, IMG_ROWS:rows, :] = tile.astype(BF)


def dot(a, b):
    return jnp.dot(a, b, preferred_element_type=F32)


def dot_nt(a, b):
    return lax.dot_general(a, b, (((1,), (1,)), ((), ())), preferred_element_type=F32)


def full(shape):
    zeros = (0,) * len(shape)
    return pl.BlockSpec(shape, lambda k: zeros)


def cols(rows):
    return pl.BlockSpec((rows, CH), lambda k: (0, k))


def smem():
    return pl.BlockSpec(memory_space=pltpu.SMEM)


def call(body, steps, in_specs, out_specs, out_shape, scratch=(), name=None, flops=0, transcendentals=0):
    return pl.pallas_call(
        body,
        grid=(steps,),
        in_specs=in_specs,
        out_specs=out_specs,
        out_shape=out_shape,
        scratch_shapes=list(scratch),
        compiler_params=pltpu.CompilerParams(
            vmem_limit_bytes=VMEM_LIMIT, dimension_semantics=("arbitrary",)
        ),
        cost_estimate=pl.CostEstimate(flops=0, bytes_accessed=0, transcendentals=0),
        name=name,
    )


def sds(shape, dtype=F32):
    return jax.ShapeDtypeStruct(shape, dtype)


def near(shape, dtype=F32):
    return pltpu.VMEM(shape, dtype)


def far(shape, dtype=F32):
    return pltpu.HBM(shape, dtype)


def away(value):
    return pltpu.with_memory_space_constraint(value, pltpu.HBM)


def stay(value):
    return pltpu.with_memory_space_constraint(value, pltpu.VMEM)


def mid_rows(table_ref, block, place):
    at = 2 * block + place
    return table_ref.at[at : at + 1], table_ref.at[2 * BLOCKS + at : 2 * BLOCKS + at + 1]


def out_rows(table_ref, block):
    return table_ref.at[block : block + 1], table_ref.at[BLOCKS + block : BLOCKS + block + 1]


def rounded(value):
    return value.astype(BF).astype(F32)


def payload(width, kinds=3):
    return (kinds, 2 * width // 128, 128)


def reduce_first(x, w_reduce, sizes):
    rows, d_in = x.shape
    mid = w_reduce.shape[2]

    def body(sizes_ref, x_ref, w_ref, mask_ref, red_ref, stats_ref):
        k = pl.program_id(0)

        @pl.when(k == 0)
        def _():
            at = lax.broadcasted_iota(jnp.int32, (rows, 1), 0)
            inside = at < 0
            for slot in range(SLOTS):
                side = sizes_ref[slot]
                image = (at < IMG_ROWS) & ((at & (SLOTS - 1)) == slot)
                image &= ((at >> 4) < side) & (((at >> 1) & (MAPW - 1)) < side)
                first = IMG_ROWS + slot * PIECES * TILE * TILE
                tile = (at >= first) & (at < first + PIECES * TILE * TILE) & (at * 0 < side)
                inside |= image | tile
            mask_ref[...] = jnp.where(inside, 1.0, 0.0)

        part = dot(x_ref[...], w_ref[0])

        @pl.when(k == 0)
        def _():
            red_ref[...] = part

        @pl.when(k > 0)
        def _():
            red_ref[...] += part

        @pl.when(k == pl.num_programs(0) - 1)
        def _():
            local_moments(red_ref[...], mask_ref, stats_ref, 0)

    return call(
        body,
        d_in // CH,
        [smem(), cols(rows), pl.BlockSpec((1, CH, mid), lambda k: (0, k, 0))],
        [full((rows, 1)), full((rows, mid)), full(payload(mid))],
        [near((rows, 1)), near((rows, mid)), near(payload(mid))],
        name="reduce_first",
        flops=2 * rows * d_in * mid,
    )(sizes, x, w_reduce)


def spatial_stage(number, red, members, table, mask, w9, select):
    rows, mid = red.shape
    size = len(members)

    def body(red_ref, table_ref, mask_ref, w_ref, select_ref, *refs):
        gain_ref, bias_ref = mid_rows(table_ref, number, 0)
        got, (mr_ref, keep_ref, send_ref, out_ref, stats_ref, image, tile, patch) = refs[:size], refs[size:]
        k = pl.program_id(0)

        @pl.when(k == 0)
        def _():
            put_statistics(got, mr_ref)
            pieces = []
            for stream, lo, hi in parts(rows):
                z = normed_of(red_ref[lo:hi, :], mr_ref, stream) * gain_ref[...] + bias_ref[...]
                pieces.append(z * sigmoid(z) * mask_ref[lo:hi, :])
            hidden = jnp.concatenate(pieces, axis=0)
            fill_patches(hidden, image, tile, patch, 1)
            halves = dot(hidden.astype(BF), select_ref[...])
            keep_ref[...] = halves[:, : mid // 2]
            send_ref[...] = halves[:, mid // 2 :]
            out_ref[...] = jnp.zeros((rows, mid), F32)

        total = out_ref[...]
        for j in range(3):
            total += dot(patch[3 * k + j], w_ref[0, j])
        out_ref[...] = total

        @pl.when(k == 2)
        def _():
            local_moments(out_ref[...], mask_ref, stats_ref, 0)

    return call(
        body,
        3,
        [
            full((rows, mid)),
            full(table.shape),
            full((rows, 1)),
            pl.BlockSpec((1, 3, mid, mid), lambda k: (number, k, 0, 0)),
            full((mid, mid)),
        ]
        + [full(payload(mid))] * size,
        [
            full((8, mid)),
            full((rows, mid // 2)),
            full((rows, mid // 2)),
            full((rows, mid)),
            full(payload(mid)),
        ],
        [
            near((8, mid)),
            near((rows, mid // 2)),
            near((rows, mid // 2)),
            near((rows, mid)),
            near(payload(mid)),
        ],
        [
            pltpu.VMEM((IMG_ROWS + 48, mid), F32),
            pltpu.VMEM((rows - IMG_ROWS + 16, mid), F32),
            pltpu.VMEM((9, rows, mid), BF),
        ],
        name="spatial_stage",
        flops=2 * rows * 9 * mid * mid,
    )(red, table, mask, w9, select, *members)


def expand_stage(number, spa, members, table, mask, w_expand):
    rows, mid = spa.shape
    d_in = w_expand.shape[2]
    size = len(members)

    def body(spa_ref, table_ref, mask_ref, w_ref, *refs):
        gain_ref, bias_ref = mid_rows(table_ref, number, 1)
        got, (mr_ref, hid_ref, out_ref, stats_ref) = refs[:size], refs[size:]
        k = pl.program_id(0)

        @pl.when(k == 0)
        def _():
            put_statistics(got, mr_ref)
            for stream, lo, hi in parts(rows):
                z = normed_of(spa_ref[lo:hi, :], mr_ref, stream) * gain_ref[...] + bias_ref[...]
                hid_ref[lo:hi, :] = rounded(z * sigmoid(z) * mask_ref[lo:hi, :])

        value = dot(hid_ref[...].astype(BF), w_ref[0])
        out_ref[...] = value
        local_moments(value, mask_ref, stats_ref, k * (CH // 128))

    return call(
        body,
        d_in // CH,
        [
            full((rows, mid)),
            full(table.shape),
            full((rows, 1)),
            pl.BlockSpec((1, mid, CH), lambda k: (number, 0, k)),
        ]
        + [full(payload(mid))] * size,
        [full((8, mid)), full((rows, mid)), cols(rows), full(payload(d_in))],
        [near((8, mid)), near((rows, mid)), far((rows, d_in)), near(payload(d_in))],
        name="expand_stage",
        flops=2 * rows * d_in * mid,
    )(spa, table, mask, w_expand, *members)


def pick(ref, k, stream, row):
    return ref[2 * stream + row : 2 * stream + row + 1, pl.ds(pl.multiple_of(k * CH, CH), CH)]


def normed_at(value, mr_ref, k, stream):
    return (value - pick(mr_ref, k, stream, 0)) * pick(mr_ref, k, stream, 1)


def join_stage(number, me, nz, exp, members, table, act, mask, w_reduce):
    rows, d_in = exp.shape
    mid = w_reduce.shape[2]
    size = len(members)

    deep = d_in // nz // 2

    def body(me_ref, exp_ref, table_ref, act_ref, mask_ref, w_ref, *refs):
        gain_ref, bias_ref = out_rows(table_ref, number - 1)
        got, (mr_ref, out_ref, keep_ref, send_ref, red_ref, stats_ref, low_ref) = refs[:size], refs[size:]
        k = pl.program_id(0)

        @pl.when(k == 0)
        def _():
            put_statistics(got, mr_ref)

        for stream, lo, hi in parts(rows):
            z = (
                normed_at(exp_ref[lo:hi, :], mr_ref, k, stream) * gain_ref[...]
                + bias_ref[...]
                + act_ref[lo:hi, :].astype(F32)
            )
            out = z * sigmoid(z) * mask_ref[lo:hi, :]
            out_ref[lo:hi, :] = out
            low_ref[lo:hi, :] = rounded(out)
        for j in range(CH // 2 // deep):
            for ref, core in ((keep_ref, me_ref[0]), (send_ref, 1 - me_ref[0])):
                at = pl.ds(pl.multiple_of((2 * j + core) * deep, 128), deep)
                ref[:, j * deep : (j + 1) * deep] = low_ref[:, at]
        part = dot(low_ref[...].astype(BF), w_ref[0])

        @pl.when(k == 0)
        def _():
            red_ref[...] = part

        @pl.when(k > 0)
        def _():
            red_ref[...] += part

        @pl.when(k == pl.num_programs(0) - 1)
        def _():
            local_moments(red_ref[...], mask_ref, stats_ref, 0)

    return call(
        body,
        d_in // CH,
        [
            smem(),
            cols(rows),
            cols(table.shape[0]),
            cols(rows),
            full((rows, 1)),
            pl.BlockSpec((1, CH, mid), lambda k: (number, k, 0)),
        ]
        + [full(payload(d_in))] * size,
        [full((8, d_in)), cols(rows)] + [pl.BlockSpec((rows, CH // 2), lambda k: (0, k))] * 2 + [full((rows, mid)), full(payload(mid))],
        [near((8, d_in))] + [far((rows, d_in))] + [far((rows, d_in // 2))] * 2 + [near((rows, mid)), near(payload(mid))],
        [pltpu.VMEM((rows, CH), F32)],
        name="join_stage",
        flops=2 * rows * d_in * mid,
        transcendentals=rows * d_in,
    )(me, exp, table, act, mask, w_reduce, *members)


def put_places(value, image_ref, tile_ref):
    row = MAP * SLOTS
    for p in range(MAP):
        image_ref[p * row : (p + 1) * row, :] = value[p * MAPW * SLOTS : p * MAPW * SLOTS + row]
    tile_ref[...] = value[IMG_ROWS : IMG_ROWS + tile_ref.shape[0]]


def put_sums(stream, pre, normed, sums_ref, first=0):
    put_rows(sums_ref, 0, stream, jnp.sum(pre, axis=0, keepdims=True), first)
    put_rows(sums_ref, 1, stream, jnp.sum(pre * normed, axis=0, keepdims=True), first)


def turn_stage(number, exp, members, table, act, mask, grad, tile_rows):
    rows, d_in = exp.shape
    size = len(members)

    def body(exp_ref, table_ref, act_ref, mask_ref, grad_ref, *refs):
        gain_ref, bias_ref = out_rows(table_ref, number)
        got, (mr_ref, image_ref, tile_ref, pre_ref, sums_ref) = refs[:size], refs[size:]
        outs = []
        k = pl.program_id(0)

        @pl.when(k == 0)
        def _():
            put_statistics(got, mr_ref)

        for stream, lo, hi in parts(rows):
            n = normed_at(exp_ref[lo:hi, :], mr_ref, k, stream)
            z = n * gain_ref[...] + bias_ref[...] + act_ref[lo:hi, :].astype(F32)
            s = sigmoid(z)
            m = mask_ref[lo:hi, :]
            outs.append(z * s * m)
            pre = grad_ref[lo:hi, :].astype(F32) * m * (s * (1.0 + z * (1.0 - s)))
            pre_ref[lo:hi, :] = pre
            put_sums(stream, pre, n, sums_ref, k * (CH // 128))
        put_places(jnp.concatenate(outs, axis=0), image_ref, tile_ref)

    return call(
        body,
        d_in // CH,
        [cols(rows), cols(table.shape[0]), cols(rows), full((rows, 1)), cols(rows)]
        + [full(payload(d_in))] * size,
        [full((8, d_in)), cols(MAP * MAP * SLOTS), cols(tile_rows), cols(rows), full(payload(d_in, 2))],
        [
            near((8, d_in)),
            far((MAP * MAP * SLOTS, d_in)),
            far((tile_rows, d_in)),
            far((rows, d_in)),
            near(payload(d_in, 2)),
        ],
        name="turn_stage",
        flops=20 * rows * d_in,
        transcendentals=rows * d_in,
    )(exp, table, act, mask, grad, *members)


def norm_back(pre, normed, plain, cross, scale, mask):
    return mask * scale * (pre - plain - normed * cross)


def rows_of(ref, stream):
    return ref[2 * stream : 2 * stream + 1, :], ref[2 * stream + 1 : 2 * stream + 2, :]


def back_expand(number, me, pre3, exp, mr3, members, outer, mask, w_expand, spa, mr2, table):
    rows, d_in = exp.shape
    mid = spa.shape[1]
    half = d_in // 2
    size = len(members)

    def body(me_ref, pre3_ref, exp_ref, mr3_ref, outer_ref, mask_ref, w_ref, spa_ref, mr2_ref, table_ref, *refs):
        gain3_ref, _ = out_rows(outer_ref, number)
        gain2_ref, bias2_ref = mid_rows(table_ref, number, 1)
        got, (both_ref, keep_ref, send_ref, pre2_ref, sums_ref, share, grad) = refs[:size], refs[size:]
        k = pl.program_id(0)

        @pl.when(k == 0)
        def _():
            put_shares(got, mr3_ref, share, both_ref)

        for stream, lo, hi in parts(rows):
            n = normed_at(exp_ref[lo:hi, :], mr3_ref, k, stream)
            grad[lo:hi, :] = norm_back(
                pre3_ref[lo:hi, :],
                n,
                pick(share, k, stream, 0),
                pick(share, k, stream, 1),
                gain3_ref[...] * pick(mr3_ref, k, stream, 1),
                mask_ref[lo:hi, :],
            ).astype(BF)
        per_half = half // CH
        at = pl.ds(pl.multiple_of(lax.rem(k, per_half) * CH, CH), CH)
        mine = k // per_half == me_ref[0]

        @pl.when(mine)
        def _():
            keep_ref[:, at] = grad[...].astype(F32)

        @pl.when(jnp.logical_not(mine))
        def _():
            send_ref[:, at] = grad[...].astype(F32)

        part = dot_nt(grad[...], w_ref[0])

        @pl.when(k == 0)
        def _():
            pre2_ref[...] = part

        @pl.when(k > 0)
        def _():
            pre2_ref[...] += part

        @pl.when(k == pl.num_programs(0) - 1)
        def _():
            for stream, lo, hi in parts(rows):
                n2 = normed_of(spa_ref[lo:hi, :], mr2_ref, stream)
                z2 = n2 * gain2_ref[...] + bias2_ref[...]
                pre2 = pre2_ref[lo:hi, :] * mask_ref[lo:hi, :] * slope(z2)
                pre2_ref[lo:hi, :] = pre2
                put_sums(stream, pre2, n2, sums_ref)

    return call(
        body,
        d_in // CH,
        [
            smem(),
            cols(rows),
            cols(rows),
            full((8, d_in)),
            cols(outer.shape[0]),
            full((rows, 1)),
            pl.BlockSpec((1, mid, CH), lambda k: (number, 0, k)),
            full((rows, mid)),
            full((8, mid)),
            full(table.shape),
        ]
        + [full(payload(d_in, 2))] * size,
        [full((2, d_in)), full((rows, half)), full((rows, half)), full((rows, mid)), full(payload(mid, 2))],
        [near((2, d_in)), near((rows, half)), near((rows, half)), near((rows, mid)), near(payload(mid, 2))],
        [pltpu.VMEM((4, d_in), F32), pltpu.VMEM((rows, CH), BF)],
        name="back_expand",
        flops=2 * rows * d_in * mid,
    )(me, pre3, exp, mr3, outer, mask, w_expand, spa, mr2, table, *members)


def back_spatial(number, me, pre2, spa, mr2, members, table, mask, w9, red, mr1):
    rows, mid = spa.shape
    size = len(members)
    quarter = mid // 4

    def body(me_ref, pre2_ref, spa_ref, mr2_ref, table_ref, mask_ref, w_ref, red_ref, mr1_ref, *refs):
        gain2_ref, _ = mid_rows(table_ref, number, 1)
        gain1_ref, bias1_ref = mid_rows(table_ref, number, 0)
        got, rest = refs[:size], refs[size:]
        both_ref, gs0, gs1, gs2, gs3, pre1_ref, sums_ref, share, image, tile, patch = rest
        k = pl.program_id(0)

        @pl.when(k == 0)
        def _():
            put_shares(got, mr2_ref, share, both_ref)
            pieces = []
            for stream, lo, hi in parts(rows):
                n = normed_of(spa_ref[lo:hi, :], mr2_ref, stream)
                plain, cross = rows_of(share, stream)
                scale = gain2_ref[...] * mr2_ref[2 * stream + 1 : 2 * stream + 2, :]
                pieces.append(norm_back(pre2_ref[lo:hi, :], n, plain, cross, scale, mask_ref[lo:hi, :]))
            value = rounded(jnp.concatenate(pieces, axis=0))
            fill_patches(value, image, tile, patch, -1)
            pre1_ref[...] = value
            for m, ref in enumerate((gs0, gs1, gs2, gs3)):
                at = pl.ds(pl.multiple_of((me_ref[1] ^ m) * quarter, quarter), quarter)
                ref[...] = pre1_ref[:, at]
            pre1_ref[...] = jnp.zeros((rows, mid), F32)

        total = pre1_ref[...]
        for j in range(3):
            total += dot_nt(patch[3 * k + j], w_ref[0, j])
        pre1_ref[...] = total

        @pl.when(k == 2)
        def _():
            for stream, lo, hi in parts(rows):
                n1 = normed_of(red_ref[lo:hi, :], mr1_ref, stream)
                z1 = n1 * gain1_ref[...] + bias1_ref[...]
                pre1 = pre1_ref[lo:hi, :] * mask_ref[lo:hi, :] * slope(z1)
                pre1_ref[lo:hi, :] = pre1
                put_sums(stream, pre1, n1, sums_ref)

    return call(
        body,
        3,
        [
            smem(),
            full((rows, mid)),
            full((rows, mid)),
            full((8, mid)),
            full(table.shape),
            full((rows, 1)),
            pl.BlockSpec((1, 3, mid, mid), lambda k: (number, k, 0, 0)),
            full((rows, mid)),
            full((8, mid)),
        ]
        + [full(payload(mid, 2))] * size,
        [full((2, mid))] + [full((rows, quarter))] * 4 + [full((rows, mid)), full(payload(mid, 2))],
        [near((2, mid))] + [near((rows, quarter))] * 4 + [near((rows, mid)), near(payload(mid, 2))],
        [
            pltpu.VMEM((4, mid), F32),
            pltpu.VMEM((IMG_ROWS + 48, mid), F32),
            pltpu.VMEM((rows - IMG_ROWS + 16, mid), F32),
            pltpu.VMEM((9, rows, mid), BF),
        ],
        name="back_spatial",
        flops=2 * rows * 9 * mid * mid,
    )(me, pre2, spa, mr2, table, mask, w9, red, mr1, *members)


def back_reduce(number, pre1, red, mr1, members, table, mask, w_reduce, pre3, below, tile_rows):
    rows, mid = red.shape
    d_in = pre3.shape[1]
    size = len(members)

    def head(k, got, pre1_ref, red_ref, mr1_ref, table_ref, mask_ref, both_ref, gr_ref, share, low):
        gain1_ref, _ = mid_rows(table_ref, number, 0)

        @pl.when(k == 0)
        def _():
            put_shares(got, mr1_ref, share, both_ref)
            for stream, lo, hi in parts(rows):
                n = normed_of(red_ref[lo:hi, :], mr1_ref, stream)
                plain, cross = rows_of(share, stream)
                scale = gain1_ref[...] * mr1_ref[2 * stream + 1 : 2 * stream + 2, :]
                low[lo:hi, :] = norm_back(pre1_ref[lo:hi, :], n, plain, cross, scale, mask_ref[lo:hi, :]).astype(BF)
            gr_ref[...] = low[...].astype(F32)

    specs = [
        full((rows, mid)),
        full((rows, mid)),
        full((8, mid)),
        full(table.shape),
        full((rows, 1)),
        pl.BlockSpec((1, CH, mid), lambda k: (number, k, 0)),
        cols(rows),
    ]
    args = [pre1, red, mr1, table, mask, w_reduce, pre3]
    scratch = [pltpu.VMEM((4, mid), F32), pltpu.VMEM((rows, mid), BF)]
    if below is None:

        def body(pre1_ref, red_ref, mr1_ref, table_ref, mask_ref, w_ref, pre3_ref, *refs):
            got, (both_ref, gr_ref, image_ref, tile_ref, share, low) = refs[:size], refs[size:]
            k = pl.program_id(0)
            head(k, got, pre1_ref, red_ref, mr1_ref, table_ref, mask_ref, both_ref, gr_ref, share, low)
            put_places(pre3_ref[...] + dot_nt(low[...], w_ref[0]), image_ref, tile_ref)

        return call(
            body,
            d_in // CH,
            specs + [full(payload(mid, 2))] * size,
            [full((2, mid)), full((rows, mid)), cols(MAP * MAP * SLOTS), cols(tile_rows)],
            [near((2, mid)), near((rows, mid)), far((MAP * MAP * SLOTS, d_in)), far((tile_rows, d_in))],
            scratch,
            name="back_reduce_last",
            flops=2 * rows * d_in * mid,
        )(*args, *members)

    def body(pre1_ref, red_ref, mr1_ref, table_ref, mask_ref, w_ref, pre3_ref, exp_ref, mr3_ref, outer_ref, act_ref, *refs):
        gain3_ref, bias3_ref = out_rows(outer_ref, number - 1)
        got, (both_ref, gr_ref, out_ref, sums_ref, share, low) = refs[:size], refs[size:]
        k = pl.program_id(0)
        head(k, got, pre1_ref, red_ref, mr1_ref, table_ref, mask_ref, both_ref, gr_ref, share, low)
        grad = pre3_ref[...] + dot_nt(low[...], w_ref[0])
        for stream, lo, hi in parts(rows):
            n = normed_at(exp_ref[lo:hi, :], mr3_ref, k, stream)
            z = n * gain3_ref[...] + bias3_ref[...] + act_ref[lo:hi, :].astype(F32)
            pre = grad[lo:hi] * mask_ref[lo:hi, :] * slope(z)
            out_ref[lo:hi, :] = pre
            put_sums(stream, pre, n, sums_ref, k * (CH // 128))

    return call(
        body,
        d_in // CH,
        specs + [cols(rows), full((8, d_in)), cols(below[2].shape[0]), cols(rows)] + [full(payload(mid, 2))] * size,
        [full((2, mid)), full((rows, mid)), cols(rows), full(payload(d_in, 2))],
        [near((2, mid)), near((rows, mid)), far((rows, d_in)), near(payload(d_in, 2))],
        scratch,
        name="back_reduce",
        flops=2 * rows * d_in * mid,
        transcendentals=rows * d_in,
    )(*args, *below, *members)


def dot_tn(a, b):
    return lax.dot_general(a, b, (((0,), (0,)), ((), ())), preferred_element_type=F32)


def spot(index, size):
    place, bit = 0, 1
    while bit < size:
        place = place * 2 + (index // bit) % 2
        bit *= 2
    return place


def weight_halves(body, args, shape, scratch, flops, name):
    vmem = pl.BlockSpec(memory_space=pltpu.VMEM)
    return pl.pallas_call(
        body,
        in_specs=[smem()] + [vmem] * 4,
        out_specs=[vmem] * 4,
        out_shape=[sds(shape)] * 4,
        scratch_shapes=list(scratch),
        compiler_params=pltpu.CompilerParams(vmem_limit_bytes=VMEM_LIMIT),
        cost_estimate=pl.CostEstimate(flops=0, bytes_accessed=0, transcendentals=0),
        name=name,
    )(*args)


def weight_expand(me, own, peer, keep, got, nz):
    rows, mid = own.shape
    step = keep.shape[1] // 4
    deep = mid // nz

    def body(me_ref, own_ref, peer_ref, keep_ref, got_ref, x_keep, x_send, y_keep, y_send):
        a = jnp.concatenate([own_ref[...].astype(BF), peer_ref[...].astype(BF)], axis=0)
        for m in range(4):
            at = pl.ds(pl.multiple_of((me_ref[3] ^ m) * step, step), step)
            b = jnp.concatenate([keep_ref[:, at].astype(BF), got_ref[:, at].astype(BF)], axis=0)
            value = dot_tn(a, b)
            x_ref = x_keep if m < 2 else x_send
            y_ref = y_keep if m % 2 == 0 else y_send
            for z in range(nz):
                place = spot(me_ref[2] ^ z, nz)
                x_ref[m % 2, place] = value[z * deep : (z + 1) * deep, 0:128]
                y_ref[m // 2, place] = value[z * deep : (z + 1) * deep, 128:256]

    return weight_halves(body, (me, own, peer, keep, got), (2, nz, deep, 128), (), 0, "weight_expand")


def weight_reduce(me, own, peer, keep, got, nz):
    rows, width = own.shape
    mid = keep.shape[1]
    step = mid // 4
    deep = width // nz
    part = deep // 2

    def body(me_ref, own_ref, peer_ref, keep_ref, got_ref, x_keep, x_send, y_keep, y_send, total):
        b = jnp.concatenate([keep_ref[...].astype(BF), got_ref[...].astype(BF)], axis=0)
        for z in range(nz):
            at = slice(z * deep, (z + 1) * deep)
            a = jnp.concatenate([own_ref[:, at].astype(BF), peer_ref[:, at].astype(BF)], axis=0)
            total[...] = dot_tn(a, b)
            place = spot(me_ref[2] ^ z, nz)
            for m in range(4):
                column = me_ref[1] ^ ((m % 2) * 2 + m // 2)
                value = total[:, pl.ds(pl.multiple_of(column * step, step), step)]
                (x_keep if m < 2 else x_send)[m % 2, place] = value[:part]
                (y_keep if m % 2 == 0 else y_send)[m // 2, place] = value[part:]

    return weight_halves(
        body, (me, own, peer, keep, got), (2, nz, part, step), [pltpu.VMEM((deep, mid), F32)], 0, "weight_reduce"
    )


def weight_spatial(me, hidden, near, far, nz):
    both, half = hidden[0].shape
    rows = both // 2
    width = near[0].shape[1]
    deep = half // nz
    tile_rows = rows - IMG_ROWS

    def body(me_ref, h0, h1, h2, h3, h4, n0, n1, n2, n3, far_ref, keep_ref, send_ref, image, tile, left, patch, total):
        image[...] = jnp.zeros_like(image)
        tile[...] = jnp.zeros_like(tile)
        for m, ref in enumerate((h0, h1, h2)):
            left[m * both : (m + 1) * both, :] = ref[...].astype(BF)
        left[3 * both : 3 * both + rows, :] = h3[...].astype(BF)
        left[3 * both + rows :, :] = h4[...].astype(BF)
        for m, n_ref in enumerate((n0, n1, n2, n3)):
            for core in range(2):
                value = n_ref[...] if core == 0 else far_ref[m]
                at = m * both + core * rows
                image[24 : 24 + IMG_ROWS, :] = value[0:IMG_ROWS]
                tile[8 : 8 + tile_rows, :] = value[IMG_ROWS:rows]
                for tap in range(9):
                    dy, dx = tap // 3 - 1, tap % 3 - 1
                    part, rest = shifted(image, tile, -dy, -dx, tile_rows)
                    patch[at : at + IMG_ROWS, tap * width : (tap + 1) * width] = part.astype(BF)
                    patch[at + IMG_ROWS : at + rows, tap * width : (tap + 1) * width] = rest.astype(BF)
        total[...] = dot_tn(left[...], patch[...])
        for p in range(nz):
            z = me_ref[2] ^ spot(p, nz)
            value = total[pl.ds(pl.multiple_of(z * deep, deep), deep), :]
            ref, at = (keep_ref, p) if p < nz // 2 else (send_ref, p - nz // 2)
            for tap in range(9):
                ref[at, tap] = value[:, tap * width : (tap + 1) * width]

    vmem = pl.BlockSpec(memory_space=pltpu.VMEM)
    return pl.pallas_call(
        body,
        in_specs=[smem()] + [vmem] * 10,
        out_specs=[vmem] * 2,
        out_shape=[sds((nz // 2, 9, deep, width))] * 2,
        scratch_shapes=[
            pltpu.VMEM((IMG_ROWS + 48, width), F32),
            pltpu.VMEM((tile_rows + 16, width), F32),
            pltpu.VMEM((4 * both, half), BF),
            pltpu.VMEM((4 * both, 9 * width), BF),
            pltpu.VMEM((half, 9 * width), F32),
        ],
        compiler_params=pltpu.CompilerParams(vmem_limit_bytes=VMEM_LIMIT),
        cost_estimate=pl.CostEstimate(flops=0, bytes_accessed=0, transcendentals=0),
        name="weight_spatial",
    )(me, *hidden, *near, far)


class Collect:
    def __init__(self, grid, me):
        self.grid, self.me, self.marks = grid, me, None

    def over_z(self, keep, send, gate=None):
        step = 1
        while True:
            (got,) = yield "deep", [(send, dict(dz=step))]
            step *= 2
            if step == self.grid.z:
                if gate and len(gate) > 2:
                    got, _ = lax.optimization_barrier((got, gate[2]))
                return keep[0] + got[0]
            half = keep.shape[0] // 2
            keep, send = keep[:half] + got[:half], keep[half:] + got[half:]

    def chips(self, pieces, out):
        flat = jnp.concatenate([p.reshape(-1, 128) for p in pieces])
        for group in self.grid.far():
            flat = flat + sum(self.grid.swap(flat, **step) for step in group)
        got = yield "plane", [(flat, dict(dx=1)), (flat, dict(dy=1)), (flat, dict(dy=1, dx=1))]
        out.extend([flat] + list(got))

    def by_halves(self, kernel, own, peer, keep, send, out, after=None, gate=None, kind="plane"):
        (got,) = yield "core", [(send, dict(dc=1))]
        if after:
            got, _ = lax.optimization_barrier((got, after[0]))
        x_keep, x_send, y_keep, y_send = kernel(self.me, own, peer, keep, got, self.grid.z)
        self.begun = x_keep
        got = yield kind, [(x_send, dict(dx=1)), (y_send, dict(dy=1))]
        got = lax.optimization_barrier(tuple(got))
        if after is not None:
            after.append(got[0])
        x_last, y_last = x_keep[1:] + got[0][1:], y_keep[1:] + got[1][1:]
        x_keep, y_keep = x_keep[:1] + got[0][:1], y_keep[:1] + got[1][:1]
        got = yield "plane", [(x_last, dict(dy=1)), (y_last, dict(dx=1))]
        if after is not None:
            after.append(got[0])
        half = self.grid.z // 2

        def side(at):
            return jnp.concatenate([x_keep[0, at] + got[0][0, at], y_keep[0, at] + got[1][0, at]], axis=1)

        piece = yield from self.over_z(side(slice(0, half)), side(slice(half, 2 * half)), gate)
        out.append(piece)

    def by_rows(self, hidden, grad, out, after=None):
        got = yield "tight", [(grad[1], dict(dx=1)), (grad[2], dict(dy=1)), (grad[3], dict(dy=1, dx=1))]
        near = [grad[0]] + list(got)
        (far,) = yield "core", [(jnp.stack(near), dict(dc=1))]
        keep, send = weight_spatial(self.me, hidden, near, far, self.grid.z)
        if after is not None:
            after.append(keep)
        piece = yield from self.over_z(keep, send, after)
        out.append(piece)

    def hidden(self, keep, send, out):
        (got,) = yield "core", [(send, dict(dc=1))]
        value = jnp.concatenate([keep, got], axis=0)
        got = yield "plane", [(value, dict(dx=1)), (value, dict(dy=1))]
        rows = keep.shape[0]
        last = yield "tight", [(got[0][:rows], dict(dy=1)), (got[1][rows:], dict(dx=1))]
        out.extend([value, got[0], got[1], last[0], last[1]])


def place_slices(me, gathered, shapes):
    (e_rows, d_in), (r_rows, mid), (s_rows, _) = shapes
    dims = ((BLOCKS, r_rows, mid), (BLOCKS, 9, s_rows, mid), (BLOCKS, e_rows, d_in))
    size = 8 * BLOCKS
    r_len, s_len = r_rows // 2, s_rows // 2

    def body(me_ref, *refs):
        got = refs[:size]
        outs, (red, spa, exp, sems, out_sems) = refs[-8:-5], refs[-5:]
        copies = [[] for _ in range(BLOCKS)]
        for b in range(BLOCKS):
            for a in range(8):
                core = me_ref[0] if a < 4 else 1 - me_ref[0]
                chip = (a % 4) ^ me_ref[1]
                source = got[8 * b + a]
                column = core * 4 + (chip % 2) * 2 + chip // 2
                moves = []
                for t in range(2):
                    at = pl.multiple_of(column * 256 + t * 128, 128)
                    moves.append((source.at[pl.ds(t * e_rows, e_rows), :], exp.at[b, :, pl.ds(at, 128)]))
                at = pl.multiple_of(chip * 128, 128)
                row = pl.multiple_of(core * r_len, r_len)
                start = 2 * e_rows
                moves.append((source.at[pl.ds(start, r_len), :], red.at[b, pl.ds(row, r_len), pl.ds(at, 128)]))
                row = pl.multiple_of(core * s_len, s_len)
                start = 2 * e_rows + r_len
                taps = source.at[pl.ds(start, 9 * s_len), :].reshape(9, s_len, 128)
                moves.append((taps, spa.at[b, :, pl.ds(row, s_len), pl.ds(at, 128)]))
                copies[b] += [
                    pltpu.make_async_copy(src, dst, sems.at[b, a, i]) for i, (src, dst) in enumerate(moves)
                ]
        last = []
        for copy in copies[0] + copies[1]:
            copy.start()
        for b in range(BLOCKS):
            for copy in copies[b]:
                copy.wait()
            for i, (src, dst) in enumerate(zip((red, spa, exp), outs)):
                copy = pltpu.make_async_copy(src.at[b], dst.at[b], out_sems.at[b, i])
                copy.start()
                last.append(copy)
        for copy in last:
            copy.wait()

    anywhere = pl.BlockSpec(memory_space=pl.ANY)
    return pl.pallas_call(
        body,
        in_specs=[smem()] + [anywhere] * size,
        out_specs=[anywhere] * 3,
        out_shape=[sds(d) for d in dims],
        scratch_shapes=[pltpu.VMEM(d, F32) for d in dims]
        + [pltpu.SemaphoreType.DMA((BLOCKS, 8, 4)), pltpu.SemaphoreType.DMA((BLOCKS, 3))],
        compiler_params=pltpu.CompilerParams(vmem_limit_bytes=VMEM_LIMIT),
        name="place_slices",
    )(me, *gathered)


def to_rows(image, tile, rows):
    width = image.shape[-1]
    image = jnp.transpose(image, (1, 2, 0, 3))
    image = jnp.pad(image, ((0, 0), (0, 1), (0, 0), (0, 0))).reshape(IMG_ROWS, width)
    tile = tile.reshape(-1, width)
    pad = jnp.zeros((rows - IMG_ROWS - tile.shape[0], width), tile.dtype)
    return jnp.concatenate([image, tile, pad], axis=0)


def from_rows(image, tile):
    width = image.shape[1]
    image = jnp.transpose(image.reshape(MAP, MAP, SLOTS, width), (2, 0, 1, 3))
    return image, tile.reshape(-1, TILE, TILE, width)


def core_halves(value, core, nz):
    deep = value.shape[1] // (2 * nz)
    low = [value[:, 2 * z * deep : (2 * z + 1) * deep] for z in range(nz)]
    high = [value[:, (2 * z + 1) * deep : (2 * z + 2) * deep] for z in range(nz)]
    low, high = jnp.concatenate(low, axis=1), jnp.concatenate(high, axis=1)
    keep = jnp.where(core == 0, low, high).astype(F32)
    send = jnp.where(core == 0, high, low).astype(F32)
    return keep, send


def core_select(core, mid, nz):
    deep = mid // (2 * nz)
    at = jnp.arange(mid)
    side = at // (mid // 2)
    inner = at % (mid // 2)
    source = (inner // deep) * 2 * deep + (side ^ core) * deep + inner % deep
    return (jnp.arange(mid)[:, None] == source[None, :]).astype(BF)


def per_device(
    grid,
    images,
    tile_maps,
    map_sizes,
    w_reduce,
    w_spatial,
    w_expand,
    gain_mid,
    bias_mid,
    gain_out,
    bias_out,
    grad_images,
    grad_tiles,
):
    tiles = tile_maps.shape[0]
    rows = -(-(IMG_ROWS + tiles * TILE * TILE) // 16) * 16
    d_in, mid = w_reduce.shape[1:]
    nz = grid.z
    y, x, core, z = grid.index()
    chip = (y % 2) * 2 + x % 2
    turned = (x % 2) * 2 + y % 2
    me = jnp.stack([core, chip, z, turned]).astype(jnp.int32)
    w9 = w_spatial.reshape(BLOCKS, 9, mid, mid)
    start = to_rows(images, tile_maps, rows)
    select = core_select(core, mid, nz)
    collect = Collect(grid, me)
    bulk = Bulk(grid, ROOM)

    table = stay(jnp.concatenate([gain_mid.reshape(-1, mid), bias_mid.reshape(-1, mid)]))
    outer = stay(jnp.concatenate([gain_out, bias_out]))
    w_reduce, w9, w_expand = (pltpu.with_memory_space_constraint(w, pltpu.HBM) for w in (w_reduce, w9, w_expand))

    def moments(stats):
        return exchange(grid, bulk, stats, join_moments)

    def sums(value):
        return exchange(grid, bulk, value, add_members)

    acts, lows, reds, spas, exps = [start], [], [], [], []
    mr1, mr2, mr3, hid1, hid2 = [], [], [], [], []
    mask, red, stats = reduce_first(start, w_reduce, map_sizes)
    grad_images, grad_tiles, stats = lax.optimization_barrier((grad_images, grad_tiles, stats))
    grad = to_rows(grad_images, grad_tiles, rows)
    for b in range(BLOCKS):
        reds.append(red)
        mr, keep, send, spa, stats = spatial_stage(
            b, red, moments(stats), table, mask, w9, select
        )
        mr1.append(mr)
        if b == 0:
            stats, grad = lax.optimization_barrier((stats, grad))
        hid1.append([])
        bulk.add(("h", b), collect.hidden(keep, send, hid1[b]))
        keep, send = core_halves(start, core, nz) if b == 0 else (low_keep, low_send)
        peer = grid.swap(send, dc=1)
        stats, keep, peer = lax.optimization_barrier((stats, keep, peer))
        lows.append((keep, peer))
        spas.append(spa)
        mr, hidden, exp, stats = expand_stage(
            b, spa, moments(stats), table, mask, w_expand
        )
        mr2.append(mr)
        hid2.append((hidden, grid.swap(hidden, dc=1)))
        exp = away(exp)
        exps.append(exp)
        if b + 1 < BLOCKS:
            mr, out, low_keep, low_send, red, stats = join_stage(
                b + 1, me, nz, exp, moments(stats), outer, acts[b], mask, w_reduce
            )
            mr3.append(mr)
            acts.append(away(out))
    last = BLOCKS - 1
    mr, *out, pre3, sums3 = turn_stage(
        last, exps[last], moments(stats), outer, acts[last], mask, grad, tiles * TILE * TILE
    )
    mr3.append(mr)
    pre3 = away(pre3)

    both1, both2, both3 = [None] * BLOCKS, [None] * BLOCKS, [None] * BLOCKS
    shapes = ((mid // nz, d_in), (d_in // nz, mid), (mid // nz, mid))
    pieces = [([], [], []) for _ in range(BLOCKS)]
    after = []
    for b in reversed(range(BLOCKS)):
        both3[b], keep, send, pre2, sums2 = back_expand(
            b, me, pre3, exps[b], mr3[b], sums(sums3), outer, mask, w_expand,
            spas[b], mr2[b], table,
        )
        bulk.add(("e", b), collect.by_halves(weight_expand, *hid2[b], keep, send, pieces[b][0]))
        both2[b], *gs, pre1, sums1 = back_spatial(
            b, me, pre2, spas[b], mr2[b], sums(sums2), table, mask, w9,
            reds[b], mr1[b],
        )
        bulk.add(("s", b), collect.by_rows(hid1[b], gs, pieces[b][2], after if b == 0 else None))
        below = None
        if b > 0:
            below = (exps[b - 1], mr3[b - 1], outer, acts[b - 1])
        result = back_reduce(
            b, pre1, reds[b], mr1[b], sums(sums1), table, mask, w_reduce, pre3, below, tiles * TILE * TILE
        )
        both1[b] = result[0]
        gr = result[1]
        reduce_flow = collect.by_halves(
            weight_reduce, *lows[b], gr, gr, pieces[b][1], after if b == 0 else None, after if b else None
        )
        if b > 0:
            bulk.add(("r", b), reduce_flow)
        if b > 0:
            pre3, sums3 = away(result[2]), result[3]
        else:
            grad_in = list(result[2:4])

    grad_in[0] = bulk.last(grad_in[0], [("s", 0)])
    bulk.add(("r", 0), reduce_flow)
    later = [(n, b) for b in range(1, BLOCKS) for n in "ers"]
    every = later + [("e", 0)]
    bulk.hold(later, collect.begun)
    bulk.resume(later, collect.begun)
    bulk.run([("r", 0)], ("plane",), 1)
    bulk.resume([("e", 0)], after[1])
    bulk.hold([("e", 0)], after[1])
    bulk.run([("r", 0)], ("plane",))
    bulk.run([("s", 0)])
    bulk.run(every, ("deep",))
    views = []
    for value in (*out, *grad_in):
        value, _ = lax.optimization_barrier((value, after[2]))
        views.append(value)
    views = from_rows(*views[:2]) + from_rows(*views[2:])
    bulk.run(every)
    gathered = [[] for _ in range(BLOCKS)]
    for b in range(1, BLOCKS):
        bulk.add(("g", b), collect.chips([p[0] for p in pieces[b]], gathered[b]))
        bulk.hold([("g", b)], after[2])
        bulk.run([("g", b)])
    bulk.run([("r", 0)])
    bulk.add(("g", 0), collect.chips([p[0] for p in pieces[0]], gathered[0]))
    bulk.run([("g", 0)])
    *views, gathered[0][1] = lax.optimization_barrier((*views, gathered[0][1]))
    final = []
    for b in range(BLOCKS):
        final += gathered[b] + [grid.swap(v, dc=1) for v in gathered[b]]
    final = [pltpu.with_memory_space_constraint(v, pltpu.HBM) for v in final]
    slices = place_slices(me, final, shapes)
    out_images, out_tiles, in_images, in_tiles = views
    g_reduce, g_spatial, g_expand = slices

    def pair(at):
        return jnp.stack([jnp.stack([both1[b][at], both2[b][at]]) for b in range(BLOCKS)])

    return (
        out_images,
        out_tiles,
        in_images,
        in_tiles,
        g_reduce,
        g_spatial.reshape(BLOCKS, 3, 3, mid // nz, mid),
        g_expand,
        pair(1),
        pair(0),
        jnp.stack([both3[b][1] for b in range(BLOCKS)]),
        jnp.stack([both3[b][0] for b in range(BLOCKS)]),
    )


def solution(mesh):
    both = ("wide", "narrow")
    batch = P(both, None, None, None)
    grid = Grid(mesh.shape["wide"], mesh.shape["narrow"])
    return jax.shard_map(
        functools.partial(per_device, grid),
        mesh=mesh,
        in_specs=(batch, batch, P(both), P(), P(), P(), P(), P(), P(), P(), batch, batch),
        out_specs=(
            batch,
            batch,
            batch,
            batch,
            P(None, "narrow", None),
            P(None, None, None, "narrow", None),
            P(None, "narrow", None),
            P(),
            P(),
            P(),
            P(),
        ),
        check_vma=False,
    )
```
